32 devices in a mesh: seq: 8 (over z, x), tp: 4 (over y, core).
Axes of the slice: x: 2, y: 2, z: 4, core: 2. Of those that a mesh axis runs over, the one named last changes fastest.
Arguments:
- queries: bfloat16 [8192, 8192], P('seq', 'tp'), may hold values from -0.29882812 to 0.29882812
- key_vectors: bfloat16 [8192, 8192], P('seq', 'tp'), may hold values from -0.29882812 to 0.29882812
- value_vectors: bfloat16 [8192, 8192], P('seq', 'tp'), may hold values from -0.29882812 to 0.29882812
- log_decay: float32 [64, 8192], P('tp', 'seq'), may hold values from -1 to 0
- grad_output: bfloat16 [8192, 6144], P('seq', 'tp'), may hold values from -6 to 6
- out_weight: bfloat16 [8192, 6144], P('tp'), may hold values from -0.0625 to 0.0625
Outputs:
- grad_queries: bfloat16 [8192, 8192], P('seq', 'tp')
- grad_keys: bfloat16 [8192, 8192], P('seq', 'tp')
- grad_values: bfloat16 [8192, 8192], P('seq', 'tp')
The draws below stay inside these ranges and needn't reach their ends.
All inputs are finite; a program needn't handle non-finite values.
Results may differ from the reference program's by a relative error of at most 0.0063.
Values may be sent and summed in bfloat16 or wider, within the bound.
No kernel may reach another device: no remote copies, remote signals or barrier semaphores. Data moves between devices by JAX's collectives and lax.ppermute only.
A program may use at most 192 MiB of HBM per device.

```python
import math
import jax
import jax.numpy as jnp
from jax import lax

D = 6144
HEAD_COUNT = 64
HD = 128
BLK = 256
TOK_DEV = 1024
TOKEN_COUNT = 8192


def draw_log_decay(key, part):
    random_subkeys = jax.random.split(key, 6)
    chooser = jax.random.uniform(random_subkeys[0], (HEAD_COUNT,))
    slow_share = 0.5
    slow_mask = chooser < slow_share
    slow_rate = math.log(10.0) * jax.random.uniform(random_subkeys[1], (HEAD_COUNT,), minval=0.02, maxval=0.2) / TOKEN_COUNT
    fast_rate = 1.0 / jax.random.uniform(random_subkeys[2], (HEAD_COUNT,), minval=30.0, maxval=50.0)
    decay_rate = jnp.where(slow_mask, slow_rate, fast_rate)
    span_count = TOKEN_COUNT // TOK_DEV
    device_factor = jnp.exp(jax.random.uniform(random_subkeys[3], (HEAD_COUNT, span_count), minval=-math.log(2.0), maxval=math.log(2.0)))
    device_factor = jnp.repeat(device_factor, TOK_DEV, axis=1)
    baseline_decay = -decay_rate[:, None] * device_factor
    spike_positions = jax.random.randint(random_subkeys[4], (2,), 0, TOKEN_COUNT)
    spike_mask = jnp.any(jnp.arange(TOKEN_COUNT)[:, None] == spike_positions[None, :], axis=1)
    spike_decay_drop = jnp.log(jax.random.uniform(random_subkeys[5], (HEAD_COUNT, TOKEN_COUNT), minval=0.5, maxval=0.8))
    return jnp.where(spike_mask[None, :], baseline_decay + spike_decay_drop, baseline_decay).astype(jnp.float32)


def level_of(key, extent, cuts, least, largest):
    loudness, own = 1.0, jax.random.fold_in(key, 6)
    for dim, parts in cuts:
        steps = jnp.exp(jax.random.uniform(jax.random.fold_in(own, dim), (parts,), jnp.float32, least / len(cuts), largest / len(cuts)))
        loudness = loudness * jnp.repeat(steps, extent[dim] // parts).reshape([-1 if axis == dim else 1 for axis in range(len(extent))])
    return loudness


def centred(key, shape, spread, reach, cuts=(), held_as=jnp.bfloat16):
    result = spread * jax.random.normal(key, shape, jnp.float32)
    if cuts:
        result = result * level_of(key, shape, cuts, -0.22, 0.18)
    return jnp.clip(result, -reach, reach).astype(held_as)


def setup_inputs(seed: int = 0) -> dict:
    key_of = jax.random.split(jax.random.key(seed), 7)
    return {
        "queries": centred(key_of[0], (TOKEN_COUNT, HEAD_COUNT * HD), 0.05, 0.29882812, ((0, 8), (1, 4))),
        "key_vectors": centred(key_of[1], (TOKEN_COUNT, HEAD_COUNT * HD), 0.05, 0.29882812, ((0, 8), (1, 4))),
        "value_vectors": centred(key_of[2], (TOKEN_COUNT, HEAD_COUNT * HD), 0.05, 0.29882812, ((0, 8), (1, 4))),
        "log_decay": draw_log_decay(jax.random.fold_in(key_of[6], 71), 0),
        "grad_output": centred(key_of[4], (TOKEN_COUNT, D), 1.0, 6.0, ((0, 8), (1, 4))),
        "out_weight": centred(key_of[5], (HEAD_COUNT * HD, D), (HEAD_COUNT * HD) ** -0.5, 0.0625, ((0, 4),)),
    }


def contract(form, left, right):
    return jnp.einsum(form, left.astype(jnp.float32), right.astype(jnp.float32))


def key_sums(key_blk, value_blk, decay_blk):
    cum_decay = jnp.cumsum(decay_blk, axis=1)
    end_decay = cum_decay[:, -1]
    key_weight = jnp.exp(end_decay[:, None] - cum_decay).T
    key_scaled = (key_blk * key_weight[:, :, None]).astype(jnp.bfloat16)
    return contract("sha,shb->hab", key_scaled, value_blk), end_decay


def query_sums(query_blk, grad_blk, decay_blk):
    cum_decay = jnp.cumsum(decay_blk, axis=1)
    query_weight = jnp.exp(cum_decay).T
    query_scaled = (query_blk * query_weight[:, :, None]).astype(jnp.bfloat16)
    return contract("tha,thb->hab", query_scaled, grad_blk)


def block_terms(query_blk, key_blk, value_blk, grad_blk, decay_blk, enter_fwd, enter_bwd):
    blk_len = query_blk.shape[0]
    cum_decay = jnp.cumsum(decay_blk, axis=1)
    end_decay = cum_decay[:, -1]
    causal = (jnp.arange(blk_len)[:, None] >= jnp.arange(blk_len)[None, :])[None]
    gap_decay = jnp.where(causal, cum_decay[:, :, None] - cum_decay[:, None, :], 0.0)
    mask_mat = jnp.where(causal, jnp.exp(gap_decay), 0.0)
    grad_scores = (contract("thd,shd->hts", grad_blk, value_blk) * mask_mat).astype(jnp.bfloat16)
    attn_scores = (contract("thd,shd->hts", query_blk, key_blk) * mask_mat).astype(jnp.bfloat16)
    fwd_round = enter_fwd.astype(jnp.bfloat16)
    bwd_round = enter_bwd.astype(jnp.bfloat16)
    head_decay = jnp.exp(cum_decay).T[:, :, None]
    tail_decay = jnp.exp(end_decay[:, None] - cum_decay).T[:, :, None]
    grad_query = contract("hts,shd->thd", grad_scores, key_blk) + contract("thb,hab->tha", grad_blk, fwd_round) * head_decay
    grad_key = contract("hts,thd->shd", grad_scores, query_blk) + contract("shb,hab->sha", value_blk, bwd_round) * tail_decay
    grad_value = contract("hts,thd->shd", attn_scores, grad_blk) + contract("sha,hab->shb", key_blk, bwd_round) * tail_decay
    return grad_query.astype(jnp.bfloat16), grad_key.astype(jnp.bfloat16), grad_value.astype(jnp.bfloat16)


def advance(memory, inputs):
    block_state, block_end = inputs
    return jnp.exp(block_end)[:, None, None] * memory + block_state, memory


def reference(queries, key_vectors, value_vectors, log_decay, grad_output, out_weight):
    head_grads = jnp.dot(grad_output, out_weight.T, preferred_element_type=jnp.float32).astype(jnp.bfloat16)
    blk_count = TOKEN_COUNT // BLK

    def split_rows(matrix):
        return matrix.reshape(blk_count, BLK, HEAD_COUNT, HD)

    query_blks = split_rows(queries)
    key_blks = split_rows(key_vectors)
    value_blks = split_rows(value_vectors)
    grad_blks = split_rows(head_grads)
    decay_blks = log_decay.reshape(HEAD_COUNT, blk_count, BLK).transpose(1, 0, 2)
    key_value, end_decay = lax.map(lambda inputs: key_sums(*inputs), (key_blks, value_blks, decay_blks))
    query_grad = lax.map(lambda inputs: query_sums(*inputs), (query_blks, grad_blks, decay_blks))
    zero_state = jnp.zeros((HEAD_COUNT, HD, HD), jnp.float32)
    _, enter_fwd = lax.scan(advance, zero_state, (key_value, end_decay))
    _, enter_bwd = lax.scan(advance, zero_state, (query_grad, end_decay), reverse=True)
    grad_q, grad_k, grad_v = lax.map(lambda inputs: block_terms(*inputs), (query_blks, key_blks, value_blks, grad_blks, decay_blks, enter_fwd, enter_bwd))

    def join_rows(blocks):
        return blocks.reshape(TOKEN_COUNT, HEAD_COUNT * HD)

    return (join_rows(grad_q), join_rows(grad_k), join_rows(grad_v))
```

```python
import functools

import jax
import jax.numpy as jnp
from jax import lax
from jax.experimental import pallas as pl
from jax.experimental.pallas import tpu as pltpu
from jax.sharding import PartitionSpec as P

HD = 128
BLK = 256
VMEM_BYTES = 56 * 2**20

NN = (((1,), (0,)), ((), ()))
NT = (((1,), (1,)), ((), ()))
TN = (((0,), (0,)), ((), ()))


def mm(left, right, form):
    return lax.dot_general(left, right, form, preferred_element_type=jnp.float32)


def params(grid_dims):
    return pltpu.CompilerParams(
        dimension_semantics=("arbitrary",) * grid_dims, vmem_limit_bytes=VMEM_BYTES
    )


def cost(flops, nbytes, exps=0):
    return pl.CostEstimate(flops=int(flops), bytes_accessed=int(nbytes), transcendentals=int(exps))


def head_lanes(h):
    return slice(h * HD, (h + 1) * HD)


def key_body(group, k_ref, v_ref, cum_ref, kv_ref, total_ref, carry_ref):
    blk, blk_count = pl.program_id(1), pl.num_programs(1)
    cum = cum_ref[0].T
    end = cum[BLK - 1 : BLK, :]
    weight = jnp.exp(end - cum)
    end_weight = jnp.exp(end)

    @pl.when(blk == 0)
    def _():
        carry_ref[...] = jnp.zeros_like(carry_ref)

    for h in range(group):
        lanes = head_lanes(h)
        scaled = (k_ref[:, lanes].astype(jnp.float32) * weight[:, h : h + 1]).astype(jnp.bfloat16)
        kv = mm(scaled, v_ref[:, lanes], TN)
        kv_ref[0, h] = kv
        carry_ref[h] = carry_ref[h] * end_weight[:, h : h + 1] + kv

    @pl.when(blk == blk_count - 1)
    def _():
        total_ref[...] = carry_ref[...].astype(total_ref.dtype)


def key_totals(keys, values, cum, group):
    rows, width = keys.shape
    heads, blk_count = width // HD, rows // BLK
    tokens = pl.BlockSpec((BLK, group * HD), lambda g, j: (j, g))
    return pl.pallas_call(
        functools.partial(key_body, group),
        grid=(heads // group, blk_count),
        in_specs=[tokens, tokens, pl.BlockSpec((1, group, BLK), lambda g, j: (g, 0, j))],
        out_specs=[
            pl.BlockSpec((1, group, HD, HD), lambda g, j: (j, g, 0, 0)),
            pl.BlockSpec((group, HD, HD), lambda g, j: (g, 0, 0)),
        ],
        out_shape=[
            jax.ShapeDtypeStruct((blk_count, heads, HD, HD), jnp.float32),
            jax.ShapeDtypeStruct((heads, HD, HD), jnp.bfloat16),
        ],
        scratch_shapes=[pltpu.VMEM((group, HD, HD), jnp.float32)],
        compiler_params=params(2),
        cost_estimate=cost(2 * rows * width * HD, 4 * rows * width + 4 * blk_count * width * HD),
        name="key_totals",
    )(keys, values, cum)


def near_body(count, ids_ref, *refs):
    total = mm(refs[0][...], refs[count][...], NT)
    for piece in range(1, count):
        total += mm(refs[piece][...], refs[count + piece][...], NT)
    refs[2 * count][...] = total


def near_product(ids, pieces, weight, wide):
    rows, depth = pieces[0].shape
    width, count = weight.shape[0], len(pieces)
    held = pl.BlockSpec((rows, depth), lambda g, ids: (0, 0))
    columns = [pl.BlockSpec((wide, depth), lambda g, ids, n=n: (g, ids[n])) for n in range(count)]
    return pl.pallas_call(
        functools.partial(near_body, count),
        grid_spec=pltpu.PrefetchScalarGridSpec(
            num_scalar_prefetch=1,
            grid=(width // wide,),
            in_specs=[held] * count + columns,
            out_specs=pl.BlockSpec((rows, wide), lambda g, ids: (0, g)),
        ),
        out_shape=jax.ShapeDtypeStruct((rows, width), jnp.float32),
        compiler_params=params(1),
        cost_estimate=cost(
            2 * rows * width * depth * count,
            2 * count * depth * (rows + width) + 4 * rows * width,
        ),
        name="near_product",
    )(ids, *pieces, *([weight] * count))


def far_body(count, group, ids_ref, before_ref, *refs):
    near_ref, q_ref, cum_ref, prior_ref, grad_ref, sums_ref, total_ref = refs[2 * count :]
    total = near_ref[...]
    for piece in range(count):
        total += mm(refs[piece][...], refs[count + piece][...], NT)
    grad_ref[...] = total.astype(jnp.bfloat16)
    cum = cum_ref[0].T
    weight = jnp.exp(cum)
    for h in range(group):
        lanes = head_lanes(h)
        scaled = (q_ref[:, lanes].astype(jnp.float32) * weight[:, h : h + 1]).astype(jnp.bfloat16)
        sums = mm(scaled, grad_ref[:, lanes], TN)
        sums_ref[h] = sums
        prior = prior_ref[pl.program_id(0) * group + h]
        total_ref[h] = (before_ref[h] + prior * sums).astype(total_ref.dtype)


def far_product(ids, before, pieces, weight, near, queries, cum, prior, blk, last):
    rows, depth = pieces[0].shape
    width, count = weight.shape[0], len(pieces)
    groups, group = cum.shape[0], cum.shape[1]
    wide, heads = group * HD, width // HD
    held = pl.BlockSpec((rows, depth), lambda g, ids: (0, 0))
    columns = [pl.BlockSpec((wide, depth), lambda g, ids, n=n: (g, ids[n])) for n in range(count)]
    tokens = pl.BlockSpec((rows, wide), lambda g, ids: (blk, g))
    states = pl.BlockSpec((group, HD, HD), lambda g, ids: (g, 0, 0))
    return pl.pallas_call(
        functools.partial(far_body, count, group),
        grid_spec=pltpu.PrefetchScalarGridSpec(
            num_scalar_prefetch=1,
            grid=(groups,),
            in_specs=[states]
            + [held] * count
            + columns
            + [
                tokens,
                tokens,
                pl.BlockSpec((1, group, rows), lambda g, ids: (g, 0, blk)),
                pl.BlockSpec(memory_space=pltpu.SMEM),
            ],
            out_specs=[pl.BlockSpec((rows, wide), lambda g, ids: (0, g)), states, states],
        ),
        out_shape=[
            jax.ShapeDtypeStruct((rows, width), jnp.bfloat16),
            jax.ShapeDtypeStruct((heads, HD, HD), jnp.float32),
            jax.ShapeDtypeStruct((heads, HD, HD), jnp.bfloat16 if last else jnp.float32),
        ],
        compiler_params=params(1),
        cost_estimate=cost(
            2 * rows * width * (depth * count + HD),
            2 * count * depth * (rows + width) + 8 * rows * width + 12 * width * HD,
        ),
        name="far_product",
    )(ids, before, *pieces, *([weight] * count), near, queries, cum, prior)


def block_body(group, blk_count, *refs):
    q_ref, k_ref, v_ref = refs[:3]
    grad_refs = refs[3 : 3 + blk_count]
    cum_ref, kv_ref, enter_ref, gq_ref, gk_ref, gv_ref, carry_ref, grad_ref = refs[3 + blk_count :]
    blk = pl.program_id(1)

    @pl.when(blk == 0)
    def _():
        carry_ref[...] = enter_ref[...].astype(jnp.float32)

    for j in range(blk_count):

        @pl.when(blk == j)
        def _(j=j):
            grad_ref[...] = grad_refs[j][...]

    rows = cum_ref[0]
    cum = rows.T
    head_weight = jnp.exp(cum)
    end_weight = head_weight[BLK - 1 : BLK, :]
    causal = lax.broadcasted_iota(jnp.int32, (BLK, BLK), 0) >= lax.broadcasted_iota(
        jnp.int32, (BLK, BLK), 1
    )
    for h in range(group):
        lanes = head_lanes(h)
        q, k, v, grad = q_ref[:, lanes], k_ref[:, lanes], v_ref[:, lanes], grad_ref[:, lanes]
        gap = jnp.where(causal, cum[:, h : h + 1] - rows[h : h + 1, :], -1e30)
        mask = jnp.exp(gap)
        grad_scores = (mm(grad, v, NT) * mask).astype(jnp.bfloat16)
        attn_scores = (mm(q, k, NT) * mask).astype(jnp.bfloat16)
        enter = carry_ref[h]
        gq = mm(grad_scores, k, NN)
        gq += mm(grad, enter.astype(jnp.bfloat16), NT) * head_weight[:, h : h + 1]
        gq_ref[:, lanes] = gq.astype(jnp.bfloat16)
        gk_ref[:, lanes] = mm(grad_scores, q, TN).astype(jnp.bfloat16)
        gv_ref[:, lanes] = mm(attn_scores, grad, TN).astype(jnp.bfloat16)
        carry_ref[h] = enter * end_weight[:, h : h + 1] + kv_ref[0, h]


def block_terms(queries, keys, values, grads, cum, kv, enter):
    rows, width = queries.shape
    heads, blk_count = width // HD, rows // BLK
    groups, group = cum.shape[0], cum.shape[1]
    tokens = pl.BlockSpec((BLK, group * HD), lambda g, j: (j, g))
    part = pl.BlockSpec((BLK, group * HD), lambda g, j: (0, g))
    out = jax.ShapeDtypeStruct((rows, width), jnp.bfloat16)
    return pl.pallas_call(
        functools.partial(block_body, group, blk_count),
        grid=(groups, blk_count),
        in_specs=[tokens] * 3
        + [part] * blk_count
        + [
            pl.BlockSpec((1, group, BLK), lambda g, j: (g, 0, j)),
            pl.BlockSpec((1, group, HD, HD), lambda g, j: (j, g, 0, 0)),
            pl.BlockSpec((group, HD, HD), lambda g, j: (g, 0, 0)),
        ],
        out_specs=[tokens] * 3,
        out_shape=[out] * 3,
        scratch_shapes=[
            pltpu.VMEM((group, HD, HD), jnp.float32),
            pltpu.VMEM((BLK, group * HD), jnp.bfloat16),
        ],
        compiler_params=params(2),
        cost_estimate=cost(
            rows * width * (10 * BLK + 2 * HD),
            14 * rows * width + 4 * blk_count * width * HD,
            rows * heads * BLK,
        ),
        name="block_terms",
    )(queries, keys, values, *grads, cum, kv, enter)


def later_body(group, blk_count, *refs):
    k_ref, v_ref, gk_in_ref, gv_in_ref = refs[:4]
    sums_refs = refs[4 : 4 + blk_count]
    cum_ref, enter_ref, gk_ref, gv_ref, carry_ref = refs[4 + blk_count :]
    blk = blk_count - 1 - pl.program_id(1)

    @pl.when(blk == blk_count - 1)
    def _():
        carry_ref[...] = enter_ref[...].astype(jnp.float32)

    cum = cum_ref[0].T
    end = cum[BLK - 1 : BLK, :]
    weight = jnp.exp(end - cum)
    end_weight = jnp.exp(end)
    for h in range(group):
        lanes = head_lanes(h)
        tail = weight[:, h : h + 1]
        enter = carry_ref[h].astype(jnp.bfloat16)
        gk = gk_in_ref[:, lanes].astype(jnp.float32) + mm(v_ref[:, lanes], enter, NT) * tail
        gv = gv_in_ref[:, lanes].astype(jnp.float32) + mm(k_ref[:, lanes], enter, NN) * tail
        gk_ref[:, lanes] = gk.astype(jnp.bfloat16)
        gv_ref[:, lanes] = gv.astype(jnp.bfloat16)
    for j in range(1, blk_count):

        @pl.when(blk == j)
        def _(j=j):
            for h in range(group):
                carry_ref[h] = carry_ref[h] * end_weight[:, h : h + 1] + sums_refs[j][h]


def later_terms(keys, values, gk, gv, sums, cum, enter):
    rows, width = keys.shape
    blk_count = rows // BLK
    groups, group = cum.shape[0], cum.shape[1]
    tokens = pl.BlockSpec((BLK, group * HD), lambda g, j: (blk_count - 1 - j, g))
    states = pl.BlockSpec((group, HD, HD), lambda g, j: (g, 0, 0))
    out = jax.ShapeDtypeStruct((rows, width), jnp.bfloat16)
    return pl.pallas_call(
        functools.partial(later_body, group, blk_count),
        grid=(groups, blk_count),
        in_specs=[tokens] * 4
        + [states] * blk_count
        + [pl.BlockSpec((1, group, BLK), lambda g, j: (g, 0, blk_count - 1 - j)), states],
        out_specs=[tokens] * 2,
        out_shape=[out] * 2,
        scratch_shapes=[pltpu.VMEM((group, HD, HD), jnp.float32)],
        input_output_aliases={2: 0, 3: 1},
        compiler_params=params(2),
        cost_estimate=cost(
            rows * width * 4 * HD, 12 * rows * width + 4 * blk_count * width * HD
        ),
        name="later_terms",
    )(keys, values, gk, gv, *sums, cum, enter)


def span_states(totals, spans, reverse):
    devices = lax.axis_size("seq")
    heads = totals.shape[0]
    share = heads * HD // devices
    flat = totals.reshape(heads * HD, HD)
    got = lax.all_to_all(flat, "seq", 0, 0, tiled=True).reshape(devices, share, HD)
    by_row = jnp.repeat(jnp.exp(spans), HD, axis=1)
    mine = lax.dynamic_slice_in_dim(by_row, lax.axis_index("seq") * share, share, axis=1)
    carry = jnp.zeros((share, HD), jnp.float32)
    out = [None] * devices
    for place in reversed(range(devices)) if reverse else range(devices):
        out[place] = carry.astype(jnp.bfloat16)
        carry = mine[place][:, None] * carry + got[place].astype(jnp.float32)
    back = lax.all_to_all(jnp.concatenate(out, axis=0), "seq", 0, 0, tiled=True)
    return back.reshape(heads, HD, HD)


def local(queries, key_vectors, value_vectors, log_decay, grad_output, out_weight):
    rows, width = queries.shape
    heads, blk_count = width // HD, rows // BLK
    tp, me = lax.axis_size("tp"), lax.axis_index("tp")
    chips = tp // 2
    core = [(i, i ^ 1) for i in range(tp)]

    def from_chip(hops):
        return [(i, (i + 2 * hops) % tp) for i in range(tp)]

    ids = jnp.stack(
        [lax.rem(me + tp - 2 * d, tp) ^ e for d in range(chips) for e in range(2)]
    ).astype(jnp.int32)
    own = grad_output
    far = []
    for j in range(blk_count):
        piece = own[j * BLK : (j + 1) * BLK]
        arrived = []
        for d in range(1, chips):
            first = lax.ppermute(piece, "tp", from_chip(d))
            arrived += [first, lax.ppermute(first, "tp", core)]
        far.append(arrived)
    sibling = lax.ppermute(own, "tp", core)

    cum = jnp.cumsum(log_decay.reshape(heads, blk_count, BLK), axis=2)
    end = cum[:, :, -1]
    spans = lax.all_gather(jnp.sum(end, axis=1), "seq")
    prior = jnp.exp(jnp.cumsum(end, axis=1) - end)
    group = 4
    cum4 = cum.reshape(heads // group, group, rows)

    kv, fwd_total = key_totals(key_vectors, value_vectors, cum4, group)
    enter_fwd = span_states(fwd_total, spans, False)

    near = near_product(ids[:2], [own, sibling], out_weight, 256)
    total = jnp.zeros((heads, HD, HD), jnp.float32)
    grads, sums = [], []
    for j in range(blk_count):
        grad, part, total = far_product(
            ids[2:],
            total,
            far[j],
            out_weight,
            near,
            queries,
            cum4,
            prior[:, j],
            j,
            j == blk_count - 1,
        )
        grads.append(grad)
        sums.append(part)
    enter_bwd = span_states(total, spans, True)
    gq, gk, gv = block_terms(queries, key_vectors, value_vectors, grads, cum4, kv, enter_fwd)
    gk, gv = later_terms(key_vectors, value_vectors, gk, gv, sums, cum4, enter_bwd)
    return gq, gk, gv


def solution(mesh):
    in_specs = (
        P("seq", "tp"),
        P("seq", "tp"),
        P("seq", "tp"),
        P("tp", "seq"),
        P("seq", "tp"),
        P("tp", None),
    )
    out_specs = (P("seq", "tp"), P("seq", "tp"), P("seq", "tp"))
    return jax.shard_map(local, mesh=mesh, in_specs=in_specs, out_specs=out_specs, check_vma=False)
```

```python
import functools

import jax
import jax.numpy as jnp
from jax import lax
from jax.experimental import pallas as pl
from jax.experimental.pallas import tpu as pltpu
from jax.sharding import PartitionSpec as P

HD = 128
BLK = 256
GROUP = 4
ROW = 16
MIB = 2**20

NN = (((1,), (0,)), ((), ()))
NT = (((1,), (1,)), ((), ()))
TN = (((0,), (0,)), ((), ()))

ANY = pl.BlockSpec(memory_space=pl.ANY)
VMEM = pl.BlockSpec(memory_space=pltpu.VMEM)
SMEM = pl.BlockSpec(memory_space=pltpu.SMEM)
BF16 = jnp.bfloat16
F32 = jnp.float32


def mm(left, right, form):
    return lax.dot_general(left, right, form, preferred_element_type=F32)


def cost(flops, nbytes, exps=0):
    return pl.CostEstimate(flops=int(flops), bytes_accessed=int(nbytes), transcendentals=int(exps))


def span(index, size):
    return slice(index * size, (index + 1) * size)


def call(body, name, ins, outs, scratch, limit, estimate, aliases=None):
    return pl.pallas_call(
        body,
        in_specs=[spec for _, spec in ins],
        out_specs=[spec for _, _, spec in outs],
        out_shape=[jax.ShapeDtypeStruct(shape, dtype) for shape, dtype, _ in outs],
        scratch_shapes=scratch,
        input_output_aliases=aliases or {},
        compiler_params=pltpu.CompilerParams(vmem_limit_bytes=limit * MIB),
        cost_estimate=estimate,
        name=name,
    )(*[array for array, _ in ins])


def copy_of(source, target, sem):
    return pltpu.make_async_copy(source, target, sem)


def lanes_of(index, size):
    return pl.ds(pl.multiple_of(index * size, size), size)


def loop(count, body):
    lax.fori_loop(0, count, lambda i, _: (body(i), 0)[1], 0)


def head_in(h):
    return slice(h * HD, (h + 1) * HD)


def key_body(k_hbm, v_hbm, cum_ref, local_hbm, total_ref, k_ref, v_ref, local_ref, load_sems, store_sems):
    blk_count, groups, group, _ = cum_ref.shape
    wide = group * HD

    def loads(j):
        rows = pl.ds(j * BLK, BLK)
        return (
            copy_of(k_hbm.at[rows], k_ref.at[rows], load_sems.at[0, j]),
            copy_of(v_hbm.at[rows], v_ref.at[rows], load_sems.at[1, j]),
        )

    def store(j):
        return copy_of(local_ref.at[j], local_hbm.at[j], store_sems.at[j])

    for j in range(blk_count):
        for copy in loads(j):
            copy.start()
    local_ref[0] = jnp.zeros_like(local_ref[0])

    def block(j):
        for copy in loads(j):
            copy.wait()
        store(j).start()
        rows = pl.ds(pl.multiple_of(j * BLK, BLK), BLK)

        def some_heads(g):
            cum = cum_ref[j, g].T
            end = cum[BLK - 1 : BLK, :]
            weight = jnp.exp(end - cum)
            end_weight = jnp.exp(end)
            lanes = lanes_of(g, wide)
            these = pl.ds(g * group, group)
            keys, values, entered = k_ref[rows, lanes], v_ref[rows, lanes], local_ref[j, these]
            left = []
            for h in range(group):
                scaled = (keys[:, head_in(h)].astype(F32) * weight[:, h : h + 1]).astype(BF16)
                sums = mm(scaled, values[:, head_in(h)], TN)
                left.append(entered[h] * end_weight[:, h : h + 1] + sums)
            local_ref[j + 1, these] = jnp.stack(left)

        loop(groups, some_heads)

    loop(blk_count, block)
    total_ref[...] = local_ref[blk_count].astype(BF16)
    for j in range(blk_count):
        store(j).wait()


def key_totals(keys, values, cum):
    rows, width = keys.shape
    blk_count, heads = cum.shape[0], width // HD
    return call(
        key_body,
        "key_totals",
        [(keys, ANY), (values, ANY), (cum, VMEM)],
        [((blk_count, heads, HD, HD), F32, ANY), ((heads, HD, HD), BF16, VMEM)],
        [
            pltpu.VMEM((rows, width), BF16),
            pltpu.VMEM((rows, width), BF16),
            pltpu.VMEM((blk_count + 1, heads, HD, HD), F32),
            pltpu.SemaphoreType.DMA((2, blk_count)),
            pltpu.SemaphoreType.DMA((blk_count,)),
        ],
        24,
        cost(2 * rows * width * HD, 4 * rows * width + 4 * blk_count * width * HD),
    )


def near_body(wide, own_hbm, sibling_hbm, w_hbm, out_hbm, grad_ref, w_ref, out_ref, w_sems, grad_sems, out_sems):
    rows, depth = own_hbm.shape
    groups, tiles = w_hbm.shape[0] // wide, rows // BLK
    me = lax.axis_index("tp")
    side = lax.rem(me, 2)
    columns = pl.ds(pl.multiple_of((me - side) * depth, 2 * depth), 2 * depth)

    def w_load(g):
        part = pl.ds(g * wide, wide)
        return copy_of(w_hbm.at[part, columns], w_ref.at[part], w_sems.at[g])

    def grad_loads(r):
        part = pl.ds(r * BLK, BLK)
        return (
            copy_of(own_hbm.at[part], grad_ref.at[part, lanes_of(side, depth)], grad_sems.at[0, r]),
            copy_of(sibling_hbm.at[part], grad_ref.at[part, lanes_of(1 - side, depth)], grad_sems.at[1, r]),
        )

    def store(g):
        return copy_of(out_ref.at[lax.rem(g, 2)], out_hbm.at[:, lanes_of(g, wide)], out_sems.at[lax.rem(g, 2)])

    w_load(0).start()
    for r in range(tiles):
        for copy in grad_loads(r):
            copy.start()
    for g in range(1, groups):
        w_load(g).start()

    def columns_of(g):
        w_load(g).wait()

        @pl.when(g >= 2)
        def _():
            store(g - 2).wait()

        part = w_ref[pl.ds(pl.multiple_of(g * wide, wide), wide)]
        out_ref[lax.rem(g, 2)] = mm(grad_ref[...], part, NT)
        store(g).start()

    for r in range(tiles):
        for copy in grad_loads(r):
            copy.wait()
    loop(groups, columns_of)
    for g in range(max(groups - 2, 0), groups):
        store(g).wait()


def near_product(own, sibling, weight):
    rows, depth = own.shape
    width = weight.shape[0]
    wide = GROUP * HD
    (out,) = call(
        functools.partial(near_body, wide),
        "near_product",
        [(own, ANY), (sibling, ANY), (weight, ANY)],
        [((rows, width), F32, ANY)],
        [
            pltpu.VMEM((rows, 2 * depth), BF16),
            pltpu.VMEM((width, 2 * depth), BF16),
            pltpu.VMEM((2, rows, wide), F32),
            pltpu.SemaphoreType.DMA((width // wide,)),
            pltpu.SemaphoreType.DMA((2, rows // BLK)),
            pltpu.SemaphoreType.DMA((2,)),
        ],
        32,
        cost(4 * rows * width * depth, 4 * depth * (rows + width) + 4 * rows * width),
    )
    return out


def far_body(blk, chips, before_hbm, near_hbm, q_hbm, cum_ref, prior_ref, w_hbm, *refs):
    pieces = refs[: 2 * (chips - 1)]
    grad_hbm, sums_hbm, total_hbm, piece_ref, w_ref, near_ref, q_ref, before_ref = refs[2 * (chips - 1) :][:8]
    grad_ref, sums_ref, total_ref, piece_sems, load_sems, store_sems = refs[2 * (chips - 1) + 8 :]
    rows, depth = pieces[0].shape
    _, groups, group, _ = cum_ref.shape
    wide = group * HD
    me = lax.axis_index("tp")
    side = lax.rem(me, 2)
    chip = lax.div(me, 2)
    block = pl.ds(blk * BLK, BLK)

    def piece_load(n):
        at = 2 * (n // 2) + (side if n % 2 == 0 else 1 - side)
        return copy_of(pieces[n], piece_ref.at[:, lanes_of(at, depth)], piece_sems.at[n])

    def loads(g):
        part, lanes = pl.ds(g * wide, wide), lanes_of(g, wide)
        these = pl.ds(g * group, group)
        found = []
        for d in range(1, chips):
            owner = lax.rem(chip + chips - d, chips)
            held = pl.ds((d - 1) * 2 * depth, 2 * depth)
            found.append(
                copy_of(w_hbm.at[part, lanes_of(owner, 2 * depth)], w_ref.at[part, held], load_sems.at[d + 2, g])
            )
        found.append(copy_of(near_hbm.at[block, lanes], near_ref.at[:, lanes], load_sems.at[0, g]))
        found.append(copy_of(q_hbm.at[block, lanes], q_ref.at[:, lanes], load_sems.at[1, g]))
        if blk:
            found.append(copy_of(before_hbm.at[these], before_ref.at[these], load_sems.at[2, g]))
        return found

    def stores(g):
        these, lanes = pl.ds(g * group, group), lanes_of(g, wide)
        return (
            copy_of(total_ref.at[these], total_hbm.at[these], store_sems.at[0, g]),
            copy_of(grad_ref.at[:, lanes], grad_hbm.at[:, lanes], store_sems.at[1, g]),
            copy_of(sums_ref.at[these], sums_hbm.at[these], store_sems.at[2, g]),
        )

    for n in range(len(pieces)):
        piece_load(n).start()
    for g in range(groups):
        for copy in loads(g):
            copy.start()
    for n in range(len(pieces)):
        piece_load(n).wait()

    def some_heads(g):
        for copy in loads(g):
            copy.wait()
        lanes = lanes_of(g, wide)
        part = pl.ds(pl.multiple_of(g * wide, wide), wide)
        weight = jnp.exp(cum_ref[blk, g].T)
        queries = q_ref[:, lanes]
        grad = (near_ref[:, lanes] + mm(piece_ref[...], w_ref[part], NT)).astype(BF16)
        these = pl.ds(g * group, group)
        before = before_ref[these] if blk else None
        sums, total = [], []
        for h in range(group):
            scaled = (queries[:, head_in(h)].astype(F32) * weight[:, h : h + 1]).astype(BF16)
            sums.append(mm(scaled, grad[:, head_in(h)], TN))
            total.append(before[h] + prior_ref[g * group + h, blk] * sums[h] if blk else sums[h])
        grad_ref[:, lanes] = grad
        sums_ref[these] = jnp.stack(sums)
        total_ref[these] = jnp.stack(total).astype(total_ref.dtype)
        for copy in stores(g):
            copy.start()

    loop(groups, some_heads)
    for g in range(groups):
        for copy in stores(g):
            copy.wait()


def far_product(blk, last, before, pieces, weight, near, queries, cum, prior):
    rows, depth = pieces[0].shape
    _, groups, group, _ = cum.shape
    heads = groups * group
    width = heads * HD
    chips = len(pieces) // 2 + 1
    total_type = BF16 if last else F32
    states = (heads, HD, HD)
    return call(
        functools.partial(far_body, blk, chips),
        "far_product",
        [(before, ANY), (near, ANY), (queries, ANY), (cum, VMEM), (prior, SMEM), (weight, ANY)]
        + [(piece, ANY) for piece in pieces],
        [((rows, width), BF16, ANY), (states, F32, ANY), (states, total_type, ANY)],
        [
            pltpu.VMEM((rows, 2 * (chips - 1) * depth), BF16),
            pltpu.VMEM((width, 2 * (chips - 1) * depth), BF16),
            pltpu.VMEM((rows, width), F32),
            pltpu.VMEM((rows, width), BF16),
            pltpu.VMEM(states, F32),
            pltpu.VMEM((rows, width), BF16),
            pltpu.VMEM(states, F32),
            pltpu.VMEM(states, total_type),
            pltpu.SemaphoreType.DMA((2 * (chips - 1),)),
            pltpu.SemaphoreType.DMA((chips + 2, groups)),
            pltpu.SemaphoreType.DMA((3, groups)),
        ],
        28,
        cost(
            2 * rows * width * (2 * (chips - 1) * depth + HD),
            4 * (chips - 1) * depth * (rows + width) + 8 * rows * width + 12 * width * HD,
        ),
    )


def block_body(blk, q_hbm, k_hbm, v_hbm, grad_hbm, cum_ref, prior_ref, local_hbm, enter_hbm, *refs):
    refs = refs[1:] if blk else refs
    gq_hbm, gk_hbm, gv_hbm, q_ref, k_ref, v_ref, grad_ref, local_ref, enter_ref = refs[:9]
    gq_ref, gk_ref, gv_ref, load_sems, store_sems = refs[9:]
    _, groups, group, _ = cum_ref.shape
    wide = group * HD
    block = pl.ds(blk * BLK, BLK)

    def loads(g):
        lanes, these = lanes_of(g, wide), pl.ds(g * group, group)
        return (
            copy_of(grad_hbm.at[:, lanes], grad_ref.at[:, lanes], load_sems.at[0, g]),
            copy_of(v_hbm.at[block, lanes], v_ref.at[:, lanes], load_sems.at[1, g]),
            copy_of(q_hbm.at[block, lanes], q_ref.at[:, lanes], load_sems.at[2, g]),
            copy_of(k_hbm.at[block, lanes], k_ref.at[:, lanes], load_sems.at[3, g]),
            copy_of(local_hbm.at[blk, these], local_ref.at[these], load_sems.at[4, g]),
            copy_of(enter_hbm.at[these], enter_ref.at[these], load_sems.at[5, g]),
        )

    def stores(g):
        lanes = lanes_of(g, wide)
        return (
            copy_of(gq_ref.at[:, lanes], gq_hbm.at[block, lanes], store_sems.at[0, g]),
            copy_of(gk_ref.at[:, lanes], gk_hbm.at[:, lanes], store_sems.at[1, g]),
            copy_of(gv_ref.at[:, lanes], gv_hbm.at[:, lanes], store_sems.at[2, g]),
        )

    for g in range(groups):
        for copy in loads(g):
            copy.start()
    at_row = lax.broadcasted_iota(jnp.int32, (BLK, BLK), 0)
    at_col = lax.broadcasted_iota(jnp.int32, (BLK, BLK), 1)
    causal, flipped = at_row >= at_col, at_row <= at_col

    def some_heads(g):
        for copy in loads(g):
            copy.wait()
        rows = cum_ref[blk, g]
        cum = rows.T
        head_weight = jnp.exp(cum)
        lanes, these = lanes_of(g, wide), pl.ds(g * group, group)
        queries, keys, values, grads = q_ref[:, lanes], k_ref[:, lanes], v_ref[:, lanes], grad_ref[:, lanes]
        entered, here = enter_ref[these], local_ref[these]
        gq, gk, gv = [], [], []
        for h in range(group):
            head = head_in(h)
            q, k, v, grad = queries[:, head], keys[:, head], values[:, head], grads[:, head]
            by_row, by_col = cum[:, h : h + 1], rows[h : h + 1, :]
            mask = jnp.exp(jnp.where(causal, by_row - by_col, -1e30))
            turned = jnp.exp(jnp.where(flipped, by_col - by_row, -1e30))
            scores = (mm(grad, v, NT) * mask).astype(BF16)
            turned_scores = (mm(v, grad, NT) * turned).astype(BF16)
            turned_attn = (mm(k, q, NT) * turned).astype(BF16)
            enter = entered[h].astype(F32) * prior_ref[g * group + h, blk] + here[h]
            inter = mm(grad, enter.astype(BF16), NT) * head_weight[:, h : h + 1]
            gq.append((mm(scores, k, NN) + inter).astype(BF16))
            gk.append(mm(turned_scores, q, NN).astype(BF16))
            gv.append(mm(turned_attn, grad, NN).astype(BF16))
        gq_ref[:, lanes] = jnp.concatenate(gq, axis=1)
        gk_ref[:, lanes] = jnp.concatenate(gk, axis=1)
        gv_ref[:, lanes] = jnp.concatenate(gv, axis=1)
        for copy in stores(g):
            copy.start()

    loop(groups, some_heads)
    for g in range(groups):
        for copy in stores(g):
            copy.wait()


def block_terms(blk, queries, keys, values, grad, cum, prior, local_enter, enter, gq):
    rows, width = queries.shape
    heads, groups = width // HD, cum.shape[1]
    tile = pltpu.VMEM((BLK, width), BF16)
    part = ((BLK, width), BF16, ANY)
    ins = [queries, keys, values, grad, cum, prior, local_enter, enter]
    specs = [ANY, ANY, ANY, ANY, VMEM, SMEM, ANY, ANY]
    if blk:
        ins, specs = ins + [gq], specs + [ANY]
    return call(
        functools.partial(block_body, blk),
        "block_terms",
        list(zip(ins, specs)),
        [((rows, width), BF16, ANY), part, part],
        [tile] * 4
        + [pltpu.VMEM((heads, HD, HD), F32), pltpu.VMEM((heads, HD, HD), BF16)]
        + [tile] * 3
        + [pltpu.SemaphoreType.DMA((6, groups)), pltpu.SemaphoreType.DMA((3, groups))],
        20,
        cost(BLK * width * (10 * BLK + 2 * HD), 14 * BLK * width + 6 * width * HD, BLK * heads * BLK),
        {8: 0} if blk else None,
    )


def later_body(k_hbm, v_hbm, cum_ref, enter_hbm, *refs):
    blk_count, groups, group, _ = cum_ref.shape
    gk_parts, gv_parts = refs[:blk_count], refs[blk_count : 2 * blk_count]
    sums_hbm = refs[2 * blk_count : 3 * blk_count - 1]
    gk_hbm, gv_hbm, k_ref, v_ref, gk_ref, gv_ref, sums_ref, enter_ref, carry_ref = refs[3 * blk_count - 1 : -2]
    load_sems, store_sems = refs[-2:]
    wide = group * HD

    def rows_of(j):
        return pl.ds(pl.multiple_of(j * BLK, BLK), BLK)

    def sums_load(j, at):
        return copy_of(sums_hbm[at - 1], sums_ref.at[j], load_sems.at[4, j])

    def loads(j, at):
        rows = rows_of(j)
        return [
            copy_of(v_hbm.at[rows], v_ref.at[rows], load_sems.at[0, j]),
            copy_of(k_hbm.at[rows], k_ref.at[rows], load_sems.at[1, j]),
            copy_of(gk_parts[at], gk_ref.at[rows], load_sems.at[2, j]),
            copy_of(gv_parts[at], gv_ref.at[rows], load_sems.at[3, j]),
        ]

    def stores(j):
        rows = rows_of(j)
        return (
            copy_of(gk_ref.at[rows], gk_hbm.at[rows], store_sems.at[0, j]),
            copy_of(gv_ref.at[rows], gv_hbm.at[rows], store_sems.at[1, j]),
        )

    enter_load = copy_of(enter_hbm, enter_ref, load_sems.at[0, blk_count])
    enter_load.start()
    for j in reversed(range(blk_count)):
        for copy in loads(j, j):
            copy.start()
        if j:
            sums_load(j, j).start()
    sums_ref[0] = jnp.zeros_like(sums_ref[0])
    enter_load.wait()
    carry_ref[...] = enter_ref[...].astype(F32)

    def block(back):
        j = blk_count - 1 - back
        rows = rows_of(j)
        for copy in loads(j, 0):
            copy.wait()

        @pl.when(j > 0)
        def _():
            sums_load(j, 1).wait()

        def some_heads(g):
            cum = cum_ref[j, g].T
            end = cum[BLK - 1 : BLK, :]
            weight = jnp.exp(end - cum)
            end_weight = jnp.exp(end)
            lanes, these = lanes_of(g, wide), pl.ds(g * group, group)
            keys, values = k_ref[rows, lanes], v_ref[rows, lanes]
            gk_in, gv_in = gk_ref[rows, lanes], gv_ref[rows, lanes]
            entered, here = carry_ref[these], sums_ref[j, these]
            gk, gv, left = [], [], []
            for h in range(group):
                head, tail = head_in(h), weight[:, h : h + 1]
                enter = entered[h].astype(BF16)
                gk.append((gk_in[:, head].astype(F32) + mm(values[:, head], enter, NT) * tail).astype(BF16))
                gv.append((gv_in[:, head].astype(F32) + mm(keys[:, head], enter, NN) * tail).astype(BF16))
                left.append(entered[h] * end_weight[:, h : h + 1] + here[h])
            gk_ref[rows, lanes] = jnp.concatenate(gk, axis=1)
            gv_ref[rows, lanes] = jnp.concatenate(gv, axis=1)
            carry_ref[these] = jnp.stack(left)

        loop(groups, some_heads)
        for copy in stores(j):
            copy.start()

    loop(blk_count, block)
    for j in range(blk_count):
        for copy in stores(j):
            copy.wait()


def later_terms(keys, values, gk_parts, gv_parts, sums, cum, enter):
    rows, width = keys.shape
    heads, blk_count = width // HD, rows // BLK
    whole = pltpu.VMEM((rows, width), BF16)
    out = ((rows, width), BF16, ANY)
    return call(
        later_body,
        "later_terms",
        [(keys, ANY), (values, ANY), (cum, VMEM), (enter, ANY)]
        + [(x, ANY) for x in gk_parts + gv_parts + sums],
        [out, out],
        [whole] * 4
        + [
            pltpu.VMEM((blk_count, heads, HD, HD), F32),
            pltpu.VMEM((heads, HD, HD), BF16),
            pltpu.VMEM((heads, HD, HD), F32),
            pltpu.SemaphoreType.DMA((5, blk_count + 1)),
            pltpu.SemaphoreType.DMA((2, blk_count)),
        ],
        28,
        cost(rows * width * 4 * HD, 12 * rows * width + 4 * blk_count * width * HD),
    )


def chain_body(reverse, got_ref, weight_ref, out_ref):
    devices, share = got_ref.shape[0], got_ref.shape[1]
    pieces = weight_ref.shape[1]
    part = share // pieces
    for p in range(pieces):
        rows = span(p, part)
        carry = jnp.zeros((part, HD), F32)
        for place in reversed(range(devices)) if reverse else range(devices):
            out_ref[place, rows] = carry.astype(BF16)
            carry = weight_ref[place, p] * carry + got_ref[place, rows].astype(F32)


def chain(got, weights, reverse):
    devices, share, _ = got.shape
    (out,) = call(
        functools.partial(chain_body, reverse),
        "chain_states",
        [(got, VMEM), (weights, SMEM)],
        [((devices, share, HD), BF16, VMEM)],
        [],
        16,
        cost(2 * devices * share * HD, 4 * devices * share * HD),
    )
    return out


def swap(x):
    devices = lax.axis_size("seq")
    flat = x.reshape(-1, HD)
    return lax.all_to_all(flat, "seq", 0, 0, tiled=True).reshape(devices, -1, HD)


def after(x, *earlier):
    return lax.optimization_barrier((x, *earlier))[0]


def local(queries, key_vectors, value_vectors, log_decay, grad_output, out_weight):
    rows, width = queries.shape
    heads, blk_count = width // HD, rows // BLK
    tp, me = lax.axis_size("tp"), lax.axis_index("tp")
    seq, place = lax.axis_size("seq"), lax.axis_index("seq")
    chips = tp // 2
    core = [(i, i ^ 1) for i in range(tp)]

    def from_chip(hops):
        return [(i, (i + 2 * hops) % tp) for i in range(tp)]

    own = grad_output
    sibling = lax.ppermute(own, "tp", core)
    first = []
    for j in range(blk_count):
        piece = own[j * BLK : (j + 1) * BLK]
        first.append([lax.ppermute(piece, "tp", from_chip(d)) for d in range(1, chips)])

    cum = jnp.cumsum(log_decay.reshape(heads, blk_count, BLK), axis=2)
    end = cum[:, :, -1]
    prior = jnp.exp(jnp.cumsum(end, axis=1) - end)
    cum = cum.transpose(1, 0, 2).reshape(blk_count, heads // GROUP, GROUP, BLK)

    own_span = jnp.broadcast_to(jnp.sum(end, axis=1)[None], (seq, heads))
    spans = lax.all_to_all(own_span, "seq", 0, 0, tiled=True)
    share = heads * HD // seq
    pieces = max(share // HD, 1)
    mine = lax.dynamic_slice_in_dim(jnp.exp(spans), place * share // HD, pieces, axis=1)

    local_enter, fwd_total = key_totals(key_vectors, value_vectors, cum)
    fwd_got = swap(fwd_total)

    near = near_product(own, sibling, out_weight)
    fwd_out = chain(after(fwd_got, near), mine, False)
    enter_fwd = swap(fwd_out).reshape(heads, HD, HD)

    total = near
    held = [near, fwd_out, enter_fwd]
    grads, sums = [], []
    for j in range(blk_count):
        wait_for = [total] + ([fwd_out] if j == 1 else []) + ([enter_fwd] if j == 2 else [])
        arrived = []
        for x in first[j]:
            x = after(x, *wait_for)
            arrived += [x, lax.ppermute(x, "tp", core)]
        before = total if j else jnp.zeros((heads, HD, HD), F32)
        grad, part, total = far_product(
            j, j == blk_count - 1, before, arrived, out_weight, near, queries, cum, prior
        )
        grads.append(grad)
        sums.append(part)

    bwd_got = swap(total)
    gq, gk_parts, gv_parts = None, [], []
    half = blk_count // 2
    cum_now = after(cum, total)
    for j in range(blk_count):
        if j == half:
            bwd_out = chain(after(bwd_got, gq), mine, True)
            enter_bwd = swap(bwd_out).reshape(heads, HD, HD)
            cum_now = after(cum, bwd_out)
        gq, gk, gv = block_terms(
            j, queries, key_vectors, value_vectors, grads[j], cum_now, prior, local_enter, enter_fwd, gq
        )
        gk_parts.append(gk)
        gv_parts.append(gv)
    gk, gv = later_terms(key_vectors, value_vectors, gk_parts, gv_parts, sums[1:], cum, enter_bwd)
    return gq, gk, gv


def solution(mesh):
    in_specs = (
        P("seq", "tp"),
        P("seq", "tp"),
        P("seq", "tp"),
        P("tp", "seq"),
        P("seq", "tp"),
        P("tp", None),
    )
    out_specs = (P("seq", "tp"), P("seq", "tp"), P("seq", "tp"))
    return jax.shard_map(local, mesh=mesh, in_specs=in_specs, out_specs=out_specs, check_vma=False)
```

```python
import functools

import jax
import jax.numpy as jnp
from jax import lax
from jax.experimental import pallas as pl
from jax.experimental.pallas import tpu as pltpu
from jax.sharding import PartitionSpec as P

HD = 128
BLK = 256
GROUP = 4
ROW = 16
MIB = 2**20

NN = (((1,), (0,)), ((), ()))
NT = (((1,), (1,)), ((), ()))
TN = (((0,), (0,)), ((), ()))

ANY = pl.BlockSpec(memory_space=pl.ANY)
HBM = pl.BlockSpec(memory_space=pltpu.HBM)
VMEM = pl.BlockSpec(memory_space=pltpu.VMEM)
SMEM = pl.BlockSpec(memory_space=pltpu.SMEM)
BF16 = jnp.bfloat16
F32 = jnp.float32


def mm(left, right, form):
    return lax.dot_general(left, right, form, preferred_element_type=F32)


def cost(flops, nbytes, exps=0):
    return pl.CostEstimate(flops=int(flops), bytes_accessed=int(nbytes), transcendentals=int(exps))


def span(index, size):
    return slice(index * size, (index + 1) * size)


def call(body, name, ins, outs, scratch, limit, estimate, aliases=None):
    return pl.pallas_call(
        body,
        in_specs=[spec for _, spec in ins],
        out_specs=[spec for _, _, spec in outs],
        out_shape=[
            pltpu.HBM(shape, dtype) if spec is HBM else jax.ShapeDtypeStruct(shape, dtype)
            for shape, dtype, spec in outs
        ],
        scratch_shapes=scratch,
        input_output_aliases=aliases or {},
        compiler_params=pltpu.CompilerParams(vmem_limit_bytes=limit * MIB),
        cost_estimate=estimate,
        name=name,
    )(*[pltpu.with_memory_space_constraint(x, pltpu.HBM) if spec is HBM else x for x, spec in ins])


def copy_of(source, target, sem):
    return pltpu.make_async_copy(source, target, sem)


def lanes_of(index, size):
    return pl.ds(pl.multiple_of(index * size, size), size)


def loop(count, body):
    lax.fori_loop(0, count, lambda i, _: (body(i), 0)[1], 0)


def head_in(h):
    return slice(h * HD, (h + 1) * HD)


def key_body(k_hbm, v_hbm, cum_ref, span_ref, local_hbm, total_ref, k_ref, v_ref, local_ref, load_sems, store_sems):
    blk_count, groups, group, _ = cum_ref.shape
    wide = group * HD

    def loads(j):
        rows = pl.ds(j * BLK, BLK)
        return (
            copy_of(k_hbm.at[rows], k_ref.at[rows], load_sems.at[0, j]),
            copy_of(v_hbm.at[rows], v_ref.at[rows], load_sems.at[1, j]),
        )

    def store(j):
        return copy_of(local_ref.at[j], local_hbm.at[j], store_sems.at[j])

    for j in range(blk_count):
        for copy in loads(j):
            copy.start()
    local_ref[0] = jnp.zeros_like(local_ref[0])

    def block(j):
        for copy in loads(j):
            copy.wait()
        store(j).start()
        rows = pl.ds(pl.multiple_of(j * BLK, BLK), BLK)

        def some_heads(g):
            cum = cum_ref[j, g]
            end = cum[:, BLK - 1 : BLK]
            weight = jnp.exp(end - cum)
            end_weight = jnp.exp(end)
            lanes = lanes_of(g, wide)
            these = pl.ds(g * group, group)
            keys, values, entered = k_ref[rows, lanes], v_ref[rows, lanes], local_ref[j, these]
            left = []
            for h in range(group):
                turned = keys[:, head_in(h)].T.astype(F32)
                scaled = (turned * weight[h : h + 1]).astype(BF16)
                sums = mm(scaled, values[:, head_in(h)], NN)
                left.append(entered[h] * end_weight[h : h + 1] + sums)
            local_ref[j + 1, these] = jnp.stack(left)

        loop(groups, some_heads)

    loop(blk_count, block)
    devices, share = total_ref.shape[0], total_ref.shape[1] - ROW
    total_ref[:, :share] = local_ref[blk_count].astype(BF16).reshape(devices, share, HD)
    left, parts = jnp.broadcast_to(span_ref[...], (ROW, HD)), jnp.zeros((ROW, HD), F32)
    at_row = lax.broadcasted_iota(jnp.int32, (ROW, HD), 0)
    for n in range(3):
        rounded = left.astype(BF16).astype(F32)
        parts = jnp.where(at_row == n, rounded, parts)
        left = left - rounded
    for d in range(devices):
        total_ref[d, share:] = parts.astype(BF16)
    for j in range(blk_count):
        store(j).wait()


def key_totals(keys, values, cum, own_span, devices):
    rows, width = keys.shape
    blk_count, heads = cum.shape[0], width // HD
    return call(
        key_body,
        "key_totals",
        [(keys, HBM), (values, HBM), (cum, VMEM), (own_span, VMEM)],
        [
            ((blk_count, heads, HD, HD), F32, HBM),
            ((devices, heads * HD // devices + ROW, HD), BF16, VMEM),
        ],
        [
            pltpu.VMEM((rows, width), BF16),
            pltpu.VMEM((rows, width), BF16),
            pltpu.VMEM((blk_count + 1, heads, HD, HD), F32),
            pltpu.SemaphoreType.DMA((2, blk_count)),
            pltpu.SemaphoreType.DMA((blk_count,)),
        ],
        24,
        cost(2 * rows * width * HD, 4 * rows * width + 4 * blk_count * width * HD),
    )


def near_body(wide, own_hbm, sibling_hbm, w_hbm, out_hbm, grad_ref, w_ref, out_ref, w_sems, grad_sems, out_sems):
    rows, depth = own_hbm.shape
    groups, tiles = w_hbm.shape[0] // wide, rows // BLK
    me = lax.axis_index("tp")
    side = lax.rem(me, 2)
    columns = pl.ds(pl.multiple_of((me - side) * depth, 2 * depth), 2 * depth)

    def w_load(g):
        part = pl.ds(g * wide, wide)
        return copy_of(w_hbm.at[part, columns], w_ref.at[part], w_sems.at[g])

    def grad_loads(r):
        part = pl.ds(r * BLK, BLK)
        return (
            copy_of(own_hbm.at[part], grad_ref.at[part, lanes_of(side, depth)], grad_sems.at[0, r]),
            copy_of(sibling_hbm.at[part], grad_ref.at[part, lanes_of(1 - side, depth)], grad_sems.at[1, r]),
        )

    def store(g):
        return copy_of(out_ref.at[lax.rem(g, 2)], out_hbm.at[:, lanes_of(g, wide)], out_sems.at[lax.rem(g, 2)])

    w_load(0).start()
    for r in range(tiles):
        for copy in grad_loads(r):
            copy.start()
    for g in range(1, groups):
        w_load(g).start()

    def columns_of(g):
        w_load(g).wait()

        @pl.when(g >= 2)
        def _():
            store(g - 2).wait()

        part = w_ref[pl.ds(pl.multiple_of(g * wide, wide), wide)]
        out_ref[lax.rem(g, 2)] = mm(grad_ref[...], part, NT)
        store(g).start()

    for r in range(tiles):
        for copy in grad_loads(r):
            copy.wait()
    loop(groups, columns_of)
    for g in range(max(groups - 2, 0), groups):
        store(g).wait()


def near_product(own, sibling, weight):
    rows, depth = own.shape
    width = weight.shape[0]
    wide = GROUP * HD
    (out,) = call(
        functools.partial(near_body, wide),
        "near_product",
        [(own, HBM), (sibling, HBM), (weight, HBM)],
        [((rows, width), F32, HBM)],
        [
            pltpu.VMEM((rows, 2 * depth), BF16),
            pltpu.VMEM((width, 2 * depth), BF16),
            pltpu.VMEM((2, rows, wide), F32),
            pltpu.SemaphoreType.DMA((width // wide,)),
            pltpu.SemaphoreType.DMA((2, rows // BLK)),
            pltpu.SemaphoreType.DMA((2,)),
        ],
        32,
        cost(4 * rows * width * depth, 4 * depth * (rows + width) + 4 * rows * width),
    )
    return out


def far_sums(blks, g, group, q_ref, cum_ref, prior_ref, grad, before_ref, sums_refs, total_ref):
    wide = group * HD
    lanes, these = lanes_of(g, wide), pl.ds(g * group, group)
    chained = before_ref[these] if before_ref is not None else None
    chained = [chained[h] for h in range(group)] if chained is not None else None
    for n, blk in enumerate(blks):
        weight = jnp.exp(cum_ref[blk, g])
        queries = q_ref[span(n, BLK), lanes]
        sums = []
        for h in range(group):
            turned = queries[:, head_in(h)].T.astype(F32)
            scaled = (turned * weight[h : h + 1]).astype(BF16)
            sums.append(mm(scaled, grad[span(n, BLK), head_in(h)], NN))
        sums_refs[n][these] = jnp.stack(sums)
        if chained is None:
            chained = sums
        else:
            chained = [chained[h] + prior_ref[g * group + h, blk] * sums[h] for h in range(group)]
    total_ref[these] = jnp.stack(chained).astype(total_ref.dtype)


def far_body(chips, blks, keep, before_ref, near_hbm, q_hbm, cum_ref, prior_ref, w_hbm, *refs):
    pieces, refs = refs[: 2 * (chips - 1)], refs[2 * (chips - 1) :]
    count = len(blks)
    (grad_hbm, total_ref, *sums_hbm), refs = refs[: 2 + count], refs[2 + count :]
    w_ref, refs = refs[0], refs[1:]
    if keep:
        (last_near_ref, last_q_ref), refs = refs[:2], refs[2:]
    piece_ref, near_ref, q_ref, grad_ref, sums_ref, piece_sems, load_sems, store_sems = refs
    here = blks[0] * BLK
    rows, depth = pieces[0].shape
    _, groups, group, _ = cum_ref.shape
    wide = group * HD
    me = lax.axis_index("tp")
    side = lax.rem(me, 2)
    chip = lax.div(me, 2)

    def piece_load(n):
        at = 2 * (n // 2) + (side if n % 2 == 0 else 1 - side)
        return copy_of(pieces[n], piece_ref.at[:, lanes_of(at, depth)], piece_sems.at[n])

    def loads(g):
        part, lanes = pl.ds(g * wide, wide), lanes_of(g, wide)
        found = []
        for d in range(1, chips):
            owner = lax.rem(chip + chips - d, chips)
            held = pl.ds((d - 1) * 2 * depth, 2 * depth)
            found.append(
                copy_of(w_hbm.at[part, lanes_of(owner, 2 * depth)], w_ref.at[part, held], load_sems.at[d + 1, g])
            )
        found.append(copy_of(near_hbm.at[pl.ds(here, rows), lanes], near_ref.at[:, lanes], load_sems.at[0, g]))
        found.append(copy_of(q_hbm.at[pl.ds(here, rows), lanes], q_ref.at[:, lanes], load_sems.at[1, g]))
        return found

    def last_loads():
        if not keep:
            return ()
        block = pl.ds(here + rows, BLK)
        return (
            copy_of(near_hbm.at[block], last_near_ref, piece_sems.at[len(pieces)]),
            copy_of(q_hbm.at[block], last_q_ref, piece_sems.at[len(pieces) + 1]),
        )

    def stores(g):
        these, lanes = pl.ds(g * group, group), lanes_of(g, wide)
        return [copy_of(grad_ref.at[:, lanes], grad_hbm.at[:, lanes], store_sems.at[count, g])] + [
            copy_of(sums_ref.at[n, these], sums_hbm[n].at[these], store_sems.at[n, g]) for n in range(count)
        ]

    for n in range(len(pieces)):
        piece_load(n).start()
    for g in range(groups):
        for copy in loads(g):
            copy.start()
    for copy in last_loads():
        copy.start()
    for n in range(len(pieces)):
        piece_load(n).wait()

    def some_heads(g):
        for copy in loads(g):
            copy.wait()
        lanes = lanes_of(g, wide)
        part = pl.ds(pl.multiple_of(g * wide, wide), wide)
        grad = (near_ref[:, lanes] + mm(piece_ref[...], w_ref[part], NT)).astype(BF16)
        grad_ref[:, lanes] = grad
        sums_refs = [sums_ref.at[n] for n in range(count)]
        before = before_ref if blks[0] else None
        far_sums(blks, g, group, q_ref, cum_ref, prior_ref, grad, before, sums_refs, total_ref)
        for copy in stores(g):
            copy.start()

    loop(groups, some_heads)
    for copy in last_loads():
        copy.wait()
    for g in range(groups):
        for copy in stores(g):
            copy.wait()


def far_product(start, keep, before, pieces, weight, near, queries, cum, prior):
    rows, depth = pieces[0].shape
    _, groups, group, _ = cum.shape
    heads = groups * group
    width = heads * HD
    chips = len(pieces) // 2 + 1
    blks = list(range(start, start + rows // BLK))
    states = (heads, HD, HD)
    far_depth = 2 * (chips - 1) * depth
    kept = [((width, far_depth), BF16, VMEM), ((BLK, width), F32, VMEM), ((BLK, width), BF16, VMEM)]
    return call(
        functools.partial(far_body, chips, blks, keep),
        "far_product",
        [(before, VMEM), (near, HBM), (queries, HBM), (cum, VMEM), (prior, SMEM), (weight, HBM)]
        + [(piece, ANY) for piece in pieces],
        [((rows, width), BF16, HBM), (states, F32, VMEM)]
        + [(states, F32, HBM)] * len(blks)
        + (kept if keep else []),
        ([] if keep else [pltpu.VMEM((width, far_depth), BF16)])
        + [
            pltpu.VMEM((rows, far_depth), BF16),
            pltpu.VMEM((rows, width), F32),
            pltpu.VMEM((rows, width), BF16),
            pltpu.VMEM((rows, width), BF16),
            pltpu.VMEM((len(blks), *states), F32),
            pltpu.SemaphoreType.DMA((len(pieces) + 2,)),
            pltpu.SemaphoreType.DMA((chips + 1, groups)),
            pltpu.SemaphoreType.DMA((len(blks) + 1, groups)),
        ],
        32,
        cost(
            2 * rows * width * (far_depth + HD),
            2 * far_depth * (rows + width) + 8 * rows * width + 12 * width * HD,
        ),
    )


def last_body(blk, before_ref, near_ref, q_ref, cum_ref, prior_ref, w_ref, *refs):
    pieces, (grad_hbm, sums_hbm, total_ref, grad_ref, sums_ref, sems) = refs[:-6], refs[-6:]
    depth = pieces[0].shape[1]
    _, groups, group, _ = cum_ref.shape
    wide = group * HD
    side = lax.rem(lax.axis_index("tp"), 2)

    def stores(g):
        these, lanes = pl.ds(g * group, group), lanes_of(g, wide)
        return (
            copy_of(grad_ref.at[:, lanes], grad_hbm.at[:, lanes], sems.at[0, g]),
            copy_of(sums_ref.at[these], sums_hbm.at[these], sems.at[1, g]),
        )

    def some_heads(g):
        lanes = lanes_of(g, wide)
        part = pl.ds(pl.multiple_of(g * wide, wide), wide)
        total = near_ref[:, lanes]
        for n, piece in enumerate(pieces):
            at = 2 * (n // 2) + (side if n % 2 == 0 else 1 - side)
            total += mm(piece[...], w_ref[part, lanes_of(at, depth)], NT)
        grad = total.astype(BF16)
        grad_ref[:, lanes] = grad
        far_sums([blk], g, group, q_ref, cum_ref, prior_ref, grad, before_ref, [sums_ref], total_ref)
        for copy in stores(g):
            copy.start()

    loop(groups, some_heads)
    for g in range(groups):
        for copy in stores(g):
            copy.wait()


def last_product(before, pieces, weight, near, queries, cum, prior):
    rows, depth = pieces[0].shape
    blk_count, groups, group, _ = cum.shape
    heads = groups * group
    width = heads * HD
    states = (heads, HD, HD)
    return call(
        functools.partial(last_body, blk_count - 1),
        "last_product",
        [(before, VMEM), (near, VMEM), (queries, VMEM), (cum, VMEM), (prior, SMEM), (weight, VMEM)]
        + [(piece, VMEM) for piece in pieces],
        [((rows, width), BF16, HBM), (states, F32, HBM), (states, BF16, VMEM)],
        [pltpu.VMEM((rows, width), BF16), pltpu.VMEM(states, F32), pltpu.SemaphoreType.DMA((2, groups))],
        8,
        cost(
            2 * rows * width * (len(pieces) * depth + HD),
            2 * len(pieces) * depth * (rows + width) + 8 * rows * width + 12 * width * HD,
        ),
    )


def block_body(blk, grad_blk, q_hbm, k_hbm, v_hbm, grad_hbm, cum_ref, prior_ref, local_hbm, enter_hbm, *refs):
    refs = refs[1:] if blk else refs
    gq_hbm, gk_hbm, gv_hbm, q_ref, k_ref, v_ref, grad_ref, local_ref, enter_ref = refs[:9]
    gq_ref, gk_ref, gv_ref, load_sems, store_sems = refs[9:]
    _, groups, group, _ = cum_ref.shape
    wide = group * HD
    block = pl.ds(blk * BLK, BLK)

    def loads(g):
        lanes, these = lanes_of(g, wide), pl.ds(g * group, group)
        return (
            copy_of(grad_hbm.at[pl.ds(grad_blk * BLK, BLK), lanes], grad_ref.at[:, lanes], load_sems.at[0, g]),
            copy_of(v_hbm.at[block, lanes], v_ref.at[:, lanes], load_sems.at[1, g]),
            copy_of(q_hbm.at[block, lanes], q_ref.at[:, lanes], load_sems.at[2, g]),
            copy_of(k_hbm.at[block, lanes], k_ref.at[:, lanes], load_sems.at[3, g]),
            copy_of(local_hbm.at[blk, these], local_ref.at[these], load_sems.at[4, g]),
            copy_of(enter_hbm.at[these], enter_ref.at[these], load_sems.at[5, g]),
        )

    def stores(g):
        lanes = lanes_of(g, wide)
        return (
            copy_of(gq_ref.at[:, lanes], gq_hbm.at[block, lanes], store_sems.at[0, g]),
            copy_of(gk_ref.at[:, lanes], gk_hbm.at[:, lanes], store_sems.at[1, g]),
            copy_of(gv_ref.at[:, lanes], gv_hbm.at[:, lanes], store_sems.at[2, g]),
        )

    for g in range(groups):
        for copy in loads(g):
            copy.start()
    at_row = lax.broadcasted_iota(jnp.int32, (BLK, BLK), 0)
    at_col = lax.broadcasted_iota(jnp.int32, (BLK, BLK), 1)
    causal, flipped = at_row >= at_col, at_row <= at_col

    def some_heads(g):
        for copy in loads(g):
            copy.wait()
        rows = cum_ref[blk, g]
        cum = rows.T
        head_weight = jnp.exp(cum)
        lanes, these = lanes_of(g, wide), pl.ds(g * group, group)
        queries, keys, values, grads = q_ref[:, lanes], k_ref[:, lanes], v_ref[:, lanes], grad_ref[:, lanes]
        entered, here = enter_ref[these], local_ref[these]
        gq, gk, gv = [], [], []
        for h in range(group):
            head = head_in(h)
            q, k, v, grad = queries[:, head], keys[:, head], values[:, head], grads[:, head]
            by_row, by_col = cum[:, h : h + 1], rows[h : h + 1, :]
            mask = jnp.exp(jnp.where(causal, by_row - by_col, -1e30))
            turned = jnp.exp(jnp.where(flipped, by_col - by_row, -1e30))
            scores = (mm(grad, v, NT) * mask).astype(BF16)
            turned_scores = (mm(v, grad, NT) * turned).astype(BF16)
            turned_attn = (mm(k, q, NT) * turned).astype(BF16)
            enter = entered[h].astype(F32) * prior_ref[g * group + h, blk] + here[h]
            inter = mm(grad, enter.astype(BF16), NT) * head_weight[:, h : h + 1]
            gq.append((mm(scores, k, NN) + inter).astype(BF16))
            gk.append(mm(turned_scores, q, NN).astype(BF16))
            gv.append(mm(turned_attn, grad, NN).astype(BF16))
        gq_ref[:, lanes] = jnp.concatenate(gq, axis=1)
        gk_ref[:, lanes] = jnp.concatenate(gk, axis=1)
        gv_ref[:, lanes] = jnp.concatenate(gv, axis=1)
        for copy in stores(g):
            copy.start()

    loop(groups, some_heads)
    for g in range(groups):
        for copy in stores(g):
            copy.wait()


def block_terms(blk, grad_blk, queries, keys, values, grad, cum, prior, local_enter, enter, gq):
    rows, width = queries.shape
    heads, groups = width // HD, cum.shape[1]
    tile = pltpu.VMEM((BLK, width), BF16)
    part = ((BLK, width), BF16, HBM)
    ins = [queries, keys, values, grad, cum, prior, local_enter, enter]
    specs = [HBM, HBM, HBM, HBM, VMEM, SMEM, HBM, HBM]
    if blk:
        ins, specs = ins + [gq], specs + [HBM]
    return call(
        functools.partial(block_body, blk, grad_blk),
        "block_terms",
        list(zip(ins, specs)),
        [((rows, width), BF16, HBM), part, part],
        [tile] * 4
        + [pltpu.VMEM((heads, HD, HD), F32), pltpu.VMEM((heads, HD, HD), BF16)]
        + [tile] * 3
        + [pltpu.SemaphoreType.DMA((6, groups)), pltpu.SemaphoreType.DMA((3, groups))],
        20,
        cost(BLK * width * (10 * BLK + 2 * HD), 14 * BLK * width + 6 * width * HD, BLK * heads * BLK),
        {8: 0} if blk else None,
    )


def later_body(k_hbm, v_hbm, cum_ref, enter_hbm, *refs):
    blk_count, groups, group, _ = cum_ref.shape
    gk_parts, gv_parts = refs[:blk_count], refs[blk_count : 2 * blk_count]
    sums_hbm = refs[2 * blk_count : 3 * blk_count - 1]
    gk_hbm, gv_hbm, k_ref, v_ref, gk_ref, gv_ref, sums_ref, enter_ref, carry_ref = refs[3 * blk_count - 1 : -2]
    load_sems, store_sems = refs[-2:]
    wide = group * HD

    def rows_of(j):
        return pl.ds(pl.multiple_of(j * BLK, BLK), BLK)

    def sums_load(j, at):
        return copy_of(sums_hbm[at - 1], sums_ref.at[j], load_sems.at[4, j])

    def loads(j, at):
        rows = rows_of(j)
        return [
            copy_of(v_hbm.at[rows], v_ref.at[rows], load_sems.at[0, j]),
            copy_of(k_hbm.at[rows], k_ref.at[rows], load_sems.at[1, j]),
            copy_of(gk_parts[at], gk_ref.at[rows], load_sems.at[2, j]),
            copy_of(gv_parts[at], gv_ref.at[rows], load_sems.at[3, j]),
        ]

    def stores(j):
        rows = rows_of(j)
        return (
            copy_of(gk_ref.at[rows], gk_hbm.at[rows], store_sems.at[0, j]),
            copy_of(gv_ref.at[rows], gv_hbm.at[rows], store_sems.at[1, j]),
        )

    enter_load = copy_of(enter_hbm, enter_ref, load_sems.at[0, blk_count])
    enter_load.start()
    for j in reversed(range(blk_count)):
        for copy in loads(j, j):
            copy.start()
        if j:
            sums_load(j, j).start()
    sums_ref[0] = jnp.zeros_like(sums_ref[0])
    enter_load.wait()
    carry_ref[...] = enter_ref[...].astype(F32)

    def block(back):
        j = blk_count - 1 - back
        rows = rows_of(j)
        for copy in loads(j, 0):
            copy.wait()

        @pl.when(j > 0)
        def _():
            sums_load(j, 1).wait()

        def some_heads(g):
            cum = cum_ref[j, g].T
            end = cum[BLK - 1 : BLK, :]
            weight = jnp.exp(end - cum)
            end_weight = jnp.exp(end)
            lanes, these = lanes_of(g, wide), pl.ds(g * group, group)
            keys, values = k_ref[rows, lanes], v_ref[rows, lanes]
            gk_in, gv_in = gk_ref[rows, lanes], gv_ref[rows, lanes]
            entered, here = carry_ref[these], sums_ref[j, these]
            gk, gv, left = [], [], []
            for h in range(group):
                head, tail = head_in(h), weight[:, h : h + 1]
                enter = entered[h].astype(BF16)
                gk.append((gk_in[:, head].astype(F32) + mm(values[:, head], enter, NT) * tail).astype(BF16))
                gv.append((gv_in[:, head].astype(F32) + mm(keys[:, head], enter, NN) * tail).astype(BF16))
                left.append(entered[h] * end_weight[:, h : h + 1] + here[h])
            gk_ref[rows, lanes] = jnp.concatenate(gk, axis=1)
            gv_ref[rows, lanes] = jnp.concatenate(gv, axis=1)
            carry_ref[these] = jnp.stack(left)

        loop(groups, some_heads)
        for copy in stores(j):
            copy.start()

    loop(blk_count, block)
    for j in range(blk_count):
        for copy in stores(j):
            copy.wait()


def later_terms(keys, values, gk_parts, gv_parts, sums, cum, enter):
    rows, width = keys.shape
    heads, blk_count = width // HD, rows // BLK
    whole = pltpu.VMEM((rows, width), BF16)
    out = ((rows, width), BF16, HBM)
    return call(
        later_body,
        "later_terms",
        [(keys, HBM), (values, HBM), (cum, VMEM), (enter, HBM)]
        + [(x, HBM) for x in gk_parts + gv_parts + sums],
        [out, out],
        [whole] * 4
        + [
            pltpu.VMEM((blk_count, heads, HD, HD), F32),
            pltpu.VMEM((heads, HD, HD), BF16),
            pltpu.VMEM((heads, HD, HD), F32),
            pltpu.SemaphoreType.DMA((5, blk_count + 1)),
            pltpu.SemaphoreType.DMA((2, blk_count)),
        ],
        28,
        cost(rows * width * 4 * HD, 12 * rows * width + 4 * blk_count * width * HD),
    )


def chain_body(reverse, got_ref, weight_ref, out_ref):
    devices, share = out_ref.shape[0], out_ref.shape[1]
    pieces = weight_ref.shape[1]
    part = share // pieces
    for p in range(pieces):
        rows = span(p, part)
        carry = jnp.zeros((part, HD), F32)
        for place in reversed(range(devices)) if reverse else range(devices):
            out_ref[place, rows] = carry.astype(BF16)
            carry = weight_ref[place, p] * carry + got_ref[place, rows].astype(F32)


def chain(got, weights, share, reverse):
    devices = got.shape[0]
    (out,) = call(
        functools.partial(chain_body, reverse),
        "chain_states",
        [(got, VMEM), (weights, SMEM)],
        [((devices, share, HD), BF16, VMEM)],
        [],
        16,
        cost(2 * devices * share * HD, 4 * devices * share * HD),
    )
    return out


def swap(x):
    devices = lax.axis_size("seq")
    flat = x.reshape(-1, HD)
    return lax.all_to_all(flat, "seq", 0, 0, tiled=True).reshape(devices, -1, HD)


def after(x, *earlier):
    return lax.optimization_barrier((x, *earlier))[0]


def local(queries, key_vectors, value_vectors, log_decay, grad_output, out_weight):
    rows, width = queries.shape
    heads, blk_count = width // HD, rows // BLK
    tp, me = lax.axis_size("tp"), lax.axis_index("tp")
    seq, place = lax.axis_size("seq"), lax.axis_index("seq")
    chips = tp // 2
    core = [(i, i ^ 1) for i in range(tp)]

    def from_chip(hops):
        return [(i, (i + 2 * hops) % tp) for i in range(tp)]

    own = grad_output
    sibling = lax.ppermute(own, "tp", core)
    starts = [0, blk_count - 2, blk_count - 1, blk_count]
    cuts, rest = [], own
    for a, b in zip(starts, starts[1:]):
        cuts.append(rest[a * BLK : b * BLK])
        rest = after(own, cuts[0])
    first = [[lax.ppermute(x, "tp", from_chip(d)) for d in range(1, chips)] for x in cuts]

    def hand_on(j, *earlier):
        arrived = []
        for x in first[j]:
            x = after(x, *earlier)
            arrived += [x, lax.ppermute(x, "tp", core)]
        return arrived

    cum = jnp.cumsum(after(log_decay, *cuts).reshape(heads, blk_count, BLK), axis=2)
    end = cum[:, :, -1]
    prior = jnp.exp(jnp.cumsum(end, axis=1) - end)
    cum = cum.transpose(1, 0, 2).reshape(blk_count, heads // GROUP, GROUP, BLK)
    own_span = jnp.pad(jnp.sum(end, axis=1), (0, HD - heads))[None]

    local_enter, fwd_total = key_totals(key_vectors, value_vectors, cum, own_span, seq)
    fwd_got = swap(fwd_total)

    near = near_product(own, sibling, out_weight)
    fwd_got = after(fwd_got, near)

    share = heads * HD // seq
    pieces = max(share // HD, 1)
    spans = jnp.sum(fwd_got[:, share : share + 3, :heads].astype(F32), axis=1)
    mine = lax.dynamic_slice_in_dim(jnp.exp(spans), place * share // HD, pieces, axis=1)
    fwd_out = chain(fwd_got, mine, share, False)
    enter_fwd = swap(fwd_out).reshape(heads, HD, HD)

    arrived = hand_on(0, near, fwd_out)
    total = jnp.zeros((heads, HD, HD), F32)
    early_grad, total, *sums = far_product(
        0, False, total, arrived, out_weight, near, queries, cum, prior
    )
    arrived = hand_on(1, early_grad)
    next_grad, total, next_sums, far_weight, last_near, last_queries = far_product(
        starts[1], True, total, arrived, out_weight, near, queries, after(cum, enter_fwd), prior
    )
    arrived = hand_on(2, next_grad)
    last_grad, last_sums, total = last_product(
        total, arrived, far_weight, last_near, last_queries, cum, prior
    )
    sums += [next_sums, last_sums]
    grads = [(j, early_grad) for j in range(starts[1])] + [(0, next_grad), (0, last_grad)]
    gq, parts = None, []

    bwd_got = swap(total)
    cum_now = after(cum, total)
    for j in range(blk_count):
        if j == blk_count // 2:
            bwd_out = chain(after(bwd_got, gq), mine, share, True)
            enter_bwd = swap(bwd_out).reshape(heads, HD, HD)
            cum_now = after(cum, bwd_out)
        gq, *part = block_terms(
            j,
            grads[j][0],
            queries,
            key_vectors,
            value_vectors,
            grads[j][1],
            cum_now,
            prior,
            local_enter,
            enter_fwd,
            gq,
        )
        parts.append(part)
    gk_parts, gv_parts = [list(x) for x in zip(*parts)]
    gk, gv = later_terms(key_vectors, value_vectors, gk_parts, gv_parts, sums[1:], cum, enter_bwd)
    return gq, gk, gv


def solution(mesh):
    in_specs = (
        P("seq", "tp"),
        P("seq", "tp"),
        P("seq", "tp"),
        P("tp", "seq"),
        P("seq", "tp"),
        P("tp", None),
    )
    out_specs = (P("seq", "tp"), P("seq", "tp"), P("seq", "tp"))
    return jax.shard_map(local, mesh=mesh, in_specs=in_specs, out_specs=out_specs, check_vma=False)
```

```python
import functools

import jax
import jax.numpy as jnp
from jax import lax
from jax.experimental import pallas as pl
from jax.experimental.pallas import tpu as pltpu
from jax.sharding import PartitionSpec as P

HD = 128
BLK = 256
GROUP = 4
ROW = 16
MIB = 2**20

NN = (((1,), (0,)), ((), ()))
NT = (((1,), (1,)), ((), ()))
TN = (((0,), (0,)), ((), ()))

ANY = pl.BlockSpec(memory_space=pl.ANY)
HBM = pl.BlockSpec(memory_space=pltpu.HBM)
VMEM = pl.BlockSpec(memory_space=pltpu.VMEM)
SMEM = pl.BlockSpec(memory_space=pltpu.SMEM)
BF16 = jnp.bfloat16
F32 = jnp.float32


def mm(left, right, form):
    return lax.dot_general(left, right, form, preferred_element_type=F32)


def cost(flops, nbytes, exps=0):
    return pl.CostEstimate(flops=int(flops), bytes_accessed=int(nbytes), transcendentals=int(exps))


def span(index, size):
    return slice(index * size, (index + 1) * size)


def call(body, name, ins, outs, scratch, limit, estimate, aliases=None):
    return pl.pallas_call(
        body,
        in_specs=[spec for _, spec in ins],
        out_specs=[spec for _, _, spec in outs],
        out_shape=[
            pltpu.HBM(shape, dtype) if spec is HBM else jax.ShapeDtypeStruct(shape, dtype)
            for shape, dtype, spec in outs
        ],
        scratch_shapes=scratch,
        input_output_aliases=aliases or {},
        compiler_params=pltpu.CompilerParams(vmem_limit_bytes=limit * MIB),
        cost_estimate=estimate,
        name=name,
    )(*[pltpu.with_memory_space_constraint(x, pltpu.HBM) if spec is HBM else x for x, spec in ins])


def copy_of(source, target, sem):
    return pltpu.make_async_copy(source, target, sem)


def lanes_of(index, size):
    return pl.ds(pl.multiple_of(index * size, size), size)


def loop(count, body):
    lax.fori_loop(0, count, lambda i, _: (body(i), 0)[1], 0)


def head_in(h):
    return slice(h * HD, (h + 1) * HD)


def key_body(k_hbm, v_hbm, cum_ref, span_ref, local_hbm, total_ref, k_ref, v_ref, local_ref, load_sems, store_sems):
    blk_count, groups, group, _ = cum_ref.shape
    wide = group * HD

    def loads(j):
        rows = pl.ds(j * BLK, BLK)
        return (
            copy_of(k_hbm.at[rows], k_ref.at[rows], load_sems.at[0, j]),
            copy_of(v_hbm.at[rows], v_ref.at[rows], load_sems.at[1, j]),
        )

    def store(j):
        return copy_of(local_ref.at[j], local_hbm.at[j], store_sems.at[j])

    for j in range(min(2, blk_count)):
        for copy in loads(j):
            copy.start()
    local_ref[0] = jnp.zeros_like(local_ref[0])

    def block(j):
        for copy in loads(j):
            copy.wait()

        @pl.when(j + 2 < blk_count)
        def _():
            for copy in loads(j + 2):
                copy.start()

        store(j).start()
        rows = pl.ds(pl.multiple_of(j * BLK, BLK), BLK)

        def some_heads(g):
            cum = cum_ref[j, g]
            end = cum[:, BLK - 1 : BLK]
            weight = jnp.exp(end - cum)
            end_weight = jnp.exp(end)
            lanes = lanes_of(g, wide)
            these = pl.ds(g * group, group)
            keys, values, entered = k_ref[rows, lanes], v_ref[rows, lanes], local_ref[j, these]
            left = []
            for h in range(group):
                turned = keys[:, head_in(h)].T.astype(F32)
                scaled = (turned * weight[h : h + 1]).astype(BF16)
                sums = mm(scaled, values[:, head_in(h)], NN)
                left.append(entered[h] * end_weight[h : h + 1] + sums)
            local_ref[j + 1, these] = jnp.stack(left)

        loop(groups, some_heads)

    loop(blk_count, block)
    devices, share = total_ref.shape[0], total_ref.shape[1] - ROW
    total_ref[:, :share] = local_ref[blk_count].astype(BF16).reshape(devices, share, HD)
    left, parts = jnp.broadcast_to(span_ref[...], (ROW, HD)), jnp.zeros((ROW, HD), F32)
    at_row = lax.broadcasted_iota(jnp.int32, (ROW, HD), 0)
    for n in range(3):
        rounded = left.astype(BF16).astype(F32)
        parts = jnp.where(at_row == n, rounded, parts)
        left = left - rounded
    for d in range(devices):
        total_ref[d, share:] = parts.astype(BF16)
    for j in range(blk_count):
        store(j).wait()


def key_totals(keys, values, cum, own_span, devices):
    rows, width = keys.shape
    blk_count, heads = cum.shape[0], width // HD
    return call(
        key_body,
        "key_totals",
        [(keys, HBM), (values, HBM), (cum, VMEM), (own_span, VMEM)],
        [
            ((blk_count, heads, HD, HD), F32, HBM),
            ((devices, heads * HD // devices + ROW, HD), BF16, VMEM),
        ],
        [
            pltpu.VMEM((rows, width), BF16),
            pltpu.VMEM((rows, width), BF16),
            pltpu.VMEM((blk_count + 1, heads, HD, HD), F32),
            pltpu.SemaphoreType.DMA((2, blk_count)),
            pltpu.SemaphoreType.DMA((blk_count,)),
        ],
        24,
        cost(2 * rows * width * HD, 4 * rows * width + 4 * blk_count * width * HD),
    )


def near_body(wide, own_hbm, sibling_hbm, w_hbm, out_hbm, grad_ref, w_ref, out_ref, w_sems, grad_sems, out_sems):
    rows, depth = own_hbm.shape
    groups, tiles = w_hbm.shape[0] // wide, rows // BLK
    me = lax.axis_index("tp")
    side = lax.rem(me, 2)
    columns = pl.ds(pl.multiple_of((me - side) * depth, 2 * depth), 2 * depth)

    def w_load(g):
        part = pl.ds(g * wide, wide)
        return copy_of(w_hbm.at[part, columns], w_ref.at[part], w_sems.at[g])

    def grad_loads(r):
        part = pl.ds(r * BLK, BLK)
        return (
            copy_of(own_hbm.at[part], grad_ref.at[part, lanes_of(side, depth)], grad_sems.at[0, r]),
            copy_of(sibling_hbm.at[part], grad_ref.at[part, lanes_of(1 - side, depth)], grad_sems.at[1, r]),
        )

    def store(g):
        return copy_of(out_ref.at[lax.rem(g, 2)], out_hbm.at[:, lanes_of(g, wide)], out_sems.at[lax.rem(g, 2)])

    w_load(0).start()
    for r in range(tiles):
        for copy in grad_loads(r):
            copy.start()

    def first_tile(r):
        for copy in grad_loads(r):
            copy.wait()
        these = pl.ds(pl.multiple_of(r * BLK, BLK), BLK)
        out_ref[0, these] = mm(grad_ref[these], w_ref[:wide], NT)

    def columns_of(before):
        g = before + 1
        w_load(g).wait()

        @pl.when(g + 1 < groups)
        def _():
            w_load(g + 1).start()

        @pl.when(g >= 2)
        def _():
            store(g - 2).wait()

        part = w_ref[pl.ds(pl.multiple_of(g * wide, wide), wide)]
        out_ref[lax.rem(g, 2)] = mm(grad_ref[...], part, NT)
        store(g).start()

    w_load(0).wait()
    if groups > 1:
        w_load(1).start()
    loop(tiles, first_tile)
    store(0).start()
    loop(groups - 1, columns_of)
    for g in range(max(groups - 2, 0), groups):
        store(g).wait()


def near_product(own, sibling, weight):
    rows, depth = own.shape
    width = weight.shape[0]
    wide = GROUP * HD
    (out,) = call(
        functools.partial(near_body, wide),
        "near_product",
        [(own, HBM), (sibling, HBM), (weight, HBM)],
        [((rows, width), F32, HBM)],
        [
            pltpu.VMEM((rows, 2 * depth), BF16),
            pltpu.VMEM((width, 2 * depth), BF16),
            pltpu.VMEM((2, rows, wide), F32),
            pltpu.SemaphoreType.DMA((width // wide,)),
            pltpu.SemaphoreType.DMA((2, rows // BLK)),
            pltpu.SemaphoreType.DMA((2,)),
        ],
        32,
        cost(4 * rows * width * depth, 4 * depth * (rows + width) + 4 * rows * width),
    )
    return out


def far_sums(blks, g, group, q_ref, cum_ref, prior_ref, grad, before_ref, sums_refs, total_ref):
    wide = group * HD
    lanes, these = lanes_of(g, wide), pl.ds(g * group, group)
    chained = None
    if before_ref is not None:
        before = before_ref[these]
        chained = [before[h] for h in range(group)]
    for n, blk in enumerate(blks):
        weight = jnp.exp(cum_ref[blk, g])
        queries = q_ref[span(n, BLK), lanes]
        sums = []
        for h in range(group):
            turned = queries[:, head_in(h)].T.astype(F32)
            scaled = (turned * weight[h : h + 1]).astype(BF16)
            sums.append(mm(scaled, grad[span(n, BLK), head_in(h)], NN))
        sums_refs[n][these] = jnp.stack(sums)
        if chained is None:
            chained = sums
        else:
            chained = [chained[h] + prior_ref[g * group + h, blk] * sums[h] for h in range(group)]
    total_ref[these] = jnp.stack(chained).astype(total_ref.dtype)


def far_grad(near, pieces, w_ref, g, wide, side):
    part = pl.ds(pl.multiple_of(g * wide, wide), wide)
    for n, piece in enumerate(pieces):
        at = 2 * (n // 2) + (side if n % 2 == 0 else 1 - side)
        near += mm(piece[...], w_ref[part, lanes_of(at, piece.shape[1])], NT)
    return near.astype(BF16)


def far_body(chips, blks, direct, *refs):
    count = len(blks)
    if blks[0]:
        before_hbm, refs = refs[0], refs[1:]
    near_hbm, q_hbm, cum_ref, prior_ref, w_hbm, *refs = refs
    pieces, refs = refs[: 2 * (chips - 1)], refs[2 * (chips - 1) :]
    total_ref, grad_hbm, *sums_hbm = refs[: 2 + count]
    refs = refs[2 + count :]
    if direct:
        held = pieces
    else:
        held, refs = refs[: len(pieces)], refs[len(pieces) :]
    w_ref, near_ref, q_ref, grad_ref, before_ref, sums_ref, piece_sems, load_sems, store_sems = refs
    rows, depth = pieces[0].shape
    _, groups, group, _ = cum_ref.shape
    wide = group * HD
    me = lax.axis_index("tp")
    side = lax.rem(me, 2)
    chip = lax.div(me, 2)
    here = pl.ds(blks[0] * BLK, rows)

    def loads(g):
        part, lanes, these = pl.ds(g * wide, wide), lanes_of(g, wide), pl.ds(g * group, group)
        found = []
        for d in range(1, chips):
            owner = lax.rem(chip + chips - d, chips)
            columns = pl.ds((d - 1) * 2 * depth, 2 * depth)
            found.append(
                copy_of(w_hbm.at[part, lanes_of(owner, 2 * depth)], w_ref.at[part, columns], load_sems.at[d + 2, g])
            )
        found.append(copy_of(near_hbm.at[here, lanes], near_ref.at[:, lanes], load_sems.at[0, g]))
        found.append(copy_of(q_hbm.at[here, lanes], q_ref.at[:, lanes], load_sems.at[1, g]))
        if blks[0]:
            found.append(copy_of(before_hbm.at[these], before_ref.at[these], load_sems.at[2, g]))
        return found

    def piece_loads():
        if direct:
            return ()
        return [copy_of(piece, held[n], piece_sems.at[n]) for n, piece in enumerate(pieces)]

    def store(g):
        lanes = lanes_of(g, wide)
        return copy_of(grad_ref.at[:, lanes], grad_hbm.at[:, lanes], store_sems.at[count, g])

    def sums_stores(g):
        these = pl.ds(g * group, group)
        return [copy_of(sums_ref.at[n, these], sums_hbm[n].at[these], store_sems.at[n, g]) for n in range(count)]

    def product(g):
        for copy in loads(g):
            copy.wait()
        return far_grad(near_ref[:, lanes_of(g, wide)], held, w_ref, g, wide, side)

    def sums_of(g, grad):
        far_sums(
            blks, g, group, q_ref, cum_ref, prior_ref, grad, before_ref if blks[0] else None,
            [sums_ref.at[n] for n in range(count)], total_ref,
        )

    for copy in loads(0):
        copy.start()
    for copy in piece_loads():
        copy.start()
    for copy in loads(1):
        copy.start()
    for copy in piece_loads():
        copy.wait()
    grad_ref[:, :wide] = product(0)
    store(0).start()

    def step(g):
        @pl.when(g + 2 < groups)
        def _():
            for copy in loads(g + 2):
                copy.start()

        mine = grad_ref[:, lanes_of(g, wide)]
        grad = product(g + 1)
        sums_of(g, mine)
        grad_ref[:, lanes_of(g + 1, wide)] = grad
        store(g + 1).start()
        for copy in sums_stores(g):
            copy.start()

    loop(groups - 1, step)
    sums_of(groups - 1, grad_ref[:, lanes_of(groups - 1, wide)])
    for copy in sums_stores(groups - 1):
        copy.start()
    for g in range(groups):
        store(g).wait()
        for copy in sums_stores(g):
            copy.wait()


def far_product(start, before, pieces, weight, near, queries, cum, prior):
    rows, depth = pieces[0].shape
    blk_count, groups, group, _ = cum.shape
    heads = groups * group
    width = heads * HD
    chips = len(pieces) // 2 + 1
    count = rows // BLK
    blks = list(range(start, start + count))
    last = start + count == blk_count
    states = (heads, HD, HD)
    far_depth = 2 * (chips - 1) * depth
    total, grad, *sums = call(
        functools.partial(far_body, chips, blks, last),
        "far_product",
        ([(before, HBM)] if start else [])
        + [(near, HBM), (queries, HBM), (cum, VMEM), (prior, SMEM), (weight, HBM)]
        + [(piece, VMEM if last else HBM) for piece in pieces],
        [(states, BF16 if last else F32, VMEM), ((rows, width), BF16, HBM)] + [(states, F32, HBM)] * count,
        ([] if last else [pltpu.VMEM(piece.shape, BF16) for piece in pieces])
        + [
            pltpu.VMEM((width, far_depth), BF16),
            pltpu.VMEM((rows, width), F32),
            pltpu.VMEM((rows, width), BF16),
            pltpu.VMEM((rows, width), BF16),
            pltpu.VMEM(states, F32),
            pltpu.VMEM((count, *states), F32),
            pltpu.SemaphoreType.DMA((len(pieces),)),
            pltpu.SemaphoreType.DMA((chips + 2, groups)),
            pltpu.SemaphoreType.DMA((count + 1, groups)),
        ],
        36,
        cost(
            2 * rows * width * (far_depth + HD),
            2 * far_depth * (rows + width) + 8 * rows * width + 12 * width * HD,
        ),
    )
    return grad, sums, total


def block_body(blks, grad_blks, q_hbm, k_hbm, v_hbm, grads_hbm, cum_ref, prior_ref, local_hbm, enter_ref, *refs):
    count = len(blks)
    gq_hbm, gk_hbm, gv_hbm, q_ref, k_ref, v_ref, grad_ref, local_ref, gq_ref, gk_ref, gv_ref = refs[-13:-2]
    load_sems, store_sems = refs[-2:]
    _, groups, group, _ = cum_ref.shape
    wide = group * HD

    def loads(n, g):
        lanes, these = lanes_of(g, wide), pl.ds(g * group, group)
        block = pl.ds((blks[0] + n) * BLK, BLK)
        return (
            copy_of(v_hbm.at[block, lanes], v_ref.at[n, :, lanes], load_sems.at[0, n, g]),
            copy_of(q_hbm.at[block, lanes], q_ref.at[n, :, lanes], load_sems.at[1, n, g]),
            copy_of(k_hbm.at[block, lanes], k_ref.at[n, :, lanes], load_sems.at[2, n, g]),
            copy_of(local_hbm.at[blks[0] + n, these], local_ref.at[n, these], load_sems.at[3, n, g]),
        )

    def grad_load(n, g, source=0):
        lanes = lanes_of(g, wide)
        block = pl.ds(grad_blks[source] * BLK, BLK)
        return copy_of(grads_hbm[source].at[block, lanes], grad_ref.at[n, :, lanes], load_sems.at[4, n, g])

    def stores(n, g):
        lanes = lanes_of(g, wide)
        block, part = pl.ds((blks[0] + n) * BLK, BLK), pl.ds(n * BLK, BLK)
        return (
            copy_of(gq_ref.at[n, :, lanes], gq_hbm.at[block, lanes], store_sems.at[0, n, g]),
            copy_of(gk_ref.at[n, :, lanes], gk_hbm.at[part, lanes], store_sems.at[1, n, g]),
            copy_of(gv_ref.at[n, :, lanes], gv_hbm.at[part, lanes], store_sems.at[2, n, g]),
        )

    def start(n, g):
        grad_load(n, g, n).start()
        for copy in loads(n, g):
            copy.start()

    for g in range(groups):
        start(0, g)
    at_row = lax.broadcasted_iota(jnp.int32, (BLK, BLK), 0)
    at_col = lax.broadcasted_iota(jnp.int32, (BLK, BLK), 1)
    causal, flipped = at_row >= at_col, at_row <= at_col

    def some_heads(at):
        n, g = lax.div(at, groups), lax.rem(at, groups)
        blk = blks[0] + n
        for m in range(1, count):

            @pl.when(n == m - 1)
            def _(m=m):
                start(m, g)

        grad_load(n, g).wait()
        for copy in loads(n, g):
            copy.wait()
        rows = cum_ref[blk, g]
        cum = rows.T
        head_weight = jnp.exp(cum)
        lanes, these = lanes_of(g, wide), pl.ds(g * group, group)
        queries, keys, values, grads = (ref[n, :, lanes] for ref in (q_ref, k_ref, v_ref, grad_ref))
        entered, here = enter_ref[these], local_ref[n, these]
        gq, gk, gv = [], [], []
        for h in range(group):
            head = head_in(h)
            q, k, v, grad = queries[:, head], keys[:, head], values[:, head], grads[:, head]
            by_row, by_col = cum[:, h : h + 1], rows[h : h + 1, :]
            mask = jnp.exp(jnp.where(causal, by_row - by_col, -1e30))
            turned = jnp.exp(jnp.where(flipped, by_col - by_row, -1e30))
            scores = (mm(grad, v, NT) * mask).astype(BF16)
            turned_scores = (mm(v, grad, NT) * turned).astype(BF16)
            turned_attn = (mm(k, q, NT) * turned).astype(BF16)
            enter = entered[h].astype(F32) * prior_ref[g * group + h, blk] + here[h]
            inter = mm(grad, enter.astype(BF16), NT) * head_weight[:, h : h + 1]
            gq.append((mm(scores, k, NN) + inter).astype(BF16))
            gk.append(mm(turned_scores, q, NN).astype(BF16))
            gv.append(mm(turned_attn, grad, NN).astype(BF16))
        gq_ref[n, :, lanes] = jnp.concatenate(gq, axis=1)
        gk_ref[n, :, lanes] = jnp.concatenate(gk, axis=1)
        gv_ref[n, :, lanes] = jnp.concatenate(gv, axis=1)
        for copy in stores(n, g):
            copy.start()

    loop(count * groups, some_heads)
    for n in range(count):
        for g in range(groups):
            for copy in stores(n, g):
                copy.wait()


def block_terms(blks, queries, keys, values, grads, cum, prior, local_enter, enter, gq):
    rows, width = queries.shape
    heads, groups, count = width // HD, cum.shape[1], len(blks)
    tile = pltpu.VMEM((count, BLK, width), BF16)
    part = ((count * BLK, width), BF16, HBM)
    ins = [(queries, HBM), (keys, HBM), (values, HBM)] + [(grad, HBM) for _, grad in grads]
    ins += [(cum, VMEM), (prior, SMEM), (local_enter, HBM), (enter, VMEM)]
    if gq is not None:
        ins.append((gq, HBM))

    def body(q_hbm, k_hbm, v_hbm, *refs):
        block_body(blks, [at for at, _ in grads], q_hbm, k_hbm, v_hbm, refs[:count], *refs[count:])

    return call(
        body,
        "block_terms",
        ins,
        [((rows, width), BF16, HBM), part, part],
        [tile] * 4
        + [pltpu.VMEM((count, heads, HD, HD), F32)]
        + [tile] * 3
        + [pltpu.SemaphoreType.DMA((5, count, groups)), pltpu.SemaphoreType.DMA((3, count, groups))],
        28,
        cost(
            count * BLK * width * (10 * BLK + 2 * HD),
            count * (14 * BLK * width + 6 * width * HD),
            count * BLK * heads * BLK,
        ),
        {len(ins) - 1: 0} if gq is not None else None,
    )


def later_body(k_hbm, v_hbm, cum_ref, enter_hbm, *refs):
    blk_count, groups, group, _ = cum_ref.shape
    halves = len(refs) - 11 - (blk_count - 1)
    gk_parts, gv_parts = refs[: halves // 2], refs[halves // 2 : halves]
    each = blk_count // len(gk_parts)
    sums_hbm = refs[halves : halves + blk_count - 1]
    gk_hbm, gv_hbm, k_ref, v_ref, gk_ref, gv_ref, sums_ref, enter_ref, carry_ref = refs[halves + blk_count - 1 : -2]
    load_sems, store_sems = refs[-2:]
    wide = group * HD

    def loads(j, g):
        rows, lanes, these = pl.ds(j * BLK, BLK), lanes_of(g, wide), pl.ds(g * group, group)
        part = pl.ds(j % each * BLK, BLK)
        found = [
            copy_of(v_hbm.at[rows, lanes], v_ref.at[rows, lanes], load_sems.at[0, j, g]),
            copy_of(k_hbm.at[rows, lanes], k_ref.at[rows, lanes], load_sems.at[1, j, g]),
            copy_of(gk_parts[j // each].at[part, lanes], gk_ref.at[rows, lanes], load_sems.at[2, j, g]),
            copy_of(gv_parts[j // each].at[part, lanes], gv_ref.at[rows, lanes], load_sems.at[3, j, g]),
        ]
        if j:
            found.append(copy_of(sums_hbm[j - 1].at[these], sums_ref.at[j, these], load_sems.at[4, j, g]))
        return found

    def stores(j, g):
        rows, lanes = pl.ds(j * BLK, BLK), lanes_of(g, wide)
        return (
            copy_of(gk_ref.at[rows, lanes], gk_hbm.at[rows, lanes], store_sems.at[0, j, g]),
            copy_of(gv_ref.at[rows, lanes], gv_hbm.at[rows, lanes], store_sems.at[1, j, g]),
        )

    enter_load = copy_of(enter_hbm, enter_ref, load_sems.at[4, 0, 0])
    enter_load.start()
    for g in range(groups):
        for copy in loads(blk_count - 1, g):
            copy.start()
    enter_load.wait()
    for j in reversed(range(blk_count)):

        def some_heads(g, j=j):
            if j:
                for copy in loads(j - 1, g):
                    copy.start()
            for copy in loads(j, g):
                copy.wait()
            rows = span(j, BLK)
            cum = cum_ref[j, g].T
            end = cum[BLK - 1 : BLK, :]
            weight = jnp.exp(end - cum)
            end_weight = jnp.exp(end)
            lanes, these = lanes_of(g, wide), pl.ds(g * group, group)
            keys, values = k_ref[rows, lanes], v_ref[rows, lanes]
            gk_in, gv_in = gk_ref[rows, lanes], gv_ref[rows, lanes]
            entered = enter_ref[these].astype(F32) if j + 1 == blk_count else carry_ref[these]
            here = sums_ref[j, these] if j else None
            gk, gv, left = [], [], []
            for h in range(group):
                head, tail = head_in(h), weight[:, h : h + 1]
                enter = entered[h].astype(BF16)
                gk.append((gk_in[:, head].astype(F32) + mm(values[:, head], enter, NT) * tail).astype(BF16))
                gv.append((gv_in[:, head].astype(F32) + mm(keys[:, head], enter, NN) * tail).astype(BF16))
                if j:
                    left.append(entered[h] * end_weight[:, h : h + 1] + here[h])
            gk_ref[rows, lanes] = jnp.concatenate(gk, axis=1)
            gv_ref[rows, lanes] = jnp.concatenate(gv, axis=1)
            if j:
                carry_ref[these] = jnp.stack(left)
            for copy in stores(j, g):
                copy.start()

        loop(groups, some_heads)
    for j in range(blk_count):
        for g in range(groups):
            for copy in stores(j, g):
                copy.wait()


def later_terms(keys, values, gk_parts, gv_parts, sums, cum, enter):
    rows, width = keys.shape
    heads, blk_count = width // HD, rows // BLK
    whole = pltpu.VMEM((rows, width), BF16)
    out = ((rows, width), BF16, HBM)
    return call(
        later_body,
        "later_terms",
        [(keys, HBM), (values, HBM), (cum, VMEM), (enter, HBM)]
        + [(x, HBM) for x in gk_parts + gv_parts + sums],
        [out, out],
        [whole] * 4
        + [
            pltpu.VMEM((blk_count, heads, HD, HD), F32),
            pltpu.VMEM((heads, HD, HD), BF16),
            pltpu.VMEM((heads, HD, HD), F32),
            pltpu.SemaphoreType.DMA((5, blk_count, cum.shape[1])),
            pltpu.SemaphoreType.DMA((2, blk_count, cum.shape[1])),
        ],
        28,
        cost(rows * width * 4 * HD, 12 * rows * width + 4 * blk_count * width * HD),
    )


def chain_body(reverse, got_ref, weight_ref, out_ref):
    devices, share = out_ref.shape[0], out_ref.shape[1]
    pieces = weight_ref.shape[1]
    part = share // pieces
    for p in range(pieces):
        rows = span(p, part)
        carry = jnp.zeros((part, HD), F32)
        for place in reversed(range(devices)) if reverse else range(devices):
            out_ref[place, rows] = carry.astype(BF16)
            carry = weight_ref[place, p] * carry + got_ref[place, rows].astype(F32)


def chain(got, weights, share, reverse):
    devices = got.shape[0]
    (out,) = call(
        functools.partial(chain_body, reverse),
        "chain_states",
        [(got, VMEM), (weights, SMEM)],
        [((devices, share, HD), BF16, VMEM)],
        [],
        16,
        cost(2 * devices * share * HD, 4 * devices * share * HD),
    )
    return out


def swap(x):
    devices = lax.axis_size("seq")
    flat = x.reshape(-1, HD)
    return lax.all_to_all(flat, "seq", 0, 0, tiled=True).reshape(devices, -1, HD)


def after(x, *earlier):
    return lax.optimization_barrier((x, *earlier))[0]


def local(queries, key_vectors, value_vectors, log_decay, grad_output, out_weight):
    rows, width = queries.shape
    heads, blk_count = width // HD, rows // BLK
    tp, me = lax.axis_size("tp"), lax.axis_index("tp")
    seq, place = lax.axis_size("seq"), lax.axis_index("seq")
    chips = tp // 2
    core = [(i, i ^ 1) for i in range(tp)]

    def from_chip(hops):
        return [(i, (i + 2 * hops) % tp) for i in range(tp)]

    own = grad_output
    sibling = lax.ppermute(own, "tp", core)
    starts = [0, 1, blk_count - 1, blk_count]
    cuts, rest = [], own
    for a, b in zip(starts, starts[1:]):
        cuts.append(rest[a * BLK : b * BLK])
        rest = after(own, cuts[0])
    first = [[lax.ppermute(x, "tp", from_chip(d)) for d in range(1, chips)] for x in cuts]

    def hand_on(j, *earlier):
        arrived = []
        for x in first[j]:
            x = after(x, *earlier)
            arrived += [x, lax.ppermute(x, "tp", core)]
        return arrived

    cum = jnp.cumsum(after(log_decay, *cuts).reshape(heads, blk_count, BLK), axis=2)
    end = cum[:, :, -1]
    prior = jnp.exp(jnp.cumsum(end, axis=1) - end)
    cum = cum.transpose(1, 0, 2).reshape(blk_count, heads // GROUP, GROUP, BLK)
    own_span = jnp.pad(jnp.sum(end, axis=1), (0, HD - heads))[None]

    local_enter, fwd_total = key_totals(key_vectors, value_vectors, cum, own_span, seq)
    fwd_got = swap(fwd_total)

    arrived = hand_on(0, fwd_total)
    near = near_product(own, after(sibling, arrived[0]), out_weight)
    fwd_got = after(fwd_got, near)

    share = heads * HD // seq
    pieces = max(share // HD, 1)
    spans = jnp.sum(fwd_got[:, share : share + 3, :heads].astype(F32), axis=1)
    mine = lax.dynamic_slice_in_dim(jnp.exp(spans), place * share // HD, pieces, axis=1)
    fwd_out = chain(fwd_got, mine, share, False)
    enter_fwd = swap(fwd_out).reshape(heads, HD, HD)

    grads, sums, total, cum_now = [], [], None, after(cum, fwd_out)
    for part, start in enumerate(starts[:-1]):
        if part:
            arrived = hand_on(part, total)
            cum_now = after(cum, enter_fwd) if part == 2 else cum
        grad, some, total = far_product(start, total, arrived, out_weight, near, queries, cum_now, prior)
        grads += [(j, grad) for j in range(grad.shape[0] // BLK)]
        sums += some
    gq, parts = None, []

    bwd_got = swap(total)
    cum_now = after(cum, total)
    half = blk_count // 2
    for blks in (list(range(half)), list(range(half, blk_count))):
        if blks[0]:
            bwd_out = chain(after(bwd_got, gq), mine, share, True)
            enter_bwd = swap(bwd_out).reshape(heads, HD, HD)
            cum_now = after(cum, bwd_out)
        gq, *part = block_terms(
            blks,
            queries,
            key_vectors,
            value_vectors,
            [grads[j] for j in blks],
            cum_now,
            prior,
            local_enter,
            enter_fwd,
            gq,
        )
        parts.append(part)
    gk_parts, gv_parts = [list(x) for x in zip(*parts)]
    gk, gv = later_terms(key_vectors, value_vectors, gk_parts, gv_parts, sums[1:], cum, enter_bwd)
    return gq, gk, gv


def solution(mesh):
    in_specs = (
        P("seq", "tp"),
        P("seq", "tp"),
        P("seq", "tp"),
        P("tp", "seq"),
        P("seq", "tp"),
        P("tp", None),
    )
    out_specs = (P("seq", "tp"), P("seq", "tp"), P("seq", "tp"))
    return jax.shard_map(local, mesh=mesh, in_specs=in_specs, out_specs=out_specs, check_vma=False)
```

```python
import functools

import jax
import jax.numpy as jnp
from jax import lax
from jax.experimental import pallas as pl
from jax.experimental.pallas import tpu as pltpu
from jax.sharding import PartitionSpec as P

HD = 128
BLK = 256
GROUP = 4
PAIR = 2
ROW = 16
MIB = 2**20

NN = (((1,), (0,)), ((), ()))
NT = (((1,), (1,)), ((), ()))
TN = (((0,), (0,)), ((), ()))

ANY = pl.BlockSpec(memory_space=pl.ANY)
HBM = pl.BlockSpec(memory_space=pltpu.HBM)
VMEM = pl.BlockSpec(memory_space=pltpu.VMEM)
SMEM = pl.BlockSpec(memory_space=pltpu.SMEM)
BF16 = jnp.bfloat16
F32 = jnp.float32


def mm(left, right, form):
    return lax.dot_general(left, right, form, preferred_element_type=F32)


def cost(flops, nbytes, exps=0):
    return pl.CostEstimate(flops=int(flops), bytes_accessed=int(nbytes), transcendentals=int(exps))


def span(index, size):
    return slice(index * size, (index + 1) * size)


def call(body, name, ins, outs, scratch, limit, estimate, aliases=None):
    return pl.pallas_call(
        body,
        in_specs=[spec for _, spec in ins],
        out_specs=[spec for _, _, spec in outs],
        out_shape=[
            pltpu.HBM(shape, dtype) if spec is HBM else jax.ShapeDtypeStruct(shape, dtype)
            for shape, dtype, spec in outs
        ],
        scratch_shapes=scratch,
        input_output_aliases=aliases or {},
        compiler_params=pltpu.CompilerParams(vmem_limit_bytes=limit * MIB),
        cost_estimate=estimate,
        name=name,
    )(*[pltpu.with_memory_space_constraint(x, pltpu.HBM) if spec is HBM else x for x, spec in ins])


def copy_of(source, target, sem):
    return pltpu.make_async_copy(source, target, sem)


def lanes_of(index, size):
    return pl.ds(pl.multiple_of(index * size, size), size)


def loop(count, body):
    lax.fori_loop(0, count, lambda i, _: (body(i), 0)[1], 0)


def head_in(h):
    return slice(h * HD, (h + 1) * HD)


def prefix_sums(x):
    at = lax.broadcasted_iota(jnp.int32, x.shape, 1)
    step = 1
    while step < x.shape[1]:
        x = x + jnp.where(at >= step, pltpu.roll(x, step, 1), 0.0)
        step *= 2
    return x


def key_body(cuts, k_hbm, v_hbm, decay_hbm, grad_hbm, local_hbm, total_ref, cum_ref, pair_ref, *refs):
    cut_hbm, refs = refs[: len(cuts)], refs[len(cuts) :]
    decay_ref, cut_ref, k_ref, v_ref, local_ref, load_sems, store_sems, cut_sems = refs
    blk_count, groups, group, _ = cum_ref.shape
    heads, wide = groups * group, group * HD

    def loads(j):
        rows = pl.ds(j * BLK, BLK)
        return (
            copy_of(k_hbm.at[rows], k_ref.at[rows], load_sems.at[0, j]),
            copy_of(v_hbm.at[rows], v_ref.at[rows], load_sems.at[1, j]),
        )

    def store(j):
        return copy_of(local_ref.at[j], local_hbm.at[j], store_sems.at[j])

    origin = cuts[0][0]
    cut_load = copy_of(grad_hbm.at[pl.ds(origin, cuts[-1][1] - origin)], cut_ref, cut_sems.at[len(cuts)])

    def cut_store(n):
        first, last = cuts[n]
        return copy_of(cut_ref.at[pl.ds(first - origin, last - first)], cut_hbm[n], cut_sems.at[n])

    decay_load = copy_of(decay_hbm, decay_ref, cut_sems.at[len(cuts) + 1])
    decay_load.start()
    for j in range(min(2, blk_count)):
        for copy in loads(j):
            copy.start()
    cut_load.start()
    decay_load.wait()
    span_of = jnp.zeros((heads, 1), F32)
    for j in range(blk_count):
        cum = prefix_sums(decay_ref[:, span(j, BLK)])
        for g in range(groups):
            cum_ref[j, g] = cum[span(g, group)]
        for g in range(heads // PAIR):
            pair_ref[j, g] = cum[span(g, PAIR)]
        span_of = span_of + cum[:, BLK - 1 : BLK]
    local_ref[0] = jnp.zeros_like(local_ref[0])
    cut_load.wait()
    for n in range(len(cuts)):
        cut_store(n).start()

    def block(j):
        for copy in loads(j):
            copy.wait()

        @pl.when(j + 2 < blk_count)
        def _():
            for copy in loads(j + 2):
                copy.start()

        store(j).start()
        rows = pl.ds(pl.multiple_of(j * BLK, BLK), BLK)

        def some_heads(g):
            cum = cum_ref[j, g]
            end = cum[:, BLK - 1 : BLK]
            weight = jnp.exp(end - cum)
            end_weight = jnp.exp(end)
            lanes = lanes_of(g, wide)
            these = pl.ds(g * group, group)
            keys, values, entered = k_ref[rows, lanes], v_ref[rows, lanes], local_ref[j, these]
            left = []
            for h in range(group):
                turned = keys[:, head_in(h)].T.astype(F32)
                scaled = (turned * weight[h : h + 1]).astype(BF16)
                sums = mm(scaled, values[:, head_in(h)], NN)
                left.append(entered[h] * end_weight[h : h + 1] + sums)
            local_ref[j + 1, these] = jnp.stack(left)

        loop(groups, some_heads)

    loop(blk_count, block)
    devices, share = total_ref.shape[0], total_ref.shape[1] - ROW
    total_ref[:, :share] = local_ref[blk_count].astype(BF16).reshape(devices, share, HD)

    diagonal = lax.broadcasted_iota(jnp.int32, (heads, HD), 0) == lax.broadcasted_iota(jnp.int32, (heads, HD), 1)
    spans = jnp.sum(jnp.where(diagonal, span_of, 0.0), axis=0, keepdims=True)
    left, parts = jnp.broadcast_to(spans, (ROW, HD)), jnp.zeros((ROW, HD), F32)
    at_row = lax.broadcasted_iota(jnp.int32, (ROW, HD), 0)
    for n in range(3):
        rounded = left.astype(BF16).astype(F32)
        parts = jnp.where(at_row == n, rounded, parts)
        left = left - rounded
    for d in range(devices):
        total_ref[d, share:] = parts.astype(BF16)
    for j in range(blk_count):
        store(j).wait()
    for n in range(len(cuts)):
        cut_store(n).wait()


def key_totals(keys, values, log_decay, grad, cuts, devices):
    rows, width = keys.shape
    blk_count, heads = rows // BLK, width // HD
    local_enter, total, cum, pair_cum, *parts = call(
        functools.partial(key_body, cuts),
        "key_totals",
        [(keys, HBM), (values, HBM), (log_decay, HBM), (grad, HBM)],
        [
            ((blk_count, heads, HD, HD), F32, HBM),
            ((devices, heads * HD // devices + ROW, HD), BF16, VMEM),
            ((blk_count, heads // GROUP, GROUP, BLK), F32, VMEM),
            ((blk_count, heads // PAIR, PAIR, BLK), F32, VMEM),
        ]
        + [((last - first, grad.shape[1]), BF16, HBM) for first, last in cuts],
        [
            pltpu.VMEM(log_decay.shape, F32),
            pltpu.VMEM((cuts[-1][1] - cuts[0][0], grad.shape[1]), BF16),
            pltpu.VMEM((rows, width), BF16),
            pltpu.VMEM((rows, width), BF16),
            pltpu.VMEM((blk_count + 1, heads, HD, HD), F32),
            pltpu.SemaphoreType.DMA((2, blk_count)),
            pltpu.SemaphoreType.DMA((blk_count,)),
            pltpu.SemaphoreType.DMA((len(cuts) + 2,)),
        ],
        24,
        cost(2 * rows * width * HD, 4 * rows * width + 4 * blk_count * width * HD),
    )
    return local_enter, total, cum, pair_cum, parts


def near_body(wide, own_hbm, sibling_hbm, w_hbm, out_hbm, grad_ref, w_ref, out_ref, w_sems, grad_sems, out_sems):
    rows, depth = own_hbm.shape
    groups, tiles = w_hbm.shape[0] // wide, rows // BLK
    me = lax.axis_index("tp")
    side = lax.rem(me, 2)
    columns = pl.ds(pl.multiple_of((me - side) * depth, 2 * depth), 2 * depth)

    def w_load(g):
        part = pl.ds(g * wide, wide)
        return copy_of(w_hbm.at[part, columns], w_ref.at[part], w_sems.at[g])

    def grad_loads(r):
        part = pl.ds(r * BLK, BLK)
        return (
            copy_of(own_hbm.at[part], grad_ref.at[part, lanes_of(side, depth)], grad_sems.at[0, r]),
            copy_of(sibling_hbm.at[part], grad_ref.at[part, lanes_of(1 - side, depth)], grad_sems.at[1, r]),
        )

    def store(g):
        return copy_of(out_ref.at[lax.rem(g, 2)], out_hbm.at[:, lanes_of(g, wide)], out_sems.at[lax.rem(g, 2)])

    w_load(0).start()
    for r in range(tiles):
        for copy in grad_loads(r):
            copy.start()

    def first_tile(r):
        for copy in grad_loads(r):
            copy.wait()
        these = pl.ds(pl.multiple_of(r * BLK, BLK), BLK)
        out_ref[0, these] = mm(grad_ref[these], w_ref[:wide], NT)

    def columns_of(before):
        g = before + 1
        w_load(g).wait()

        @pl.when(g + 1 < groups)
        def _():
            w_load(g + 1).start()

        @pl.when(g >= 2)
        def _():
            store(g - 2).wait()

        part = w_ref[pl.ds(pl.multiple_of(g * wide, wide), wide)]
        out_ref[lax.rem(g, 2)] = mm(grad_ref[...], part, NT)
        store(g).start()

    w_load(0).wait()
    if groups > 1:
        w_load(1).start()
    loop(tiles, first_tile)
    store(0).start()
    loop(groups - 1, columns_of)
    for g in range(max(groups - 2, 0), groups):
        store(g).wait()


def near_product(own, sibling, weight):
    rows, depth = own.shape
    width = weight.shape[0]
    wide = GROUP * HD
    (out,) = call(
        functools.partial(near_body, wide),
        "near_product",
        [(own, HBM), (sibling, HBM), (weight, HBM)],
        [((rows, width), F32, HBM)],
        [
            pltpu.VMEM((rows, 2 * depth), BF16),
            pltpu.VMEM((width, 2 * depth), BF16),
            pltpu.VMEM((2, rows, wide), F32),
            pltpu.SemaphoreType.DMA((width // wide,)),
            pltpu.SemaphoreType.DMA((2, rows // BLK)),
            pltpu.SemaphoreType.DMA((2,)),
        ],
        32,
        cost(4 * rows * width * depth, 4 * depth * (rows + width) + 4 * rows * width),
    )
    return out


def far_sums(blks, g, group, q_ref, cum_ref, prior_ref, grad, before_ref, sums_refs, total_ref):
    wide = group * HD
    lanes, these = lanes_of(g, wide), pl.ds(g * group, group)
    chained = None
    if before_ref is not None:
        before = before_ref[these]
        chained = [before[h] for h in range(group)]
    for n, blk in enumerate(blks):
        weight = jnp.exp(cum_ref[blk, g])
        queries = q_ref[span(n, BLK), lanes]
        sums = []
        for h in range(group):
            turned = queries[:, head_in(h)].T.astype(F32)
            scaled = (turned * weight[h : h + 1]).astype(BF16)
            sums.append(mm(scaled, grad[span(n, BLK), head_in(h)], NN))
        sums_refs[n][these] = jnp.stack(sums)
        if chained is None:
            chained = sums
        else:
            chained = [chained[h] + prior_ref[g * group + h, blk] * sums[h] for h in range(group)]
    total_ref[these] = jnp.stack(chained).astype(total_ref.dtype)


def far_grad(near, pieces, w_ref, g, wide, side):
    part = pl.ds(pl.multiple_of(g * wide, wide), wide)
    for n, piece in enumerate(pieces):
        at = 2 * (n // 2) + (side if n % 2 == 0 else 1 - side)
        near += mm(piece[...], w_ref[part, lanes_of(at, piece.shape[1])], NT)
    return near.astype(BF16)


def far_body(chips, blks, direct, *refs):
    count = len(blks)
    if blks[0]:
        before_hbm, refs = refs[0], refs[1:]
    near_hbm, q_hbm, cum_ref, prior_ref, w_hbm, *refs = refs
    pieces, refs = refs[: 2 * (chips - 1)], refs[2 * (chips - 1) :]
    total_ref, grad_hbm, *sums_hbm = refs[: 2 + count]
    refs = refs[2 + count :]
    if direct:
        held, total_hbm = pieces, None
    else:
        held, total_hbm, total_ref, refs = refs[: len(pieces)], total_ref, refs[len(pieces)], refs[len(pieces) + 1 :]
    w_ref, near_ref, q_ref, grad_ref, before_ref, sums_ref, piece_sems, load_sems, store_sems = refs
    rows, depth = pieces[0].shape
    _, groups, group, _ = cum_ref.shape
    wide = group * HD
    me = lax.axis_index("tp")
    side = lax.rem(me, 2)
    chip = lax.div(me, 2)
    here = pl.ds(blks[0] * BLK, rows)

    def loads(g):
        part, lanes, these = pl.ds(g * wide, wide), lanes_of(g, wide), pl.ds(g * group, group)
        found = []
        for d in range(1, chips):
            owner = lax.rem(chip + chips - d, chips)
            columns = pl.ds((d - 1) * 2 * depth, 2 * depth)
            found.append(
                copy_of(w_hbm.at[part, lanes_of(owner, 2 * depth)], w_ref.at[part, columns], load_sems.at[d + 2, g])
            )
        found.append(copy_of(near_hbm.at[here, lanes], near_ref.at[:, lanes], load_sems.at[0, g]))
        found.append(copy_of(q_hbm.at[here, lanes], q_ref.at[:, lanes], load_sems.at[1, g]))
        if blks[0]:
            found.append(copy_of(before_hbm.at[these], before_ref.at[these], load_sems.at[2, g]))
        return found

    def piece_loads():
        if direct:
            return ()
        return [copy_of(piece, held[n], piece_sems.at[n]) for n, piece in enumerate(pieces)]

    def store(g):
        lanes = lanes_of(g, wide)
        return copy_of(grad_ref.at[:, lanes], grad_hbm.at[:, lanes], store_sems.at[count, g])

    def sums_stores(g):
        these = pl.ds(g * group, group)
        found = [copy_of(sums_ref.at[n, these], sums_hbm[n].at[these], store_sems.at[n, g]) for n in range(count)]
        if total_hbm is not None:
            found.append(copy_of(total_ref.at[these], total_hbm.at[these], store_sems.at[count + 1, g]))
        return found

    def product(g):
        for copy in loads(g):
            copy.wait()
        return far_grad(near_ref[:, lanes_of(g, wide)], held, w_ref, g, wide, side)

    def sums_of(g, grad):
        far_sums(
            blks, g, group, q_ref, cum_ref, prior_ref, grad, before_ref if blks[0] else None,
            [sums_ref.at[n] for n in range(count)], total_ref,
        )

    for copy in loads(0):
        copy.start()
    for copy in piece_loads():
        copy.start()
    for copy in loads(1):
        copy.start()
    for copy in piece_loads():
        copy.wait()
    for copy in loads(2) if groups > 2 else ():
        copy.start()
    grad_ref[:, :wide] = product(0)
    store(0).start()

    def step(g):
        @pl.when(g + 3 < groups)
        def _():
            for copy in loads(g + 3):
                copy.start()

        mine = grad_ref[:, lanes_of(g, wide)]
        grad = product(g + 1)
        sums_of(g, mine)
        grad_ref[:, lanes_of(g + 1, wide)] = grad
        store(g + 1).start()
        for copy in sums_stores(g):
            copy.start()

    loop(groups - 1, step)
    sums_of(groups - 1, grad_ref[:, lanes_of(groups - 1, wide)])
    for copy in sums_stores(groups - 1):
        copy.start()
    for g in range(groups):
        store(g).wait()
        for copy in sums_stores(g):
            copy.wait()


def far_product(start, before, pieces, weight, near, queries, cum, prior):
    rows, depth = pieces[0].shape
    blk_count, groups, group, _ = cum.shape
    heads = groups * group
    width = heads * HD
    chips = len(pieces) // 2 + 1
    count = rows // BLK
    blks = list(range(start, start + count))
    last = start + count == blk_count
    states = (heads, HD, HD)
    far_depth = 2 * (chips - 1) * depth
    total, grad, *sums = call(
        functools.partial(far_body, chips, blks, last),
        "far_product",
        ([(before, HBM)] if start else [])
        + [(near, HBM), (queries, HBM), (cum, VMEM), (prior, SMEM), (weight, HBM)]
        + [(piece, VMEM if last else ANY) for piece in pieces],
        [(states, BF16 if last else F32, VMEM if last else HBM), ((rows, width), BF16, HBM)] + [(states, F32, HBM)] * count,
        ([] if last else [pltpu.VMEM(piece.shape, BF16) for piece in pieces] + [pltpu.VMEM(states, F32)])
        + [
            pltpu.VMEM((width, far_depth), BF16),
            pltpu.VMEM((rows, width), F32),
            pltpu.VMEM((rows, width), BF16),
            pltpu.VMEM((rows, width), BF16),
            pltpu.VMEM(states, F32),
            pltpu.VMEM((count, *states), F32),
            pltpu.SemaphoreType.DMA((len(pieces),)),
            pltpu.SemaphoreType.DMA((chips + 2, groups)),
            pltpu.SemaphoreType.DMA((count + 2, groups)),
        ],
        36,
        cost(
            2 * rows * width * (far_depth + HD),
            2 * far_depth * (rows + width) + 8 * rows * width + 12 * width * HD,
        ),
    )
    return grad, sums, total


def block_body(blks, grad_blks, q_hbm, k_hbm, v_hbm, grads_hbm, cum_ref, prior_ref, local_hbm, enter_ref, *refs):
    count = len(blks)
    gq_hbm, gk_hbm, gv_hbm, q_ref, k_ref, v_ref, grad_ref, local_ref, gq_ref, gk_ref, gv_ref = refs[-13:-2]
    load_sems, store_sems = refs[-2:]
    _, groups, group, _ = cum_ref.shape
    wide = group * HD

    def loads(n, g):
        lanes, these = lanes_of(g, wide), pl.ds(g * group, group)
        block = pl.ds((blks[0] + n) * BLK, BLK)
        return (
            copy_of(v_hbm.at[block, lanes], v_ref.at[n, :, lanes], load_sems.at[0, n, g]),
            copy_of(q_hbm.at[block, lanes], q_ref.at[n, :, lanes], load_sems.at[1, n, g]),
            copy_of(k_hbm.at[block, lanes], k_ref.at[n, :, lanes], load_sems.at[2, n, g]),
            copy_of(local_hbm.at[blks[0] + n, these], local_ref.at[n, these], load_sems.at[3, n, g]),
        )

    def grad_load(n, g, source=0):
        lanes = lanes_of(g, wide)
        block = pl.ds(grad_blks[source] * BLK, BLK)
        return copy_of(grads_hbm[source].at[block, lanes], grad_ref.at[n, :, lanes], load_sems.at[4, n, g])

    def stores(n, g):
        lanes = lanes_of(g, wide)
        block, part = pl.ds((blks[0] + n) * BLK, BLK), pl.ds(n * BLK, BLK)
        return (
            copy_of(gq_ref.at[n, :, lanes], gq_hbm.at[block, lanes], store_sems.at[0, n, g]),
            copy_of(gk_ref.at[n, :, lanes], gk_hbm.at[part, lanes], store_sems.at[1, n, g]),
            copy_of(gv_ref.at[n, :, lanes], gv_hbm.at[part, lanes], store_sems.at[2, n, g]),
        )

    def start(n, g):
        grad_load(n, g, n).start()
        for copy in loads(n, g):
            copy.start()

    for g in range(groups):
        start(0, g)
    at_row = lax.broadcasted_iota(jnp.int32, (BLK, BLK), 0)
    at_col = lax.broadcasted_iota(jnp.int32, (BLK, BLK), 1)
    causal, flipped = at_row >= at_col, at_row <= at_col

    def some_heads(at):
        n, g = lax.div(at, groups), lax.rem(at, groups)
        blk = blks[0] + n
        for m in range(1, count):

            @pl.when(n == m - 1)
            def _(m=m):
                start(m, g)

        grad_load(n, g).wait()
        for copy in loads(n, g):
            copy.wait()
        rows = cum_ref[blk, g]
        cum = rows.T
        head_weight = jnp.exp(cum)
        lanes, these = lanes_of(g, wide), pl.ds(g * group, group)
        queries, keys, values, grads = (ref[n, :, lanes] for ref in (q_ref, k_ref, v_ref, grad_ref))
        entered, here = enter_ref[these], local_ref[n, these]
        gq, gk, gv = [], [], []
        for h in range(group):
            head = head_in(h)
            q, k, v, grad = queries[:, head], keys[:, head], values[:, head], grads[:, head]
            by_row, by_col = cum[:, h : h + 1], rows[h : h + 1, :]
            mask = jnp.exp(jnp.where(causal, by_row - by_col, -1e30))
            turned = jnp.exp(jnp.where(flipped, by_col - by_row, -1e30))
            scores = (mm(grad, v, NT) * mask).astype(BF16)
            turned_scores = (mm(v, grad, NT) * turned).astype(BF16)
            turned_attn = (mm(k, q, NT) * turned).astype(BF16)
            enter = entered[h].astype(F32) * prior_ref[g * group + h, blk] + here[h]
            inter = mm(grad, enter.astype(BF16), NT) * head_weight[:, h : h + 1]
            gq.append((mm(scores, k, NN) + inter).astype(BF16))
            gk.append(mm(turned_scores, q, NN).astype(BF16))
            gv.append(mm(turned_attn, grad, NN).astype(BF16))
        gq_ref[n, :, lanes] = jnp.concatenate(gq, axis=1)
        gk_ref[n, :, lanes] = jnp.concatenate(gk, axis=1)
        gv_ref[n, :, lanes] = jnp.concatenate(gv, axis=1)
        for copy in stores(n, g):
            copy.start()

    loop(count * groups, some_heads)
    for n in range(count):
        for g in range(groups):
            for copy in stores(n, g):
                copy.wait()


def block_terms(blks, queries, keys, values, grads, cum, prior, local_enter, enter, gq):
    rows, width = queries.shape
    heads, groups, count = width // HD, cum.shape[1], len(blks)
    tile = pltpu.VMEM((count, BLK, width), BF16)
    part = ((count * BLK, width), BF16, HBM)
    ins = [(queries, HBM), (keys, HBM), (values, HBM)] + [(grad, HBM) for _, grad in grads]
    ins += [(cum, VMEM), (prior, SMEM), (local_enter, HBM), (enter, VMEM)]
    if gq is not None:
        ins.append((gq, HBM))

    def body(q_hbm, k_hbm, v_hbm, *refs):
        block_body(blks, [at for at, _ in grads], q_hbm, k_hbm, v_hbm, refs[:count], *refs[count:])

    return call(
        body,
        "block_terms",
        ins,
        [((rows, width), BF16, HBM), part, part],
        [tile] * 4
        + [pltpu.VMEM((count, heads, HD, HD), F32)]
        + [tile] * 3
        + [pltpu.SemaphoreType.DMA((5, count, groups)), pltpu.SemaphoreType.DMA((3, count, groups))],
        28,
        cost(
            count * BLK * width * (10 * BLK + 2 * HD),
            count * (14 * BLK * width + 6 * width * HD),
            count * BLK * heads * BLK,
        ),
        {len(ins) - 1: 0} if gq is not None else None,
    )


def later_body(k_hbm, v_hbm, cum_ref, enter_ref, *refs):
    blk_count, groups, group, _ = cum_ref.shape
    halves = len(refs) - 10 - (blk_count - 1)
    gk_parts, gv_parts = refs[: halves // 2], refs[halves // 2 : halves]
    each = blk_count // len(gk_parts)
    sums_hbm = refs[halves : halves + blk_count - 1]
    gk_hbm, gv_hbm, k_ref, v_ref, gk_ref, gv_ref, sums_ref, carry_ref = refs[halves + blk_count - 1 : -2]
    load_sems, store_sems = refs[-2:]
    wide = group * HD

    def loads(j, g):
        rows, lanes, these = pl.ds(j * BLK, BLK), lanes_of(g, wide), pl.ds(g * group, group)
        part = pl.ds(j % each * BLK, BLK)
        found = [
            copy_of(v_hbm.at[rows, lanes], v_ref.at[rows, lanes], load_sems.at[0, j, g]),
            copy_of(k_hbm.at[rows, lanes], k_ref.at[rows, lanes], load_sems.at[1, j, g]),
            copy_of(gk_parts[j // each].at[part, lanes], gk_ref.at[rows, lanes], load_sems.at[2, j, g]),
            copy_of(gv_parts[j // each].at[part, lanes], gv_ref.at[rows, lanes], load_sems.at[3, j, g]),
        ]
        if j:
            found.append(copy_of(sums_hbm[j - 1].at[these], sums_ref.at[j, these], load_sems.at[4, j, g]))
        return found

    def stores(j, g):
        rows, lanes = pl.ds(j * BLK, BLK), lanes_of(g, wide)
        return (
            copy_of(gk_ref.at[rows, lanes], gk_hbm.at[rows, lanes], store_sems.at[0, j, g]),
            copy_of(gv_ref.at[rows, lanes], gv_hbm.at[rows, lanes], store_sems.at[1, j, g]),
        )

    for g in range(groups):
        for copy in loads(blk_count - 1, g):
            copy.start()
    for j in reversed(range(blk_count)):

        def some_heads(g, j=j):
            if j:
                for copy in loads(j - 1, g):
                    copy.start()
            for copy in loads(j, g):
                copy.wait()
            rows = span(j, BLK)
            cum = cum_ref[j, g].T
            end = cum[BLK - 1 : BLK, :]
            weight = jnp.exp(end - cum)
            end_weight = jnp.exp(end)
            lanes, these = lanes_of(g, wide), pl.ds(g * group, group)
            keys, values = k_ref[rows, lanes], v_ref[rows, lanes]
            gk_in, gv_in = gk_ref[rows, lanes], gv_ref[rows, lanes]
            entered = enter_ref[these].astype(F32) if j + 1 == blk_count else carry_ref[these]
            here = sums_ref[j, these] if j else None
            gk, gv, left = [], [], []
            for h in range(group):
                head, tail = head_in(h), weight[:, h : h + 1]
                enter = entered[h].astype(BF16)
                gk.append((gk_in[:, head].astype(F32) + mm(values[:, head], enter, NT) * tail).astype(BF16))
                gv.append((gv_in[:, head].astype(F32) + mm(keys[:, head], enter, NN) * tail).astype(BF16))
                if j:
                    left.append(entered[h] * end_weight[:, h : h + 1] + here[h])
            gk_ref[rows, lanes] = jnp.concatenate(gk, axis=1)
            gv_ref[rows, lanes] = jnp.concatenate(gv, axis=1)
            if j:
                carry_ref[these] = jnp.stack(left)
            for copy in stores(j, g):
                copy.start()

        loop(groups, some_heads)
    for j in range(blk_count):
        for g in range(groups):
            for copy in stores(j, g):
                copy.wait()


def later_terms(keys, values, gk_parts, gv_parts, sums, cum, enter):
    rows, width = keys.shape
    heads, blk_count = width // HD, rows // BLK
    whole = pltpu.VMEM((rows, width), BF16)
    out = ((rows, width), BF16, HBM)
    return call(
        later_body,
        "later_terms",
        [(keys, HBM), (values, HBM), (cum, VMEM), (enter, VMEM)]
        + [(x, HBM) for x in gk_parts + gv_parts + sums],
        [out, out],
        [whole] * 4
        + [
            pltpu.VMEM((blk_count, heads, HD, HD), F32),
            pltpu.VMEM((heads, HD, HD), F32),
            pltpu.SemaphoreType.DMA((5, blk_count, cum.shape[1])),
            pltpu.SemaphoreType.DMA((2, blk_count, cum.shape[1])),
        ],
        28,
        cost(rows * width * 4 * HD, 12 * rows * width + 4 * blk_count * width * HD),
    )


def chain_body(reverse, got_ref, weight_ref, out_ref):
    devices, share = out_ref.shape[0], out_ref.shape[1]
    pieces = weight_ref.shape[1]
    part = share // pieces
    for p in range(pieces):
        rows = span(p, part)
        carry = jnp.zeros((part, HD), F32)
        for place in reversed(range(devices)) if reverse else range(devices):
            out_ref[place, rows] = carry.astype(BF16)
            carry = weight_ref[place, p] * carry + got_ref[place, rows].astype(F32)


def chain(got, weights, share, reverse):
    devices = got.shape[0]
    (out,) = call(
        functools.partial(chain_body, reverse),
        "chain_states",
        [(got, VMEM), (weights, SMEM)],
        [((devices, share, HD), BF16, VMEM)],
        [],
        16,
        cost(2 * devices * share * HD, 4 * devices * share * HD),
    )
    return out


def swap(x):
    devices = lax.axis_size("seq")
    flat = x.reshape(-1, HD)
    return lax.all_to_all(flat, "seq", 0, 0, tiled=True).reshape(devices, -1, HD)


def after(x, *earlier):
    return lax.optimization_barrier((x, *earlier))[0]


def local(queries, key_vectors, value_vectors, log_decay, grad_output, out_weight):
    rows, width = queries.shape
    heads, blk_count = width // HD, rows // BLK
    tp, me = lax.axis_size("tp"), lax.axis_index("tp")
    seq, place = lax.axis_size("seq"), lax.axis_index("seq")
    chips = tp // 2
    core = [(i, i ^ 1) for i in range(tp)]

    def from_chip(hops):
        return [(i, (i + 2 * hops) % tp) for i in range(tp)]

    own = grad_output
    sibling = lax.ppermute(own, "tp", core)
    starts = [0, 1, blk_count - 1, blk_count]
    cuts = [(a * BLK, b * BLK) for a, b in zip(starts, starts[1:])]
    head_rows = own[: cuts[0][1]]
    local_enter, fwd_total, cum, pair_cum, rest = key_totals(
        key_vectors, value_vectors, after(log_decay, head_rows), own, cuts[1:], seq
    )
    fwd_got = swap(fwd_total)
    first = [[lax.ppermute(x, "tp", from_chip(d)) for d in range(1, chips)] for x in [head_rows, *rest]]

    def hand_on(j, *earlier):
        arrived = []
        for x in first[j]:
            x = after(x, *earlier)
            arrived += [x, lax.ppermute(x, "tp", core)]
        return arrived

    end = cum[:, :, :, BLK - 1].reshape(blk_count, heads)
    prior = jnp.exp(jnp.cumsum(end, axis=0) - end).T

    arrived = hand_on(0, fwd_total)
    near = near_product(own, after(sibling, arrived[0]), out_weight)
    fwd_got = after(fwd_got, near)

    share = heads * HD // seq
    pieces = max(share // HD, 1)
    spans = jnp.sum(fwd_got[:, share : share + 3, :heads].astype(F32), axis=1)
    mine = lax.dynamic_slice_in_dim(jnp.exp(spans), place * share // HD, pieces, axis=1)
    fwd_out = chain(fwd_got, mine, share, False)
    enter_fwd = swap(fwd_out).reshape(heads, HD, HD)

    grads, sums, total, cum_now = [], [], None, after(pair_cum, fwd_out)
    for part, start in enumerate(starts[:-1]):
        if part:
            arrived = hand_on(part, total)
            cum_now = after(pair_cum, enter_fwd) if part == 2 else pair_cum
        grad, some, total = far_product(start, total, arrived, out_weight, near, queries, cum_now, prior)
        grads += [(j, grad) for j in range(grad.shape[0] // BLK)]
        sums += some
    gq, parts = None, []

    bwd_got = swap(total)
    cum_now = after(cum, total)
    half = blk_count // 2
    for blks in (list(range(half)), list(range(half, blk_count))):
        if blks[0]:
            bwd_out = chain(after(bwd_got, gq), mine, share, True)
            enter_bwd = swap(bwd_out).reshape(heads, HD, HD)
            cum_now = after(cum, bwd_out)
        gq, *part = block_terms(
            blks,
            queries,
            key_vectors,
            value_vectors,
            [grads[j] for j in blks],
            cum_now,
            prior,
            local_enter,
            enter_fwd,
            gq,
        )
        parts.append(part)
    gk_parts, gv_parts = [list(x) for x in zip(*parts)]
    gk, gv = later_terms(key_vectors, value_vectors, gk_parts, gv_parts, sums[1:], cum, enter_bwd)
    return gq, gk, gv


def solution(mesh):
    in_specs = (
        P("seq", "tp"),
        P("seq", "tp"),
        P("seq", "tp"),
        P("tp", "seq"),
        P("seq", "tp"),
        P("tp", None),
    )
    out_specs = (P("seq", "tp"), P("seq", "tp"), P("seq", "tp"))
    return jax.shard_map(local, mesh=mesh, in_specs=in_specs, out_specs=out_specs, check_vma=False)
```

```python
import functools

import jax
import jax.numpy as jnp
from jax import lax
from jax.experimental import pallas as pl
from jax.experimental.pallas import tpu as pltpu
from jax.sharding import PartitionSpec as P

HD = 128
BLK = 256
GROUP = 4
PAIR = 2
ROW = 16
MIB = 2**20

NN = (((1,), (0,)), ((), ()))
NT = (((1,), (1,)), ((), ()))
TN = (((0,), (0,)), ((), ()))

ANY = pl.BlockSpec(memory_space=pl.ANY)
HBM = pl.BlockSpec(memory_space=pltpu.HBM)
VMEM = pl.BlockSpec(memory_space=pltpu.VMEM)
SMEM = pl.BlockSpec(memory_space=pltpu.SMEM)
BF16 = jnp.bfloat16
F32 = jnp.float32


def mm(left, right, form):
    return lax.dot_general(left, right, form, preferred_element_type=F32)


def cost(flops, nbytes, exps=0):
    return pl.CostEstimate(flops=int(flops), bytes_accessed=int(nbytes), transcendentals=int(exps))


def span(index, size):
    return slice(index * size, (index + 1) * size)


def call(body, name, ins, outs, scratch, limit, estimate, aliases=None):
    return pl.pallas_call(
        body,
        in_specs=[spec for _, spec in ins],
        out_specs=[spec for _, _, spec in outs],
        out_shape=[
            pltpu.HBM(shape, dtype) if spec is HBM else jax.ShapeDtypeStruct(shape, dtype)
            for shape, dtype, spec in outs
        ],
        scratch_shapes=scratch,
        input_output_aliases=aliases or {},
        compiler_params=pltpu.CompilerParams(vmem_limit_bytes=limit * MIB),
        cost_estimate=estimate,
        name=name,
    )(*[pltpu.with_memory_space_constraint(x, pltpu.HBM) if spec is HBM else x for x, spec in ins])


def copy_of(source, target, sem):
    return pltpu.make_async_copy(source, target, sem)


def lanes_of(index, size):
    return pl.ds(pl.multiple_of(index * size, size), size)


def loop(count, body):
    lax.fori_loop(0, count, lambda i, _: (body(i), 0)[1], 0)


def head_in(h):
    return slice(h * HD, (h + 1) * HD)


def prefix_sums(x):
    at = lax.broadcasted_iota(jnp.int32, x.shape, 1)
    step = 1
    while step < x.shape[1]:
        x = x + jnp.where(at >= step, pltpu.roll(x, step, 1), 0.0)
        step *= 2
    return x


def key_body(cuts, k_hbm, v_hbm, decay_hbm, grad_hbm, local_hbm, total_ref, cum_ref, pair_ref, *refs):
    cut_hbm, refs = refs[: len(cuts)], refs[len(cuts) :]
    decay_ref, cut_ref, k_ref, v_ref, local_ref, load_sems, store_sems, cut_sems = refs
    blk_count, groups, group, _ = cum_ref.shape
    heads, wide = groups * group, group * HD

    def loads(j):
        rows = pl.ds(j * BLK, BLK)
        return (
            copy_of(k_hbm.at[rows], k_ref.at[rows], load_sems.at[0, j]),
            copy_of(v_hbm.at[rows], v_ref.at[rows], load_sems.at[1, j]),
        )

    def store(j):
        return copy_of(local_ref.at[j], local_hbm.at[j], store_sems.at[j])

    origin = cuts[0][0]
    cut_load = copy_of(grad_hbm.at[pl.ds(origin, cuts[-1][1] - origin)], cut_ref, cut_sems.at[len(cuts)])

    def cut_store(n):
        first, last = cuts[n]
        return copy_of(cut_ref.at[pl.ds(first - origin, last - first)], cut_hbm[n], cut_sems.at[n])

    decay_load = copy_of(decay_hbm, decay_ref, cut_sems.at[len(cuts) + 1])
    decay_load.start()
    for j in range(min(2, blk_count)):
        for copy in loads(j):
            copy.start()
    cut_load.start()
    decay_load.wait()
    span_of = jnp.zeros((heads, 1), F32)
    for j in range(blk_count):
        cum = prefix_sums(decay_ref[:, span(j, BLK)])
        for g in range(groups):
            cum_ref[j, g] = cum[span(g, group)]
        for g in range(heads // PAIR):
            pair_ref[j, g] = cum[span(g, PAIR)]
        span_of = span_of + cum[:, BLK - 1 : BLK]
    local_ref[0] = jnp.zeros_like(local_ref[0])
    cut_load.wait()
    for n in range(len(cuts)):
        cut_store(n).start()

    def block(j):
        for copy in loads(j):
            copy.wait()

        @pl.when(j + 2 < blk_count)
        def _():
            for copy in loads(j + 2):
                copy.start()

        store(j).start()
        rows = pl.ds(pl.multiple_of(j * BLK, BLK), BLK)

        def some_heads(g):
            cum = cum_ref[j, g]
            end = cum[:, BLK - 1 : BLK]
            weight = jnp.exp(end - cum)
            end_weight = jnp.exp(end)
            lanes = lanes_of(g, wide)
            these = pl.ds(g * group, group)
            keys, values, entered = k_ref[rows, lanes], v_ref[rows, lanes], local_ref[j, these]
            left = []
            for h in range(group):
                turned = keys[:, head_in(h)].T.astype(F32)
                scaled = (turned * weight[h : h + 1]).astype(BF16)
                sums = mm(scaled, values[:, head_in(h)], NN)
                left.append(entered[h] * end_weight[h : h + 1] + sums)
            local_ref[j + 1, these] = jnp.stack(left)

        loop(groups, some_heads)

    loop(blk_count, block)
    devices, share = total_ref.shape[0], total_ref.shape[1] - ROW
    total_ref[:, :share] = local_ref[blk_count].astype(BF16).reshape(devices, share, HD)

    diagonal = lax.broadcasted_iota(jnp.int32, (heads, HD), 0) == lax.broadcasted_iota(jnp.int32, (heads, HD), 1)
    spans = jnp.sum(jnp.where(diagonal, span_of, 0.0), axis=0, keepdims=True)
    left, parts = jnp.broadcast_to(spans, (ROW, HD)), jnp.zeros((ROW, HD), F32)
    at_row = lax.broadcasted_iota(jnp.int32, (ROW, HD), 0)
    for n in range(3):
        rounded = left.astype(BF16).astype(F32)
        parts = jnp.where(at_row == n, rounded, parts)
        left = left - rounded
    for d in range(devices):
        total_ref[d, share:] = parts.astype(BF16)
    for j in range(blk_count):
        store(j).wait()
    for n in range(len(cuts)):
        cut_store(n).wait()


def key_totals(keys, values, log_decay, grad, cuts, devices):
    rows, width = keys.shape
    blk_count, heads = rows // BLK, width // HD
    local_enter, total, cum, pair_cum, *parts = call(
        functools.partial(key_body, cuts),
        "key_totals",
        [(keys, HBM), (values, HBM), (log_decay, HBM), (grad, HBM)],
        [
            ((blk_count, heads, HD, HD), F32, HBM),
            ((devices, heads * HD // devices + ROW, HD), BF16, VMEM),
            ((blk_count, heads // GROUP, GROUP, BLK), F32, VMEM),
            ((blk_count, heads // PAIR, PAIR, BLK), F32, VMEM),
        ]
        + [((last - first, grad.shape[1]), BF16, HBM) for first, last in cuts],
        [
            pltpu.VMEM(log_decay.shape, F32),
            pltpu.VMEM((cuts[-1][1] - cuts[0][0], grad.shape[1]), BF16),
            pltpu.VMEM((rows, width), BF16),
            pltpu.VMEM((rows, width), BF16),
            pltpu.VMEM((blk_count + 1, heads, HD, HD), F32),
            pltpu.SemaphoreType.DMA((2, blk_count)),
            pltpu.SemaphoreType.DMA((blk_count,)),
            pltpu.SemaphoreType.DMA((len(cuts) + 2,)),
        ],
        24,
        cost(2 * rows * width * HD, 4 * rows * width + 4 * blk_count * width * HD),
    )
    return local_enter, total, cum, pair_cum, parts


def near_body(wide, own_hbm, sibling_hbm, w_hbm, out_hbm, grad_ref, w_ref, out_ref, w_sems, grad_sems, out_sems):
    rows, depth = own_hbm.shape
    groups, tiles = w_hbm.shape[0] // wide, rows // BLK
    me = lax.axis_index("tp")
    side = lax.rem(me, 2)
    columns = pl.ds(pl.multiple_of((me - side) * depth, 2 * depth), 2 * depth)

    def w_load(g):
        part = pl.ds(g * wide, wide)
        return copy_of(w_hbm.at[part, columns], w_ref.at[part], w_sems.at[g])

    def grad_loads(r):
        part = pl.ds(r * BLK, BLK)
        return (
            copy_of(own_hbm.at[part], grad_ref.at[part, lanes_of(side, depth)], grad_sems.at[0, r]),
            copy_of(sibling_hbm.at[part], grad_ref.at[part, lanes_of(1 - side, depth)], grad_sems.at[1, r]),
        )

    def store(g):
        return copy_of(out_ref.at[lax.rem(g, 2)], out_hbm.at[:, lanes_of(g, wide)], out_sems.at[lax.rem(g, 2)])

    w_load(0).start()
    for r in range(tiles):
        for copy in grad_loads(r):
            copy.start()

    def first_tile(r):
        for copy in grad_loads(r):
            copy.wait()
        these = pl.ds(pl.multiple_of(r * BLK, BLK), BLK)
        out_ref[0, these] = mm(grad_ref[these], w_ref[:wide], NT)

    def columns_of(before):
        g = before + 1
        w_load(g).wait()

        @pl.when(g + 1 < groups)
        def _():
            w_load(g + 1).start()

        @pl.when(g >= 2)
        def _():
            store(g - 2).wait()

        part = w_ref[pl.ds(pl.multiple_of(g * wide, wide), wide)]
        out_ref[lax.rem(g, 2)] = mm(grad_ref[...], part, NT)
        store(g).start()

    w_load(0).wait()
    if groups > 1:
        w_load(1).start()
    loop(tiles, first_tile)
    store(0).start()
    loop(groups - 1, columns_of)
    for g in range(max(groups - 2, 0), groups):
        store(g).wait()


def near_product(own, sibling, weight):
    rows, depth = own.shape
    width = weight.shape[0]
    wide = GROUP * HD
    (out,) = call(
        functools.partial(near_body, wide),
        "near_product",
        [(own, HBM), (sibling, HBM), (weight, HBM)],
        [((rows, width), F32, HBM)],
        [
            pltpu.VMEM((rows, 2 * depth), BF16),
            pltpu.VMEM((width, 2 * depth), BF16),
            pltpu.VMEM((2, rows, wide), F32),
            pltpu.SemaphoreType.DMA((width // wide,)),
            pltpu.SemaphoreType.DMA((2, rows // BLK)),
            pltpu.SemaphoreType.DMA((2,)),
        ],
        32,
        cost(4 * rows * width * depth, 4 * depth * (rows + width) + 4 * rows * width),
    )
    return out


def far_sums(blks, g, group, q_ref, cum_ref, prior_ref, grad, before_ref, sums_refs, total_ref):
    wide = group * HD
    lanes, these = lanes_of(g, wide), pl.ds(g * group, group)
    chained = None
    if before_ref is not None:
        before = before_ref[these]
        chained = [before[h] for h in range(group)]
    for n, blk in enumerate(blks):
        weight = jnp.exp(cum_ref[blk, g])
        queries = q_ref[span(n, BLK), lanes]
        sums = []
        for h in range(group):
            turned = queries[:, head_in(h)].T.astype(F32)
            scaled = (turned * weight[h : h + 1]).astype(BF16)
            sums.append(mm(scaled, grad[span(n, BLK), head_in(h)], NN))
        sums_refs[n][these] = jnp.stack(sums)
        if chained is None:
            chained = sums
        else:
            chained = [chained[h] + prior_ref[g * group + h, blk] * sums[h] for h in range(group)]
    total_ref[these] = jnp.stack(chained).astype(total_ref.dtype)


def far_grad(near, pieces, w_ref, g, wide, side):
    part = pl.ds(pl.multiple_of(g * wide, wide), wide)
    for n, piece in enumerate(pieces):
        at = 2 * (n // 2) + (side if n % 2 == 0 else 1 - side)
        near += mm(piece[...], w_ref[part, lanes_of(at, piece.shape[1])], NT)
    return near.astype(BF16)


def far_products(blks, held, w_ref, near_ref, q_ref, cum_ref, prior_ref, before_ref, total_ref, grad_ref, sums_ref, side, ahead, after_group, ready):
    _, groups, group, _ = cum_ref.shape
    wide = group * HD

    def product(g):
        ready(g)
        return far_grad(near_ref[:, lanes_of(g, wide)], held, w_ref, g, wide, side)

    def sums_of(g, grad):
        sums_refs = [sums_ref.at[n] for n in range(len(blks))]
        far_sums(blks, g, group, q_ref, cum_ref, prior_ref, grad, before_ref, sums_refs, total_ref)

    grad_ref[:, :wide] = product(0)

    def step(g):
        ahead(g + 3)
        mine = grad_ref[:, lanes_of(g, wide)]
        grad = product(g + 1)
        sums_of(g, mine)
        grad_ref[:, lanes_of(g + 1, wide)] = grad
        after_group(g)

    loop(groups - 1, step)
    sums_of(groups - 1, grad_ref[:, lanes_of(groups - 1, wide)])
    after_group(groups - 1)


def far_body(chips, blks, keep, *refs):
    count = len(blks)
    if blks[0]:
        before_hbm, refs = refs[0], refs[1:]
    near_hbm, q_hbm, cum_ref, prior_ref, w_hbm, *refs = refs
    pieces, refs = refs[: 2 * (chips - 1)], refs[2 * (chips - 1) :]
    (total_out, grad_hbm, *sums_hbm), refs = refs[: 2 + count], refs[2 + count :]
    if keep:
        (last_near_ref, last_q_ref), refs = refs[:2], refs[2:]
    w_ref, refs = refs[0], refs[1:]
    held, refs = refs[: len(pieces)], refs[len(pieces) :]
    total_ref, near_ref, q_ref, grad_ref, before_ref, sums_ref, piece_sems, load_sems, store_sems = refs
    total_ref = total_out if keep else total_ref
    rows, depth = pieces[0].shape
    _, groups, group, _ = cum_ref.shape
    wide = group * HD
    me = lax.axis_index("tp")
    side = lax.rem(me, 2)
    chip = lax.div(me, 2)
    here = pl.ds(blks[0] * BLK, rows)

    def loads(g):
        part, lanes, these = pl.ds(g * wide, wide), lanes_of(g, wide), pl.ds(g * group, group)
        found = []
        for d in range(1, chips):
            owner = lax.rem(chip + chips - d, chips)
            columns = pl.ds((d - 1) * 2 * depth, 2 * depth)
            found.append(
                copy_of(w_hbm.at[part, lanes_of(owner, 2 * depth)], w_ref.at[part, columns], load_sems.at[d + 2, g])
            )
        found.append(copy_of(near_hbm.at[here, lanes], near_ref.at[:, lanes], load_sems.at[0, g]))
        found.append(copy_of(q_hbm.at[here, lanes], q_ref.at[:, lanes], load_sems.at[1, g]))
        if blks[0]:
            found.append(copy_of(before_hbm.at[these], before_ref.at[these], load_sems.at[2, g]))
        return found

    def piece_loads():
        return [copy_of(piece, held[n], piece_sems.at[n]) for n, piece in enumerate(pieces)]

    def last_loads():
        if not keep:
            return ()
        block = pl.ds(blks[0] * BLK + rows, BLK)
        return (
            copy_of(near_hbm.at[block], last_near_ref, piece_sems.at[len(pieces)]),
            copy_of(q_hbm.at[block], last_q_ref, piece_sems.at[len(pieces) + 1]),
        )

    def stores(g):
        these, lanes = pl.ds(g * group, group), lanes_of(g, wide)
        found = [copy_of(grad_ref.at[:, lanes], grad_hbm.at[:, lanes], store_sems.at[count, g])]
        found += [copy_of(sums_ref.at[n, these], sums_hbm[n].at[these], store_sems.at[n, g]) for n in range(count)]
        if not keep:
            found.append(copy_of(total_ref.at[these], total_out.at[these], store_sems.at[count + 1, g]))
        return found

    def start(copies):
        for copy in copies:
            copy.start()

    def wait(copies):
        for copy in copies:
            copy.wait()

    def ahead(g):
        @pl.when(g < groups)
        def _():
            start(loads(g))

        @pl.when(g == groups)
        def _():
            start(last_loads())

    start(loads(0))
    start(piece_loads())
    start(loads(1))
    wait(piece_loads())
    if groups > 2:
        start(loads(2))
    far_products(
        blks, held, w_ref, near_ref, q_ref, cum_ref, prior_ref, before_ref if blks[0] else None, total_ref, grad_ref,
        sums_ref, side, ahead, lambda g: start(stores(g)), lambda g: wait(loads(g)),
    )
    wait(last_loads())
    for g in range(groups):
        wait(stores(g))


def far_product(start, before, pieces, weight, near, queries, cum, prior):
    rows, depth = pieces[0].shape
    blk_count, groups, group, _ = cum.shape
    heads = groups * group
    width = heads * HD
    chips = len(pieces) // 2 + 1
    count = rows // BLK
    blks = list(range(start, start + count))
    keep = start + count == blk_count - 1
    states = (heads, HD, HD)
    far_depth = 2 * (chips - 1) * depth
    kept = [((BLK, width), F32, VMEM), ((BLK, width), BF16, VMEM), ((width, far_depth), BF16, VMEM)]
    total, grad, *rest = call(
        functools.partial(far_body, chips, blks, keep),
        "far_product",
        ([(before, HBM)] if start else [])
        + [(near, HBM), (queries, HBM), (cum, VMEM), (prior, SMEM), (weight, HBM)]
        + [(piece, ANY) for piece in pieces],
        [(states, F32, VMEM if keep else HBM), ((rows, width), BF16, HBM)]
        + [(states, F32, HBM)] * count
        + (kept if keep else []),
        ([] if keep else [pltpu.VMEM((width, far_depth), BF16)])
        + [pltpu.VMEM(piece.shape, BF16) for piece in pieces]
        + [
            pltpu.VMEM(states, F32),
            pltpu.VMEM((rows, width), F32),
            pltpu.VMEM((rows, width), BF16),
            pltpu.VMEM((rows, width), BF16),
            pltpu.VMEM(states, F32),
            pltpu.VMEM((count, *states), F32),
            pltpu.SemaphoreType.DMA((len(pieces) + 2,)),
            pltpu.SemaphoreType.DMA((chips + 2, groups)),
            pltpu.SemaphoreType.DMA((count + 2, groups)),
        ],
        24 if keep else 36,
        cost(
            2 * rows * width * (far_depth + HD),
            2 * far_depth * (rows + width) + 8 * rows * width + 12 * width * HD,
        ),
    )
    return grad, rest[:count], total, rest[count:]


def last_body(blk, before_ref, near_ref, q_ref, w_ref, cum_ref, prior_ref, *refs):
    pieces, (total_ref, grad_hbm, sums_hbm, grad_ref, sums_ref, sems) = refs[:-6], refs[-6:]
    _, groups, group, _ = cum_ref.shape
    wide = group * HD

    def stores(g):
        these, lanes = pl.ds(g * group, group), lanes_of(g, wide)
        return (
            copy_of(grad_ref.at[:, lanes], grad_hbm.at[:, lanes], sems.at[0, g]),
            copy_of(sums_ref.at[0, these], sums_hbm.at[these], sems.at[1, g]),
        )

    def after_group(g):
        for copy in stores(g):
            copy.start()

    far_products(
        [blk], pieces, w_ref, near_ref, q_ref, cum_ref, prior_ref, before_ref, total_ref, grad_ref,
        sums_ref, lax.rem(lax.axis_index("tp"), 2), lambda g: None, after_group, lambda g: None,
    )
    for g in range(groups):
        for copy in stores(g):
            copy.wait()


def last_product(before, near, queries, weight, pieces, cum, prior):
    rows, depth = pieces[0].shape
    blk_count, groups, group, _ = cum.shape
    heads = groups * group
    width = heads * HD
    states = (heads, HD, HD)
    total, grad, sums = call(
        functools.partial(last_body, blk_count - 1),
        "last_product",
        [(before, VMEM), (near, VMEM), (queries, VMEM), (weight, VMEM), (cum, VMEM), (prior, SMEM)]
        + [(piece, VMEM) for piece in pieces],
        [(states, BF16, VMEM), ((rows, width), BF16, HBM), (states, F32, HBM)],
        [
            pltpu.VMEM((rows, width), BF16),
            pltpu.VMEM((1, *states), F32),
            pltpu.SemaphoreType.DMA((2, groups)),
        ],
        8,
        cost(0, 0),
    )
    return grad, sums, total


def block_body(blks, grad_blks, q_hbm, k_hbm, v_hbm, grads_hbm, cum_ref, prior_ref, local_hbm, enter_ref, *refs):
    count = len(blks)
    gq_hbm, gk_hbm, gv_hbm, q_ref, k_ref, v_ref, grad_ref, local_ref, gq_ref, gk_ref, gv_ref = refs[-13:-2]
    load_sems, store_sems = refs[-2:]
    _, groups, group, _ = cum_ref.shape
    wide = group * HD

    def loads(n, g):
        lanes, these = lanes_of(g, wide), pl.ds(g * group, group)
        block = pl.ds((blks[0] + n) * BLK, BLK)
        return (
            copy_of(v_hbm.at[block, lanes], v_ref.at[n, :, lanes], load_sems.at[0, n, g]),
            copy_of(q_hbm.at[block, lanes], q_ref.at[n, :, lanes], load_sems.at[1, n, g]),
            copy_of(k_hbm.at[block, lanes], k_ref.at[n, :, lanes], load_sems.at[2, n, g]),
            copy_of(local_hbm.at[blks[0] + n, these], local_ref.at[n, these], load_sems.at[3, n, g]),
        )

    def grad_load(n, g, source=0):
        lanes = lanes_of(g, wide)
        block = pl.ds(grad_blks[source] * BLK, BLK)
        return copy_of(grads_hbm[source].at[block, lanes], grad_ref.at[n, :, lanes], load_sems.at[4, n, g])

    def stores(n, g):
        lanes = lanes_of(g, wide)
        block, part = pl.ds((blks[0] + n) * BLK, BLK), pl.ds(n * BLK, BLK)
        return (
            copy_of(gq_ref.at[n, :, lanes], gq_hbm.at[block, lanes], store_sems.at[0, n, g]),
            copy_of(gk_ref.at[n, :, lanes], gk_hbm.at[part, lanes], store_sems.at[1, n, g]),
            copy_of(gv_ref.at[n, :, lanes], gv_hbm.at[part, lanes], store_sems.at[2, n, g]),
        )

    def start(n, g):
        grad_load(n, g, n).start()
        for copy in loads(n, g):
            copy.start()

    for g in range(groups):
        start(0, g)
    at_row = lax.broadcasted_iota(jnp.int32, (BLK, BLK), 0)
    at_col = lax.broadcasted_iota(jnp.int32, (BLK, BLK), 1)
    causal, flipped = at_row >= at_col, at_row <= at_col

    def some_heads(at):
        n, g = lax.div(at, groups), lax.rem(at, groups)
        blk = blks[0] + n
        for m in range(1, count):

            @pl.when(n == m - 1)
            def _(m=m):
                start(m, g)

        grad_load(n, g).wait()
        for copy in loads(n, g):
            copy.wait()
        rows = cum_ref[blk, g]
        cum = rows.T
        head_weight = jnp.exp(cum)
        lanes, these = lanes_of(g, wide), pl.ds(g * group, group)
        queries, keys, values, grads = (ref[n, :, lanes] for ref in (q_ref, k_ref, v_ref, grad_ref))
        entered, here = enter_ref[these], local_ref[n, these]
        gq, gk, gv = [], [], []
        for h in range(group):
            head = head_in(h)
            q, k, v, grad = queries[:, head], keys[:, head], values[:, head], grads[:, head]
            by_row, by_col = cum[:, h : h + 1], rows[h : h + 1, :]
            mask = jnp.exp(jnp.where(causal, by_row - by_col, -1e30))
            turned = jnp.exp(jnp.where(flipped, by_col - by_row, -1e30))
            scores = (mm(grad, v, NT) * mask).astype(BF16)
            turned_scores = (mm(v, grad, NT) * turned).astype(BF16)
            turned_attn = (mm(k, q, NT) * turned).astype(BF16)
            enter = entered[h].astype(F32) * prior_ref[g * group + h, blk] + here[h]
            inter = mm(grad, enter.astype(BF16), NT) * head_weight[:, h : h + 1]
            gq.append((mm(scores, k, NN) + inter).astype(BF16))
            gk.append(mm(turned_scores, q, NN).astype(BF16))
            gv.append(mm(turned_attn, grad, NN).astype(BF16))
        gq_ref[n, :, lanes] = jnp.concatenate(gq, axis=1)
        gk_ref[n, :, lanes] = jnp.concatenate(gk, axis=1)
        gv_ref[n, :, lanes] = jnp.concatenate(gv, axis=1)
        for copy in stores(n, g):
            copy.start()

    loop(count * groups, some_heads)
    for n in range(count):
        for g in range(groups):
            for copy in stores(n, g):
                copy.wait()


def block_terms(blks, queries, keys, values, grads, cum, prior, local_enter, enter, gq):
    rows, width = queries.shape
    heads, groups, count = width // HD, cum.shape[1], len(blks)
    tile = pltpu.VMEM((count, BLK, width), BF16)
    part = ((count * BLK, width), BF16, HBM)
    ins = [(queries, HBM), (keys, HBM), (values, HBM)] + [(grad, HBM) for _, grad in grads]
    ins += [(cum, VMEM), (prior, SMEM), (local_enter, HBM), (enter, VMEM)]
    if gq is not None:
        ins.append((gq, HBM))

    def body(q_hbm, k_hbm, v_hbm, *refs):
        block_body(blks, [at for at, _ in grads], q_hbm, k_hbm, v_hbm, refs[:count], *refs[count:])

    return call(
        body,
        "block_terms",
        ins,
        [((rows, width), BF16, HBM), part, part],
        [tile] * 4
        + [pltpu.VMEM((count, heads, HD, HD), F32)]
        + [tile] * 3
        + [pltpu.SemaphoreType.DMA((5, count, groups)), pltpu.SemaphoreType.DMA((3, count, groups))],
        28,
        cost(
            count * BLK * width * (10 * BLK + 2 * HD),
            count * (14 * BLK * width + 6 * width * HD),
            count * BLK * heads * BLK,
        ),
        {len(ins) - 1: 0} if gq is not None else None,
    )


def later_body(k_hbm, v_hbm, cum_ref, enter_ref, *refs):
    blk_count, groups, group, _ = cum_ref.shape
    halves = len(refs) - 10 - (blk_count - 1)
    gk_parts, gv_parts = refs[: halves // 2], refs[halves // 2 : halves]
    each = blk_count // len(gk_parts)
    sums_hbm = refs[halves : halves + blk_count - 1]
    gk_hbm, gv_hbm, k_ref, v_ref, gk_ref, gv_ref, sums_ref, carry_ref = refs[halves + blk_count - 1 : -2]
    load_sems, store_sems = refs[-2:]
    wide = group * HD

    def loads(j, g):
        rows, lanes, these = pl.ds(j * BLK, BLK), lanes_of(g, wide), pl.ds(g * group, group)
        part = pl.ds(j % each * BLK, BLK)
        found = [
            copy_of(v_hbm.at[rows, lanes], v_ref.at[rows, lanes], load_sems.at[0, j, g]),
            copy_of(k_hbm.at[rows, lanes], k_ref.at[rows, lanes], load_sems.at[1, j, g]),
            copy_of(gk_parts[j // each].at[part, lanes], gk_ref.at[rows, lanes], load_sems.at[2, j, g]),
            copy_of(gv_parts[j // each].at[part, lanes], gv_ref.at[rows, lanes], load_sems.at[3, j, g]),
        ]
        if j:
            found.append(copy_of(sums_hbm[j - 1].at[these], sums_ref.at[j, these], load_sems.at[4, j, g]))
        return found

    def stores(j, g):
        rows, lanes = pl.ds(j * BLK, BLK), lanes_of(g, wide)
        return (
            copy_of(gk_ref.at[rows, lanes], gk_hbm.at[rows, lanes], store_sems.at[0, j, g]),
            copy_of(gv_ref.at[rows, lanes], gv_hbm.at[rows, lanes], store_sems.at[1, j, g]),
        )

    for g in range(groups):
        for copy in loads(blk_count - 1, g):
            copy.start()
    for j in reversed(range(blk_count)):

        def some_heads(g, j=j):
            if j:
                for copy in loads(j - 1, g):
                    copy.start()
            for copy in loads(j, g):
                copy.wait()
            rows = span(j, BLK)
            cum = cum_ref[j, g].T
            end = cum[BLK - 1 : BLK, :]
            weight = jnp.exp(end - cum)
            end_weight = jnp.exp(end)
            lanes, these = lanes_of(g, wide), pl.ds(g * group, group)
            keys, values = k_ref[rows, lanes], v_ref[rows, lanes]
            gk_in, gv_in = gk_ref[rows, lanes], gv_ref[rows, lanes]
            entered = enter_ref[these].astype(F32) if j + 1 == blk_count else carry_ref[these]
            here = sums_ref[j, these] if j else None
            gk, gv, left = [], [], []
            for h in range(group):
                head, tail = head_in(h), weight[:, h : h + 1]
                enter = entered[h].astype(BF16)
                gk.append((gk_in[:, head].astype(F32) + mm(values[:, head], enter, NT) * tail).astype(BF16))
                gv.append((gv_in[:, head].astype(F32) + mm(keys[:, head], enter, NN) * tail).astype(BF16))
                if j:
                    left.append(entered[h] * end_weight[:, h : h + 1] + here[h])
            gk_ref[rows, lanes] = jnp.concatenate(gk, axis=1)
            gv_ref[rows, lanes] = jnp.concatenate(gv, axis=1)
            if j:
                carry_ref[these] = jnp.stack(left)
            for copy in stores(j, g):
                copy.start()

        loop(groups, some_heads)
    for j in range(blk_count):
        for g in range(groups):
            for copy in stores(j, g):
                copy.wait()


def later_terms(keys, values, gk_parts, gv_parts, sums, cum, enter):
    rows, width = keys.shape
    heads, blk_count = width // HD, rows // BLK
    whole = pltpu.VMEM((rows, width), BF16)
    out = ((rows, width), BF16, HBM)
    return call(
        later_body,
        "later_terms",
        [(keys, HBM), (values, HBM), (cum, VMEM), (enter, VMEM)]
        + [(x, HBM) for x in gk_parts + gv_parts + sums],
        [out, out],
        [whole] * 4
        + [
            pltpu.VMEM((blk_count, heads, HD, HD), F32),
            pltpu.VMEM((heads, HD, HD), F32),
            pltpu.SemaphoreType.DMA((5, blk_count, cum.shape[1])),
            pltpu.SemaphoreType.DMA((2, blk_count, cum.shape[1])),
        ],
        28,
        cost(rows * width * 4 * HD, 12 * rows * width + 4 * blk_count * width * HD),
    )


def chain_body(reverse, got_ref, weight_ref, out_ref):
    devices, share = out_ref.shape[0], out_ref.shape[1]
    pieces = weight_ref.shape[1]
    part = share // pieces
    for p in range(pieces):
        rows = span(p, part)
        carry = jnp.zeros((part, HD), F32)
        for place in reversed(range(devices)) if reverse else range(devices):
            out_ref[place, rows] = carry.astype(BF16)
            carry = weight_ref[place, p] * carry + got_ref[place, rows].astype(F32)


def chain(got, weights, share, reverse):
    devices = got.shape[0]
    (out,) = call(
        functools.partial(chain_body, reverse),
        "chain_states",
        [(got, VMEM), (weights, SMEM)],
        [((devices, share, HD), BF16, VMEM)],
        [],
        16,
        cost(2 * devices * share * HD, 4 * devices * share * HD),
    )
    return out


def swap(x):
    devices = lax.axis_size("seq")
    flat = x.reshape(-1, HD)
    return lax.all_to_all(flat, "seq", 0, 0, tiled=True).reshape(devices, -1, HD)


def after(x, *earlier):
    return lax.optimization_barrier((x, *earlier))[0]


def local(queries, key_vectors, value_vectors, log_decay, grad_output, out_weight):
    rows, width = queries.shape
    heads, blk_count = width // HD, rows // BLK
    tp, me = lax.axis_size("tp"), lax.axis_index("tp")
    seq, place = lax.axis_size("seq"), lax.axis_index("seq")
    chips = tp // 2
    core = [(i, i ^ 1) for i in range(tp)]

    def from_chip(hops):
        return [(i, (i + 2 * hops) % tp) for i in range(tp)]

    own = grad_output
    starts = [0, 1, blk_count - 1, blk_count]
    cuts = [(a * BLK, b * BLK) for a, b in zip(starts, starts[1:])]
    head_rows = own[: cuts[0][1]]
    sibling = lax.ppermute(after(own, head_rows), "tp", core)
    local_enter, fwd_total, cum, pair_cum, rest = key_totals(
        key_vectors, value_vectors, after(log_decay, head_rows), own, cuts[1:], seq
    )
    fwd_got = swap(fwd_total)
    first = [[lax.ppermute(x, "tp", from_chip(d)) for d in range(1, chips)] for x in [head_rows, *rest]]

    def hand_on(j, *earlier):
        arrived = []
        for x in first[j]:
            x = after(x, *earlier)
            arrived += [x, lax.ppermute(x, "tp", core)]
        return arrived

    end = cum[:, :, :, BLK - 1].reshape(blk_count, heads)
    prior = jnp.exp(jnp.cumsum(end, axis=0) - end).T

    near = near_product(own, sibling, out_weight)
    arrived = hand_on(0, near)
    fwd_got = after(fwd_got, near)

    share = heads * HD // seq
    pieces = max(share // HD, 1)
    spans = jnp.sum(fwd_got[:, share : share + 3, :heads].astype(F32), axis=1)
    mine = lax.dynamic_slice_in_dim(jnp.exp(spans), place * share // HD, pieces, axis=1)
    fwd_out = chain(fwd_got, mine, share, False)
    enter_fwd = swap(fwd_out).reshape(heads, HD, HD)

    first_grad, sums, total, _ = far_product(
        0, None, arrived, out_weight, near, queries, after(pair_cum, fwd_out), prior
    )
    arrived = hand_on(1, total)
    next_grad, next_sums, total, kept = far_product(
        1, total, arrived, out_weight, near, queries, pair_cum, prior
    )
    last_grad, last_sums, total = last_product(total, *kept, hand_on(2, next_grad), pair_cum, prior)
    grads = [(0, first_grad)] + [(j, next_grad) for j in range(blk_count - 2)] + [(0, last_grad)]
    sums = [*sums, *next_sums, last_sums]
    gq, parts = None, []

    bwd_got = swap(total)
    cum_now = after(cum, total)
    half = blk_count // 2
    for blks in (list(range(half)), list(range(half, blk_count))):
        if blks[0]:
            bwd_out = chain(after(bwd_got, gq), mine, share, True)
            enter_bwd = swap(bwd_out).reshape(heads, HD, HD)
            cum_now = after(cum, bwd_out)
        gq, *part = block_terms(
            blks,
            queries,
            key_vectors,
            value_vectors,
            [grads[j] for j in blks],
            cum_now,
            prior,
            local_enter,
            enter_fwd,
            gq,
        )
        parts.append(part)
    gk_parts, gv_parts = [list(x) for x in zip(*parts)]
    gk, gv = later_terms(key_vectors, value_vectors, gk_parts, gv_parts, sums[1:], cum, enter_bwd)
    return gq, gk, gv


def solution(mesh):
    in_specs = (
        P("seq", "tp"),
        P("seq", "tp"),
        P("seq", "tp"),
        P("tp", "seq"),
        P("seq", "tp"),
        P("tp", None),
    )
    out_specs = (P("seq", "tp"), P("seq", "tp"), P("seq", "tp"))
    return jax.shard_map(local, mesh=mesh, in_specs=in_specs, out_specs=out_specs, check_vma=False)
```

```python
import functools

import jax
import jax.numpy as jnp
from jax import lax
from jax.experimental import pallas as pl
from jax.experimental.pallas import tpu as pltpu
from jax.sharding import PartitionSpec as P

HD = 128
BLK = 256
GROUP = 4
PAIR = 2
ROW = 16
MIB = 2**20

NN = (((1,), (0,)), ((), ()))
NT = (((1,), (1,)), ((), ()))
TN = (((0,), (0,)), ((), ()))

ANY = pl.BlockSpec(memory_space=pl.ANY)
HBM = pl.BlockSpec(memory_space=pltpu.HBM)
VMEM = pl.BlockSpec(memory_space=pltpu.VMEM)
SMEM = pl.BlockSpec(memory_space=pltpu.SMEM)
BF16 = jnp.bfloat16
F32 = jnp.float32


def mm(left, right, form):
    return lax.dot_general(left, right, form, preferred_element_type=F32)


def cost(flops, nbytes, exps=0):
    return pl.CostEstimate(flops=int(flops), bytes_accessed=int(nbytes), transcendentals=int(exps))


def span(index, size):
    return slice(index * size, (index + 1) * size)


def call(body, name, ins, outs, scratch, limit, estimate, aliases=None):
    return pl.pallas_call(
        body,
        in_specs=[spec for _, spec in ins],
        out_specs=[spec for _, _, spec in outs],
        out_shape=[
            pltpu.HBM(shape, dtype) if spec is HBM else jax.ShapeDtypeStruct(shape, dtype)
            for shape, dtype, spec in outs
        ],
        scratch_shapes=scratch,
        input_output_aliases=aliases or {},
        compiler_params=pltpu.CompilerParams(vmem_limit_bytes=limit * MIB),
        cost_estimate=estimate,
        name=name,
    )(*[pltpu.with_memory_space_constraint(x, pltpu.HBM) if spec is HBM else x for x, spec in ins])


def copy_of(source, target, sem):
    return pltpu.make_async_copy(source, target, sem)


def lanes_of(index, size):
    return pl.ds(pl.multiple_of(index * size, size), size)


def loop(count, body):
    lax.fori_loop(0, count, lambda i, _: (body(i), 0)[1], 0)


def head_in(h):
    return slice(h * HD, (h + 1) * HD)


def take_body(grad_hbm, out_ref, sems):
    copy = copy_of(grad_hbm.at[pl.ds(0, out_ref.shape[0])], out_ref, sems.at[0])
    copy.start()
    copy.wait()


def take_rows(grad, rows):
    (out,) = call(
        take_body,
        "take_rows",
        [(grad, HBM)],
        [((rows, grad.shape[1]), BF16, VMEM)],
        [pltpu.SemaphoreType.DMA((1,))],
        1,
        cost(0, 4 * rows * grad.shape[1]),
    )
    return out


def prefix_sums(x):
    at = lax.broadcasted_iota(jnp.int32, x.shape, 1)
    step = 1
    while step < x.shape[1]:
        x = x + jnp.where(at >= step, pltpu.roll(x, step, 1), 0.0)
        step *= 2
    return x


def key_body(cuts, k_hbm, v_hbm, decay_hbm, grad_hbm, local_hbm, total_ref, cum_ref, pair_ref, *refs):
    cut_hbm, refs = refs[: len(cuts)], refs[len(cuts) :]
    decay_ref, cut_ref, k_ref, v_ref, local_ref, load_sems, store_sems, cut_sems = refs
    blk_count, groups, group, _ = cum_ref.shape
    heads, wide = groups * group, group * HD

    def loads(j):
        rows = pl.ds(j * BLK, BLK)
        return (
            copy_of(k_hbm.at[rows], k_ref.at[rows], load_sems.at[0, j]),
            copy_of(v_hbm.at[rows], v_ref.at[rows], load_sems.at[1, j]),
        )

    def store(j):
        return copy_of(local_ref.at[j], local_hbm.at[j], store_sems.at[j])

    origin = cuts[0][0]
    cut_load = copy_of(grad_hbm.at[pl.ds(origin, cuts[-1][1] - origin)], cut_ref, cut_sems.at[len(cuts)])

    def cut_store(n):
        first, last = cuts[n]
        return copy_of(cut_ref.at[pl.ds(first - origin, last - first)], cut_hbm[n], cut_sems.at[n])

    decay_load = copy_of(decay_hbm, decay_ref, cut_sems.at[len(cuts) + 1])
    decay_load.start()
    for j in range(min(2, blk_count)):
        for copy in loads(j):
            copy.start()
    cut_load.start()
    decay_load.wait()
    span_of = jnp.zeros((heads, 1), F32)
    for j in range(blk_count):
        cum = prefix_sums(decay_ref[:, span(j, BLK)])
        for g in range(groups):
            cum_ref[j, g] = cum[span(g, group)]
        for g in range(heads // PAIR):
            pair_ref[j, g] = cum[span(g, PAIR)]
        span_of = span_of + cum[:, BLK - 1 : BLK]
    local_ref[0] = jnp.zeros_like(local_ref[0])
    cut_load.wait()
    for n in range(len(cuts)):
        cut_store(n).start()

    def block(j):
        for copy in loads(j):
            copy.wait()

        @pl.when(j + 2 < blk_count)
        def _():
            for copy in loads(j + 2):
                copy.start()

        store(j).start()
        rows = pl.ds(pl.multiple_of(j * BLK, BLK), BLK)

        def some_heads(g):
            cum = cum_ref[j, g]
            end = cum[:, BLK - 1 : BLK]
            weight = jnp.exp(end - cum)
            end_weight = jnp.exp(end)
            lanes = lanes_of(g, wide)
            these = pl.ds(g * group, group)
            keys, values, entered = k_ref[rows, lanes], v_ref[rows, lanes], local_ref[j, these]
            left = []
            for h in range(group):
                turned = keys[:, head_in(h)].T.astype(F32)
                scaled = (turned * weight[h : h + 1]).astype(BF16)
                sums = mm(scaled, values[:, head_in(h)], NN)
                left.append(entered[h] * end_weight[h : h + 1] + sums)
            local_ref[j + 1, these] = jnp.stack(left)

        loop(groups, some_heads)

    loop(blk_count, block)
    devices, share = total_ref.shape[0], total_ref.shape[1] - ROW
    total_ref[:, :share] = local_ref[blk_count].astype(BF16).reshape(devices, share, HD)

    diagonal = lax.broadcasted_iota(jnp.int32, (heads, HD), 0) == lax.broadcasted_iota(jnp.int32, (heads, HD), 1)
    spans = jnp.sum(jnp.where(diagonal, span_of, 0.0), axis=0, keepdims=True)
    left, parts = jnp.broadcast_to(spans, (ROW, HD)), jnp.zeros((ROW, HD), F32)
    at_row = lax.broadcasted_iota(jnp.int32, (ROW, HD), 0)
    for n in range(3):
        rounded = left.astype(BF16).astype(F32)
        parts = jnp.where(at_row == n, rounded, parts)
        left = left - rounded
    for d in range(devices):
        total_ref[d, share:] = parts.astype(BF16)
    for j in range(blk_count):
        store(j).wait()
    for n in range(len(cuts)):
        cut_store(n).wait()


def key_totals(keys, values, log_decay, grad, cuts, devices):
    rows, width = keys.shape
    blk_count, heads = rows // BLK, width // HD
    local_enter, total, cum, pair_cum, *parts = call(
        functools.partial(key_body, cuts),
        "key_totals",
        [(keys, HBM), (values, HBM), (log_decay, HBM), (grad, HBM)],
        [
            ((blk_count, heads, HD, HD), F32, HBM),
            ((devices, heads * HD // devices + ROW, HD), BF16, VMEM),
            ((blk_count, heads // GROUP, GROUP, BLK), F32, VMEM),
            ((blk_count, heads // PAIR, PAIR, BLK), F32, VMEM),
        ]
        + [((last - first, grad.shape[1]), BF16, HBM) for first, last in cuts],
        [
            pltpu.VMEM(log_decay.shape, F32),
            pltpu.VMEM((cuts[-1][1] - cuts[0][0], grad.shape[1]), BF16),
            pltpu.VMEM((rows, width), BF16),
            pltpu.VMEM((rows, width), BF16),
            pltpu.VMEM((blk_count + 1, heads, HD, HD), F32),
            pltpu.SemaphoreType.DMA((2, blk_count)),
            pltpu.SemaphoreType.DMA((blk_count,)),
            pltpu.SemaphoreType.DMA((len(cuts) + 2,)),
        ],
        24,
        cost(2 * rows * width * HD, 4 * rows * width + 4 * blk_count * width * HD),
    )
    return local_enter, total, cum, pair_cum, parts


def near_body(wide, own_hbm, sibling_hbm, w_hbm, out_hbm, grad_ref, w_ref, out_ref, w_sems, grad_sems, out_sems):
    rows, depth = own_hbm.shape
    groups, tiles = w_hbm.shape[0] // wide, rows // BLK
    me = lax.axis_index("tp")
    side = lax.rem(me, 2)
    columns = pl.ds(pl.multiple_of((me - side) * depth, 2 * depth), 2 * depth)

    def w_load(g):
        part = pl.ds(g * wide, wide)
        return copy_of(w_hbm.at[part, columns], w_ref.at[part], w_sems.at[g])

    def grad_loads(r):
        part = pl.ds(r * BLK, BLK)
        return (
            copy_of(own_hbm.at[part], grad_ref.at[part, lanes_of(side, depth)], grad_sems.at[0, r]),
            copy_of(sibling_hbm.at[part], grad_ref.at[part, lanes_of(1 - side, depth)], grad_sems.at[1, r]),
        )

    def store(g):
        return copy_of(out_ref.at[lax.rem(g, 2)], out_hbm.at[:, lanes_of(g, wide)], out_sems.at[lax.rem(g, 2)])

    w_load(0).start()
    for r in range(tiles):
        for copy in grad_loads(r):
            copy.start()

    def first_tile(r):
        for copy in grad_loads(r):
            copy.wait()
        these = pl.ds(pl.multiple_of(r * BLK, BLK), BLK)
        out_ref[0, these] = mm(grad_ref[these], w_ref[:wide], NT)

    def columns_of(before):
        g = before + 1
        w_load(g).wait()

        @pl.when(g + 1 < groups)
        def _():
            w_load(g + 1).start()

        @pl.when(g >= 2)
        def _():
            store(g - 2).wait()

        part = w_ref[pl.ds(pl.multiple_of(g * wide, wide), wide)]
        out_ref[lax.rem(g, 2)] = mm(grad_ref[...], part, NT)
        store(g).start()

    w_load(0).wait()
    if groups > 1:
        w_load(1).start()
    loop(tiles, first_tile)
    store(0).start()
    loop(groups - 1, columns_of)
    for g in range(max(groups - 2, 0), groups):
        store(g).wait()


def near_product(own, sibling, weight):
    rows, depth = own.shape
    width = weight.shape[0]
    wide = GROUP * HD
    (out,) = call(
        functools.partial(near_body, wide),
        "near_product",
        [(own, HBM), (sibling, HBM), (weight, HBM)],
        [((rows, width), F32, HBM)],
        [
            pltpu.VMEM((rows, 2 * depth), BF16),
            pltpu.VMEM((width, 2 * depth), BF16),
            pltpu.VMEM((2, rows, wide), F32),
            pltpu.SemaphoreType.DMA((width // wide,)),
            pltpu.SemaphoreType.DMA((2, rows // BLK)),
            pltpu.SemaphoreType.DMA((2,)),
        ],
        32,
        cost(4 * rows * width * depth, 4 * depth * (rows + width) + 4 * rows * width),
    )
    return out


def far_sums(blks, g, group, q_ref, cum_ref, prior_ref, grad, before_ref, sums_refs, total_ref):
    wide = group * HD
    lanes, these = lanes_of(g, wide), pl.ds(g * group, group)
    chained = None
    if before_ref is not None:
        before = before_ref[these]
        chained = [before[h] for h in range(group)]
    for n, blk in enumerate(blks):
        weight = jnp.exp(cum_ref[blk, g])
        queries = q_ref[span(n, BLK), lanes]
        sums = []
        for h in range(group):
            turned = queries[:, head_in(h)].T.astype(F32)
            scaled = (turned * weight[h : h + 1]).astype(BF16)
            sums.append(mm(scaled, grad[span(n, BLK), head_in(h)], NN))
        sums_refs[n][these] = jnp.stack(sums)
        if chained is None:
            chained = sums
        else:
            chained = [chained[h] + prior_ref[g * group + h, blk] * sums[h] for h in range(group)]
    total_ref[these] = jnp.stack(chained).astype(total_ref.dtype)


def far_grad(near, pieces, w_ref, g, wide, side):
    part = pl.ds(pl.multiple_of(g * wide, wide), wide)
    for n, piece in enumerate(pieces):
        at = 2 * (n // 2) + (side if n % 2 == 0 else 1 - side)
        near += mm(piece[...], w_ref[part, lanes_of(at, piece.shape[1])], NT)
    return near.astype(BF16)


def far_products(blks, held, w_ref, near_ref, q_ref, cum_ref, prior_ref, before_ref, total_ref, grad_ref, sums_ref, side, ahead, after_group, ready):
    _, groups, group, _ = cum_ref.shape
    wide = group * HD

    def product(g):
        ready(g)
        return far_grad(near_ref[:, lanes_of(g, wide)], held, w_ref, g, wide, side)

    def sums_of(g, grad):
        sums_refs = [sums_ref.at[n] for n in range(len(blks))]
        far_sums(blks, g, group, q_ref, cum_ref, prior_ref, grad, before_ref, sums_refs, total_ref)

    grad_ref[:, :wide] = product(0)

    def step(g):
        ahead(g + 3)
        mine = grad_ref[:, lanes_of(g, wide)]
        grad = product(g + 1)
        sums_of(g, mine)
        grad_ref[:, lanes_of(g + 1, wide)] = grad
        after_group(g)

    loop(groups - 1, step)
    sums_of(groups - 1, grad_ref[:, lanes_of(groups - 1, wide)])
    after_group(groups - 1)


def far_body(chips, blks, keep, *refs):
    count = len(blks)
    if blks[0]:
        before_hbm, refs = refs[0], refs[1:]
    near_hbm, q_hbm, cum_ref, prior_ref, w_hbm, *refs = refs
    pieces, refs = refs[: 2 * (chips - 1)], refs[2 * (chips - 1) :]
    (total_out, grad_hbm, *sums_hbm), refs = refs[: 2 + count], refs[2 + count :]
    if keep:
        (last_near_ref, last_q_ref), refs = refs[:2], refs[2:]
    w_ref, refs = refs[0], refs[1:]
    held, refs = refs[: len(pieces)], refs[len(pieces) :]
    total_ref, near_ref, q_ref, grad_ref, before_ref, sums_ref, piece_sems, load_sems, store_sems = refs
    total_ref = total_out if keep else total_ref
    rows, depth = pieces[0].shape
    _, groups, group, _ = cum_ref.shape
    wide = group * HD
    me = lax.axis_index("tp")
    side = lax.rem(me, 2)
    chip = lax.div(me, 2)
    here = pl.ds(blks[0] * BLK, rows)

    def loads(g):
        part, lanes, these = pl.ds(g * wide, wide), lanes_of(g, wide), pl.ds(g * group, group)
        found = []
        for d in range(1, chips):
            owner = lax.rem(chip + chips - d, chips)
            columns = pl.ds((d - 1) * 2 * depth, 2 * depth)
            found.append(
                copy_of(w_hbm.at[part, lanes_of(owner, 2 * depth)], w_ref.at[part, columns], load_sems.at[d + 2, g])
            )
        found.append(copy_of(near_hbm.at[here, lanes], near_ref.at[:, lanes], load_sems.at[0, g]))
        found.append(copy_of(q_hbm.at[here, lanes], q_ref.at[:, lanes], load_sems.at[1, g]))
        if blks[0]:
            found.append(copy_of(before_hbm.at[these], before_ref.at[these], load_sems.at[2, g]))
        return found

    def piece_loads():
        return [copy_of(piece, held[n], piece_sems.at[n]) for n, piece in enumerate(pieces)]

    def last_loads():
        if not keep:
            return ()
        block = pl.ds(blks[0] * BLK + rows, BLK)
        return (
            copy_of(near_hbm.at[block], last_near_ref, piece_sems.at[len(pieces)]),
            copy_of(q_hbm.at[block], last_q_ref, piece_sems.at[len(pieces) + 1]),
        )

    def stores(g):
        these, lanes = pl.ds(g * group, group), lanes_of(g, wide)
        found = [copy_of(grad_ref.at[:, lanes], grad_hbm.at[:, lanes], store_sems.at[count, g])]
        found += [copy_of(sums_ref.at[n, these], sums_hbm[n].at[these], store_sems.at[n, g]) for n in range(count)]
        if not keep:
            found.append(copy_of(total_ref.at[these], total_out.at[these], store_sems.at[count + 1, g]))
        return found

    def start(copies):
        for copy in copies:
            copy.start()

    def wait(copies):
        for copy in copies:
            copy.wait()

    def ahead(g):
        @pl.when(g < groups)
        def _():
            start(loads(g))

        @pl.when(g == groups)
        def _():
            start(last_loads())

    start(loads(0))
    start(piece_loads())
    start(loads(1))
    wait(piece_loads())
    if groups > 2:
        start(loads(2))
    far_products(
        blks, held, w_ref, near_ref, q_ref, cum_ref, prior_ref, before_ref if blks[0] else None, total_ref, grad_ref,
        sums_ref, side, ahead, lambda g: start(stores(g)), lambda g: wait(loads(g)),
    )
    wait(last_loads())
    for g in range(groups):
        wait(stores(g))


def far_product(start, before, pieces, weight, near, queries, cum, prior):
    rows, depth = pieces[0].shape
    blk_count, groups, group, _ = cum.shape
    heads = groups * group
    width = heads * HD
    chips = len(pieces) // 2 + 1
    count = rows // BLK
    blks = list(range(start, start + count))
    keep = start + count == blk_count - 1
    states = (heads, HD, HD)
    far_depth = 2 * (chips - 1) * depth
    kept = [((BLK, width), F32, VMEM), ((BLK, width), BF16, VMEM), ((width, far_depth), BF16, VMEM)]
    total, grad, *rest = call(
        functools.partial(far_body, chips, blks, keep),
        "far_product",
        ([(before, HBM)] if start else [])
        + [(near, HBM), (queries, HBM), (cum, VMEM), (prior, SMEM), (weight, HBM)]
        + [(piece, ANY) for piece in pieces],
        [(states, F32, VMEM if keep else HBM), ((rows, width), BF16, HBM)]
        + [(states, F32, HBM)] * count
        + (kept if keep else []),
        ([] if keep else [pltpu.VMEM((width, far_depth), BF16)])
        + [pltpu.VMEM(piece.shape, BF16) for piece in pieces]
        + [
            pltpu.VMEM(states, F32),
            pltpu.VMEM((rows, width), F32),
            pltpu.VMEM((rows, width), BF16),
            pltpu.VMEM((rows, width), BF16),
            pltpu.VMEM(states, F32),
            pltpu.VMEM((count, *states), F32),
            pltpu.SemaphoreType.DMA((len(pieces) + 2,)),
            pltpu.SemaphoreType.DMA((chips + 2, groups)),
            pltpu.SemaphoreType.DMA((count + 2, groups)),
        ],
        24 if keep else 36,
        cost(
            2 * rows * width * (far_depth + HD),
            2 * far_depth * (rows + width) + 8 * rows * width + 12 * width * HD,
        ),
    )
    return grad, rest[:count], total, rest[count:]


def last_body(blk, before_ref, near_ref, q_ref, w_ref, cum_ref, prior_ref, *refs):
    pieces, (total_ref, grad_hbm, sums_hbm, grad_ref, sums_ref, sems) = refs[:-6], refs[-6:]
    _, groups, group, _ = cum_ref.shape
    wide = group * HD

    def stores(g):
        these, lanes = pl.ds(g * group, group), lanes_of(g, wide)
        return (
            copy_of(grad_ref.at[:, lanes], grad_hbm.at[:, lanes], sems.at[0, g]),
            copy_of(sums_ref.at[0, these], sums_hbm.at[these], sems.at[1, g]),
        )

    def after_group(g):
        for copy in stores(g):
            copy.start()

    far_products(
        [blk], pieces, w_ref, near_ref, q_ref, cum_ref, prior_ref, before_ref, total_ref, grad_ref,
        sums_ref, lax.rem(lax.axis_index("tp"), 2), lambda g: None, after_group, lambda g: None,
    )
    for g in range(groups):
        for copy in stores(g):
            copy.wait()


def last_product(before, near, queries, weight, pieces, cum, prior):
    rows, depth = pieces[0].shape
    blk_count, groups, group, _ = cum.shape
    heads = groups * group
    width = heads * HD
    states = (heads, HD, HD)
    total, grad, sums = call(
        functools.partial(last_body, blk_count - 1),
        "last_product",
        [(before, VMEM), (near, VMEM), (queries, VMEM), (weight, VMEM), (cum, VMEM), (prior, SMEM)]
        + [(piece, VMEM) for piece in pieces],
        [(states, BF16, VMEM), ((rows, width), BF16, HBM), (states, F32, HBM)],
        [
            pltpu.VMEM((rows, width), BF16),
            pltpu.VMEM((1, *states), F32),
            pltpu.SemaphoreType.DMA((2, groups)),
        ],
        8,
        cost(0, 0),
    )
    return grad, sums, total


def block_body(blks, grad_blks, q_hbm, k_hbm, v_hbm, grads_hbm, cum_ref, prior_ref, local_hbm, enter_ref, *refs):
    count = len(blks)
    gq_hbm, gk_hbm, gv_hbm, q_ref, k_ref, v_ref, grad_ref, local_ref, gq_ref, gk_ref, gv_ref = refs[-13:-2]
    load_sems, store_sems = refs[-2:]
    _, groups, group, _ = cum_ref.shape
    wide = group * HD

    def loads(n, g):
        lanes, these = lanes_of(g, wide), pl.ds(g * group, group)
        block = pl.ds((blks[0] + n) * BLK, BLK)
        return (
            copy_of(v_hbm.at[block, lanes], v_ref.at[n, :, lanes], load_sems.at[0, n, g]),
            copy_of(q_hbm.at[block, lanes], q_ref.at[n, :, lanes], load_sems.at[1, n, g]),
            copy_of(k_hbm.at[block, lanes], k_ref.at[n, :, lanes], load_sems.at[2, n, g]),
            copy_of(local_hbm.at[blks[0] + n, these], local_ref.at[n, these], load_sems.at[3, n, g]),
        )

    def grad_load(n, g, source=0):
        lanes = lanes_of(g, wide)
        block = pl.ds(grad_blks[source] * BLK, BLK)
        return copy_of(grads_hbm[source].at[block, lanes], grad_ref.at[n, :, lanes], load_sems.at[4, n, g])

    def stores(n, g):
        lanes = lanes_of(g, wide)
        block, part = pl.ds((blks[0] + n) * BLK, BLK), pl.ds(n * BLK, BLK)
        return (
            copy_of(gq_ref.at[n, :, lanes], gq_hbm.at[block, lanes], store_sems.at[0, n, g]),
            copy_of(gk_ref.at[n, :, lanes], gk_hbm.at[part, lanes], store_sems.at[1, n, g]),
            copy_of(gv_ref.at[n, :, lanes], gv_hbm.at[part, lanes], store_sems.at[2, n, g]),
        )

    def start(n, g):
        grad_load(n, g, n).start()
        for copy in loads(n, g):
            copy.start()

    for g in range(groups):
        start(0, g)
    at_row = lax.broadcasted_iota(jnp.int32, (BLK, BLK), 0)
    at_col = lax.broadcasted_iota(jnp.int32, (BLK, BLK), 1)
    causal, flipped = at_row >= at_col, at_row <= at_col

    def some_heads(at):
        n, g = lax.div(at, groups), lax.rem(at, groups)
        blk = blks[0] + n
        for m in range(1, count):

            @pl.when(n == m - 1)
            def _(m=m):
                start(m, g)

        grad_load(n, g).wait()
        for copy in loads(n, g):
            copy.wait()
        rows = cum_ref[blk, g]
        cum = rows.T
        head_weight = jnp.exp(cum)
        lanes, these = lanes_of(g, wide), pl.ds(g * group, group)
        queries, keys, values, grads = (ref[n, :, lanes] for ref in (q_ref, k_ref, v_ref, grad_ref))
        entered, here = enter_ref[these], local_ref[n, these]
        gq, gk, gv = [], [], []
        for h in range(group):
            head = head_in(h)
            q, k, v, grad = queries[:, head], keys[:, head], values[:, head], grads[:, head]
            by_row, by_col = cum[:, h : h + 1], rows[h : h + 1, :]
            mask = jnp.exp(jnp.where(causal, by_row - by_col, -1e30))
            turned = jnp.exp(jnp.where(flipped, by_col - by_row, -1e30))
            scores = (mm(grad, v, NT) * mask).astype(BF16)
            turned_scores = (mm(v, grad, NT) * turned).astype(BF16)
            turned_attn = (mm(k, q, NT) * turned).astype(BF16)
            enter = entered[h].astype(F32) * prior_ref[g * group + h, blk] + here[h]
            inter = mm(grad, enter.astype(BF16), NT) * head_weight[:, h : h + 1]
            gq.append((mm(scores, k, NN) + inter).astype(BF16))
            gk.append(mm(turned_scores, q, NN).astype(BF16))
            gv.append(mm(turned_attn, grad, NN).astype(BF16))
        gq_ref[n, :, lanes] = jnp.concatenate(gq, axis=1)
        gk_ref[n, :, lanes] = jnp.concatenate(gk, axis=1)
        gv_ref[n, :, lanes] = jnp.concatenate(gv, axis=1)
        for copy in stores(n, g):
            copy.start()

    loop(count * groups, some_heads)
    for n in range(count):
        for g in range(groups):
            for copy in stores(n, g):
                copy.wait()


def block_terms(blks, queries, keys, values, grads, cum, prior, local_enter, enter, gq):
    rows, width = queries.shape
    heads, groups, count = width // HD, cum.shape[1], len(blks)
    tile = pltpu.VMEM((count, BLK, width), BF16)
    part = ((count * BLK, width), BF16, HBM)
    ins = [(queries, HBM), (keys, HBM), (values, HBM)] + [(grad, HBM) for _, grad in grads]
    ins += [(cum, VMEM), (prior, SMEM), (local_enter, HBM), (enter, VMEM)]
    if gq is not None:
        ins.append((gq, HBM))

    def body(q_hbm, k_hbm, v_hbm, *refs):
        block_body(blks, [at for at, _ in grads], q_hbm, k_hbm, v_hbm, refs[:count], *refs[count:])

    return call(
        body,
        "block_terms",
        ins,
        [((rows, width), BF16, HBM), part, part],
        [tile] * 4
        + [pltpu.VMEM((count, heads, HD, HD), F32)]
        + [tile] * 3
        + [pltpu.SemaphoreType.DMA((5, count, groups)), pltpu.SemaphoreType.DMA((3, count, groups))],
        28,
        cost(
            count * BLK * width * (10 * BLK + 2 * HD),
            count * (14 * BLK * width + 6 * width * HD),
            count * BLK * heads * BLK,
        ),
        {len(ins) - 1: 0} if gq is not None else None,
    )


def later_body(k_hbm, v_hbm, cum_ref, enter_ref, *refs):
    blk_count, groups, group, _ = cum_ref.shape
    halves = len(refs) - 10 - (blk_count - 1)
    gk_parts, gv_parts = refs[: halves // 2], refs[halves // 2 : halves]
    each = blk_count // len(gk_parts)
    sums_hbm = refs[halves : halves + blk_count - 1]
    gk_hbm, gv_hbm, k_ref, v_ref, gk_ref, gv_ref, sums_ref, carry_ref = refs[halves + blk_count - 1 : -2]
    load_sems, store_sems = refs[-2:]
    wide = group * HD

    def loads(j, g):
        rows, lanes, these = pl.ds(j * BLK, BLK), lanes_of(g, wide), pl.ds(g * group, group)
        part = pl.ds(j % each * BLK, BLK)
        found = [
            copy_of(v_hbm.at[rows, lanes], v_ref.at[rows, lanes], load_sems.at[0, j, g]),
            copy_of(k_hbm.at[rows, lanes], k_ref.at[rows, lanes], load_sems.at[1, j, g]),
            copy_of(gk_parts[j // each].at[part, lanes], gk_ref.at[rows, lanes], load_sems.at[2, j, g]),
            copy_of(gv_parts[j // each].at[part, lanes], gv_ref.at[rows, lanes], load_sems.at[3, j, g]),
        ]
        if j:
            found.append(copy_of(sums_hbm[j - 1].at[these], sums_ref.at[j, these], load_sems.at[4, j, g]))
        return found

    def stores(j, g):
        rows, lanes = pl.ds(j * BLK, BLK), lanes_of(g, wide)
        return (
            copy_of(gk_ref.at[rows, lanes], gk_hbm.at[rows, lanes], store_sems.at[0, j, g]),
            copy_of(gv_ref.at[rows, lanes], gv_hbm.at[rows, lanes], store_sems.at[1, j, g]),
        )

    for g in range(groups):
        for copy in loads(blk_count - 1, g):
            copy.start()
    for j in reversed(range(blk_count)):

        def some_heads(g, j=j):
            if j:
                for copy in loads(j - 1, g):
                    copy.start()
            for copy in loads(j, g):
                copy.wait()
            rows = span(j, BLK)
            cum = cum_ref[j, g].T
            end = cum[BLK - 1 : BLK, :]
            weight = jnp.exp(end - cum)
            end_weight = jnp.exp(end)
            lanes, these = lanes_of(g, wide), pl.ds(g * group, group)
            keys, values = k_ref[rows, lanes], v_ref[rows, lanes]
            gk_in, gv_in = gk_ref[rows, lanes], gv_ref[rows, lanes]
            entered = enter_ref[these].astype(F32) if j + 1 == blk_count else carry_ref[these]
            here = sums_ref[j, these] if j else None
            gk, gv, left = [], [], []
            for h in range(group):
                head, tail = head_in(h), weight[:, h : h + 1]
                enter = entered[h].astype(BF16)
                gk.append((gk_in[:, head].astype(F32) + mm(values[:, head], enter, NT) * tail).astype(BF16))
                gv.append((gv_in[:, head].astype(F32) + mm(keys[:, head], enter, NN) * tail).astype(BF16))
                if j:
                    left.append(entered[h] * end_weight[:, h : h + 1] + here[h])
            gk_ref[rows, lanes] = jnp.concatenate(gk, axis=1)
            gv_ref[rows, lanes] = jnp.concatenate(gv, axis=1)
            if j:
                carry_ref[these] = jnp.stack(left)
            for copy in stores(j, g):
                copy.start()

        loop(groups, some_heads)
    for j in range(blk_count):
        for g in range(groups):
            for copy in stores(j, g):
                copy.wait()


def later_terms(keys, values, gk_parts, gv_parts, sums, cum, enter):
    rows, width = keys.shape
    heads, blk_count = width // HD, rows // BLK
    whole = pltpu.VMEM((rows, width), BF16)
    out = ((rows, width), BF16, HBM)
    return call(
        later_body,
        "later_terms",
        [(keys, HBM), (values, HBM), (cum, VMEM), (enter, VMEM)]
        + [(x, HBM) for x in gk_parts + gv_parts + sums],
        [out, out],
        [whole] * 4
        + [
            pltpu.VMEM((blk_count, heads, HD, HD), F32),
            pltpu.VMEM((heads, HD, HD), F32),
            pltpu.SemaphoreType.DMA((5, blk_count, cum.shape[1])),
            pltpu.SemaphoreType.DMA((2, blk_count, cum.shape[1])),
        ],
        28,
        cost(rows * width * 4 * HD, 12 * rows * width + 4 * blk_count * width * HD),
    )


def chain_body(reverse, got_ref, weight_ref, out_ref):
    devices, share = out_ref.shape[0], out_ref.shape[1]
    pieces = weight_ref.shape[1]
    part = share // pieces
    for p in range(pieces):
        rows = span(p, part)
        carry = jnp.zeros((part, HD), F32)
        for place in reversed(range(devices)) if reverse else range(devices):
            out_ref[place, rows] = carry.astype(BF16)
            carry = weight_ref[place, p] * carry + got_ref[place, rows].astype(F32)


def chain(got, weights, share, reverse):
    devices = got.shape[0]
    (out,) = call(
        functools.partial(chain_body, reverse),
        "chain_states",
        [(got, VMEM), (weights, SMEM)],
        [((devices, share, HD), BF16, VMEM)],
        [],
        16,
        cost(2 * devices * share * HD, 4 * devices * share * HD),
    )
    return out


def swap(x):
    devices = lax.axis_size("seq")
    flat = x.reshape(-1, HD)
    return lax.all_to_all(flat, "seq", 0, 0, tiled=True).reshape(devices, -1, HD)


def after(x, *earlier):
    return lax.optimization_barrier((x, *earlier))[0]


def local(queries, key_vectors, value_vectors, log_decay, grad_output, out_weight):
    rows, width = queries.shape
    heads, blk_count = width // HD, rows // BLK
    tp, me = lax.axis_size("tp"), lax.axis_index("tp")
    seq, place = lax.axis_size("seq"), lax.axis_index("seq")
    chips = tp // 2
    core = [(i, i ^ 1) for i in range(tp)]

    def from_chip(hops):
        return [(i, (i + 2 * hops) % tp) for i in range(tp)]

    own = grad_output
    starts = [0, 1, blk_count - 1, blk_count]
    cuts = [(a * BLK, b * BLK) for a, b in zip(starts, starts[1:])]
    head_rows = take_rows(own, cuts[0][1])
    sibling = lax.ppermute(after(own, head_rows), "tp", core)
    local_enter, fwd_total, cum, pair_cum, rest = key_totals(
        key_vectors, value_vectors, after(log_decay, head_rows), own, cuts[1:], seq
    )
    fwd_got = swap(fwd_total)
    first = [[lax.ppermute(x, "tp", from_chip(d)) for d in range(1, chips)] for x in [head_rows, *rest]]

    def hand_on(j, *earlier):
        arrived = []
        for x in first[j]:
            x = after(x, *earlier)
            arrived += [x, lax.ppermute(x, "tp", core)]
        return arrived

    end = cum[:, :, :, BLK - 1].reshape(blk_count, heads)
    prior = jnp.exp(jnp.cumsum(end, axis=0) - end).T

    near = near_product(own, sibling, out_weight)
    arrived = hand_on(0, near)
    fwd_got = after(fwd_got, near)

    share = heads * HD // seq
    pieces = max(share // HD, 1)
    spans = jnp.sum(fwd_got[:, share : share + 3, :heads].astype(F32), axis=1)
    mine = lax.dynamic_slice_in_dim(jnp.exp(spans), place * share // HD, pieces, axis=1)
    fwd_out = chain(fwd_got, mine, share, False)
    enter_fwd = swap(fwd_out).reshape(heads, HD, HD)

    first_grad, sums, total, _ = far_product(
        0, None, arrived, out_weight, near, queries, after(pair_cum, fwd_out), prior
    )
    arrived = hand_on(1, total)
    next_grad, next_sums, total, kept = far_product(
        1, total, arrived, out_weight, near, queries, pair_cum, prior
    )
    last_grad, last_sums, total = last_product(total, *kept, hand_on(2, next_grad), pair_cum, prior)
    grads = [(0, first_grad)] + [(j, next_grad) for j in range(blk_count - 2)] + [(0, last_grad)]
    sums = [*sums, *next_sums, last_sums]
    gq, parts = None, []

    bwd_got = swap(total)
    cum_now = after(cum, total)
    half = blk_count // 2
    for blks in (list(range(half)), list(range(half, blk_count))):
        if blks[0]:
            bwd_out = chain(after(bwd_got, gq), mine, share, True)
            enter_bwd = swap(bwd_out).reshape(heads, HD, HD)
            cum_now = after(cum, bwd_out)
        gq, *part = block_terms(
            blks,
            queries,
            key_vectors,
            value_vectors,
            [grads[j] for j in blks],
            cum_now,
            prior,
            local_enter,
            enter_fwd,
            gq,
        )
        parts.append(part)
    gk_parts, gv_parts = [list(x) for x in zip(*parts)]
    gk, gv = later_terms(key_vectors, value_vectors, gk_parts, gv_parts, sums[1:], cum, enter_bwd)
    return gq, gk, gv


def solution(mesh):
    in_specs = (
        P("seq", "tp"),
        P("seq", "tp"),
        P("seq", "tp"),
        P("tp", "seq"),
        P("seq", "tp"),
        P("tp", None),
    )
    out_specs = (P("seq", "tp"), P("seq", "tp"), P("seq", "tp"))
    return jax.shard_map(local, mesh=mesh, in_specs=in_specs, out_specs=out_specs, check_vma=False)
```

```python
import functools

import jax
import jax.numpy as jnp
from jax import lax
from jax.experimental import pallas as pl
from jax.experimental.pallas import tpu as pltpu
from jax.sharding import PartitionSpec as P

HD = 128
BLK = 256
GROUP = 4
PAIR = 2
ROW = 16
MIB = 2**20

NN = (((1,), (0,)), ((), ()))
NT = (((1,), (1,)), ((), ()))
TN = (((0,), (0,)), ((), ()))

ANY = pl.BlockSpec(memory_space=pl.ANY)
HBM = pl.BlockSpec(memory_space=pltpu.HBM)
VMEM = pl.BlockSpec(memory_space=pltpu.VMEM)
SMEM = pl.BlockSpec(memory_space=pltpu.SMEM)
BF16 = jnp.bfloat16
F32 = jnp.float32


def mm(left, right, form):
    return lax.dot_general(left, right, form, preferred_element_type=F32)


def cost(flops, nbytes, exps=0):
    return pl.CostEstimate(flops=int(flops), bytes_accessed=int(nbytes), transcendentals=int(exps))


def span(index, size):
    return slice(index * size, (index + 1) * size)


def call(body, name, ins, outs, scratch, limit, estimate, aliases=None):
    return pl.pallas_call(
        body,
        in_specs=[spec for _, spec in ins],
        out_specs=[spec for _, _, spec in outs],
        out_shape=[
            pltpu.HBM(shape, dtype) if spec is HBM else jax.ShapeDtypeStruct(shape, dtype)
            for shape, dtype, spec in outs
        ],
        scratch_shapes=scratch,
        input_output_aliases=aliases or {},
        compiler_params=pltpu.CompilerParams(vmem_limit_bytes=limit * MIB),
        cost_estimate=estimate,
        name=name,
    )(*[pltpu.with_memory_space_constraint(x, pltpu.HBM) if spec is HBM else x for x, spec in ins])


def copy_of(source, target, sem):
    return pltpu.make_async_copy(source, target, sem)


def lanes_of(index, size):
    return pl.ds(pl.multiple_of(index * size, size), size)


def loop(count, body):
    lax.fori_loop(0, count, lambda i, _: (body(i), 0)[1], 0)


def head_in(h):
    return slice(h * HD, (h + 1) * HD)


def take_body(grad_hbm, out_ref, sems):
    copy = copy_of(grad_hbm.at[pl.ds(0, out_ref.shape[0])], out_ref, sems.at[0])
    copy.start()
    copy.wait()


def take_rows(grad, rows):
    (out,) = call(
        take_body,
        "take_rows",
        [(grad, HBM)],
        [((rows, grad.shape[1]), BF16, VMEM)],
        [pltpu.SemaphoreType.DMA((1,))],
        1,
        cost(0, 4 * rows * grad.shape[1]),
    )
    return out


def prefix_sums(x):
    at = lax.broadcasted_iota(jnp.int32, x.shape, 1)
    step = 1
    while step < x.shape[1]:
        x = x + jnp.where(at >= step, pltpu.roll(x, step, 1), 0.0)
        step *= 2
    return x


def key_body(cuts, k_hbm, v_hbm, decay_hbm, grad_hbm, local_hbm, total_ref, cum_ref, pair_ref, *refs):
    cut_hbm, refs = refs[: len(cuts)], refs[len(cuts) :]
    decay_ref, cut_ref, k_ref, v_ref, local_ref, load_sems, store_sems, cut_sems = refs
    blk_count, groups, group, _ = cum_ref.shape
    heads, wide = groups * group, group * HD

    def loads(j):
        rows = pl.ds(j * BLK, BLK)
        return (
            copy_of(k_hbm.at[rows], k_ref.at[rows], load_sems.at[0, j]),
            copy_of(v_hbm.at[rows], v_ref.at[rows], load_sems.at[1, j]),
        )

    def store(j):
        return copy_of(local_ref.at[j], local_hbm.at[j], store_sems.at[j])

    origin = cuts[0][0]
    cut_load = copy_of(grad_hbm.at[pl.ds(origin, cuts[-1][1] - origin)], cut_ref, cut_sems.at[len(cuts)])

    def cut_store(n):
        first, last = cuts[n]
        return copy_of(cut_ref.at[pl.ds(first - origin, last - first)], cut_hbm[n], cut_sems.at[n])

    decay_load = copy_of(decay_hbm, decay_ref, cut_sems.at[len(cuts) + 1])
    decay_load.start()
    for j in range(min(2, blk_count)):
        for copy in loads(j):
            copy.start()
    cut_load.start()
    decay_load.wait()
    span_of = jnp.zeros((heads, 1), F32)
    for j in range(blk_count):
        cum = prefix_sums(decay_ref[:, span(j, BLK)])
        for g in range(groups):
            cum_ref[j, g] = cum[span(g, group)]
        for g in range(heads // PAIR):
            pair_ref[j, g] = cum[span(g, PAIR)]
        span_of = span_of + cum[:, BLK - 1 : BLK]
    local_ref[0] = jnp.zeros_like(local_ref[0])
    cut_load.wait()
    for n in range(len(cuts)):
        cut_store(n).start()

    def block(j):
        for copy in loads(j):
            copy.wait()

        @pl.when(j + 2 < blk_count)
        def _():
            for copy in loads(j + 2):
                copy.start()

        store(j).start()
        rows = pl.ds(pl.multiple_of(j * BLK, BLK), BLK)

        def some_heads(g):
            cum = cum_ref[j, g]
            end = cum[:, BLK - 1 : BLK]
            weight = jnp.exp(end - cum)
            end_weight = jnp.exp(end)
            lanes = lanes_of(g, wide)
            these = pl.ds(g * group, group)
            keys, values, entered = k_ref[rows, lanes], v_ref[rows, lanes], local_ref[j, these]
            left = []
            for h in range(group):
                turned = keys[:, head_in(h)].T.astype(F32)
                scaled = (turned * weight[h : h + 1]).astype(BF16)
                sums = mm(scaled, values[:, head_in(h)], NN)
                left.append(entered[h] * end_weight[h : h + 1] + sums)
            local_ref[j + 1, these] = jnp.stack(left)

        loop(groups, some_heads)

    loop(blk_count, block)
    devices, share = total_ref.shape[0], total_ref.shape[1] - ROW
    total_ref[:, :share] = local_ref[blk_count].astype(BF16).reshape(devices, share, HD)

    diagonal = lax.broadcasted_iota(jnp.int32, (heads, HD), 0) == lax.broadcasted_iota(jnp.int32, (heads, HD), 1)
    spans = jnp.sum(jnp.where(diagonal, span_of, 0.0), axis=0, keepdims=True)
    left, parts = jnp.broadcast_to(spans, (ROW, HD)), jnp.zeros((ROW, HD), F32)
    at_row = lax.broadcasted_iota(jnp.int32, (ROW, HD), 0)
    for n in range(3):
        rounded = left.astype(BF16).astype(F32)
        parts = jnp.where(at_row == n, rounded, parts)
        left = left - rounded
    for d in range(devices):
        total_ref[d, share:] = parts.astype(BF16)
    for j in range(blk_count):
        store(j).wait()
    for n in range(len(cuts)):
        cut_store(n).wait()


def key_totals(keys, values, log_decay, grad, cuts, devices):
    rows, width = keys.shape
    blk_count, heads = rows // BLK, width // HD
    local_enter, total, cum, pair_cum, *parts = call(
        functools.partial(key_body, cuts),
        "key_totals",
        [(keys, HBM), (values, HBM), (log_decay, HBM), (grad, HBM)],
        [
            ((blk_count, heads, HD, HD), F32, HBM),
            ((devices, heads * HD // devices + ROW, HD), BF16, VMEM),
            ((blk_count, heads // GROUP, GROUP, BLK), F32, VMEM),
            ((blk_count, heads // PAIR, PAIR, BLK), F32, VMEM),
        ]
        + [((last - first, grad.shape[1]), BF16, HBM) for first, last in cuts],
        [
            pltpu.VMEM(log_decay.shape, F32),
            pltpu.VMEM((cuts[-1][1] - cuts[0][0], grad.shape[1]), BF16),
            pltpu.VMEM((rows, width), BF16),
            pltpu.VMEM((rows, width), BF16),
            pltpu.VMEM((blk_count + 1, heads, HD, HD), F32),
            pltpu.SemaphoreType.DMA((2, blk_count)),
            pltpu.SemaphoreType.DMA((blk_count,)),
            pltpu.SemaphoreType.DMA((len(cuts) + 2,)),
        ],
        24,
        cost(2 * rows * width * HD, 4 * rows * width + 4 * blk_count * width * HD),
    )
    return local_enter, total, cum, pair_cum, parts


def near_body(wide, own_hbm, sibling_hbm, w_hbm, out_hbm, grad_ref, w_ref, out_ref, w_sems, grad_sems, out_sems):
    rows, depth = own_hbm.shape
    groups, tiles = w_hbm.shape[0] // wide, rows // BLK
    me = lax.axis_index("tp")
    side = lax.rem(me, 2)
    columns = pl.ds(pl.multiple_of((me - side) * depth, 2 * depth), 2 * depth)

    def w_load(g):
        part = pl.ds(g * wide, wide)
        return copy_of(w_hbm.at[part, columns], w_ref.at[part], w_sems.at[g])

    def grad_loads(r):
        part = pl.ds(r * BLK, BLK)
        return (
            copy_of(own_hbm.at[part], grad_ref.at[part, lanes_of(side, depth)], grad_sems.at[0, r]),
            copy_of(sibling_hbm.at[part], grad_ref.at[part, lanes_of(1 - side, depth)], grad_sems.at[1, r]),
        )

    def store(g):
        return copy_of(out_ref.at[lax.rem(g, 2)], out_hbm.at[:, lanes_of(g, wide)], out_sems.at[lax.rem(g, 2)])

    w_load(0).start()
    for r in range(tiles):
        for copy in grad_loads(r):
            copy.start()

    def first_tile(r):
        for copy in grad_loads(r):
            copy.wait()
        these = pl.ds(pl.multiple_of(r * BLK, BLK), BLK)
        out_ref[0, these] = mm(grad_ref[these], w_ref[:wide], NT)

    def columns_of(before):
        g = before + 1
        w_load(g).wait()

        @pl.when(g + 1 < groups)
        def _():
            w_load(g + 1).start()

        @pl.when(g >= 2)
        def _():
            store(g - 2).wait()

        part = w_ref[pl.ds(pl.multiple_of(g * wide, wide), wide)]
        out_ref[lax.rem(g, 2)] = mm(grad_ref[...], part, NT)
        store(g).start()

    w_load(0).wait()
    if groups > 1:
        w_load(1).start()
    loop(tiles, first_tile)
    store(0).start()
    loop(groups - 1, columns_of)
    for g in range(max(groups - 2, 0), groups):
        store(g).wait()


def near_product(own, sibling, weight):
    rows, depth = own.shape
    width = weight.shape[0]
    wide = GROUP * HD
    (out,) = call(
        functools.partial(near_body, wide),
        "near_product",
        [(own, HBM), (sibling, HBM), (weight, HBM)],
        [((rows, width), F32, HBM)],
        [
            pltpu.VMEM((rows, 2 * depth), BF16),
            pltpu.VMEM((width, 2 * depth), BF16),
            pltpu.VMEM((2, rows, wide), F32),
            pltpu.SemaphoreType.DMA((width // wide,)),
            pltpu.SemaphoreType.DMA((2, rows // BLK)),
            pltpu.SemaphoreType.DMA((2,)),
        ],
        32,
        cost(4 * rows * width * depth, 4 * depth * (rows + width) + 4 * rows * width),
    )
    return out


def far_sums(blks, g, group, q_ref, cum_ref, prior_ref, grad, before_ref, sums_refs, total_ref):
    wide = group * HD
    lanes, these = lanes_of(g, wide), pl.ds(g * group, group)
    chained = None
    if before_ref is not None:
        before = before_ref[these]
        chained = [before[h] for h in range(group)]
    for n, blk in enumerate(blks):
        weight = jnp.exp(cum_ref[blk, g])
        queries = q_ref[span(n, BLK), lanes]
        sums = []
        for h in range(group):
            turned = queries[:, head_in(h)].T.astype(F32)
            scaled = (turned * weight[h : h + 1]).astype(BF16)
            sums.append(mm(scaled, grad[span(n, BLK), head_in(h)], NN))
        sums_refs[n][these] = jnp.stack(sums)
        if chained is None:
            chained = sums
        else:
            chained = [chained[h] + prior_ref[g * group + h, blk] * sums[h] for h in range(group)]
    total_ref[these] = jnp.stack(chained).astype(total_ref.dtype)


def far_grad(near, pieces, places, w_ref, g, wide, side):
    part = pl.ds(pl.multiple_of(g * wide, wide), wide)
    for n, piece in zip(places, pieces):
        at = 2 * (n // 2) + (side if n % 2 == 0 else 1 - side)
        near += mm(piece[...], w_ref[part, lanes_of(at, piece.shape[1])], NT)
    return near.astype(BF16)


def far_products(blks, held, places, w_ref, near_ref, q_ref, cum_ref, prior_ref, before_ref, total_ref, grad_ref, sums_ref, side, ahead, after_group, ready):
    _, groups, group, _ = cum_ref.shape
    wide = group * HD

    def product(g):
        ready(g)
        return far_grad(near_ref[:, lanes_of(g, wide)], held, places, w_ref, g, wide, side)

    def sums_of(g, grad):
        sums_refs = [sums_ref.at[n] for n in range(len(blks))]
        far_sums(blks, g, group, q_ref, cum_ref, prior_ref, grad, before_ref, sums_refs, total_ref)

    grad_ref[:, :wide] = product(0)

    def step(g):
        ahead(g + 3)
        mine = grad_ref[:, lanes_of(g, wide)]
        grad = product(g + 1)
        sums_of(g, mine)
        grad_ref[:, lanes_of(g + 1, wide)] = grad
        after_group(g)

    loop(groups - 1, step)
    sums_of(groups - 1, grad_ref[:, lanes_of(groups - 1, wide)])
    after_group(groups - 1)


def far_body(chips, blks, keep, *refs):
    count = len(blks)
    if blks[0]:
        before_hbm, refs = refs[0], refs[1:]
    near_hbm, q_hbm, cum_ref, prior_ref, w_hbm, *refs = refs
    pieces, refs = refs[: 2 * (chips - 1)], refs[2 * (chips - 1) :]
    (total_out, grad_hbm, *sums_hbm), refs = refs[: 2 + count], refs[2 + count :]
    if keep:
        (last_near_ref, last_q_ref), refs = refs[:2], refs[2:]
    w_ref, refs = refs[0], refs[1:]
    held, refs = refs[: len(pieces)], refs[len(pieces) :]
    total_ref, near_ref, q_ref, grad_ref, before_ref, sums_ref, piece_sems, load_sems, store_sems = refs
    total_ref = total_out if keep else total_ref
    rows, depth = pieces[0].shape
    _, groups, group, _ = cum_ref.shape
    wide = group * HD
    me = lax.axis_index("tp")
    side = lax.rem(me, 2)
    chip = lax.div(me, 2)
    here = pl.ds(blks[0] * BLK, rows)

    def loads(g):
        part, lanes, these = pl.ds(g * wide, wide), lanes_of(g, wide), pl.ds(g * group, group)
        found = []
        for d in range(1, chips):
            owner = lax.rem(chip + chips - d, chips)
            columns = pl.ds((d - 1) * 2 * depth, 2 * depth)
            found.append(
                copy_of(w_hbm.at[part, lanes_of(owner, 2 * depth)], w_ref.at[part, columns], load_sems.at[d + 2, g])
            )
        found.append(copy_of(near_hbm.at[here, lanes], near_ref.at[:, lanes], load_sems.at[0, g]))
        found.append(copy_of(q_hbm.at[here, lanes], q_ref.at[:, lanes], load_sems.at[1, g]))
        if blks[0]:
            found.append(copy_of(before_hbm.at[these], before_ref.at[these], load_sems.at[2, g]))
        return found

    def piece_loads():
        return [copy_of(piece, held[n], piece_sems.at[n]) for n, piece in enumerate(pieces)]

    def last_loads():
        if not keep:
            return ()
        block = pl.ds(blks[0] * BLK + rows, BLK)
        return (
            copy_of(near_hbm.at[block], last_near_ref, piece_sems.at[len(pieces)]),
            copy_of(q_hbm.at[block], last_q_ref, piece_sems.at[len(pieces) + 1]),
        )

    def stores(g):
        these, lanes = pl.ds(g * group, group), lanes_of(g, wide)
        found = [copy_of(grad_ref.at[:, lanes], grad_hbm.at[:, lanes], store_sems.at[count, g])]
        found += [copy_of(sums_ref.at[n, these], sums_hbm[n].at[these], store_sems.at[n, g]) for n in range(count)]
        if not keep:
            found.append(copy_of(total_ref.at[these], total_out.at[these], store_sems.at[count + 1, g]))
        return found

    def start(copies):
        for copy in copies:
            copy.start()

    def wait(copies):
        for copy in copies:
            copy.wait()

    def ahead(g):
        @pl.when(g < groups)
        def _():
            start(loads(g))

        @pl.when(g == groups)
        def _():
            start(last_loads())

    start(loads(0))
    start(piece_loads())
    start(loads(1))
    wait(piece_loads())
    if groups > 2:
        start(loads(2))
    far_products(
        blks, held, range(len(held)), w_ref, near_ref, q_ref, cum_ref, prior_ref, before_ref if blks[0] else None, total_ref, grad_ref,
        sums_ref, side, ahead, lambda g: start(stores(g)), lambda g: wait(loads(g)),
    )
    wait(last_loads())
    for g in range(groups):
        wait(stores(g))


def far_product(start, before, pieces, weight, near, queries, cum, prior):
    rows, depth = pieces[0].shape
    blk_count, groups, group, _ = cum.shape
    heads = groups * group
    width = heads * HD
    chips = len(pieces) // 2 + 1
    count = rows // BLK
    blks = list(range(start, start + count))
    keep = start + count == blk_count - 1
    states = (heads, HD, HD)
    far_depth = 2 * (chips - 1) * depth
    kept = [((BLK, width), F32, VMEM), ((BLK, width), BF16, VMEM), ((width, far_depth), BF16, VMEM)]
    total, grad, *rest = call(
        functools.partial(far_body, chips, blks, keep),
        "far_product",
        ([(before, HBM)] if start else [])
        + [(near, HBM), (queries, HBM), (cum, VMEM), (prior, SMEM), (weight, HBM)]
        + [(piece, ANY) for piece in pieces],
        [(states, F32, VMEM if keep else HBM), ((rows, width), BF16, HBM)]
        + [(states, F32, HBM)] * count
        + (kept if keep else []),
        ([] if keep else [pltpu.VMEM((width, far_depth), BF16)])
        + [pltpu.VMEM(piece.shape, BF16) for piece in pieces]
        + [
            pltpu.VMEM(states, F32),
            pltpu.VMEM((rows, width), F32),
            pltpu.VMEM((rows, width), BF16),
            pltpu.VMEM((rows, width), BF16),
            pltpu.VMEM(states, F32),
            pltpu.VMEM((count, *states), F32),
            pltpu.SemaphoreType.DMA((len(pieces) + 2,)),
            pltpu.SemaphoreType.DMA((chips + 2, groups)),
            pltpu.SemaphoreType.DMA((count + 2, groups)),
        ],
        24 if keep else 36,
        cost(
            2 * rows * width * (far_depth + HD),
            2 * far_depth * (rows + width) + 8 * rows * width + 12 * width * HD,
        ),
    )
    return grad, rest[:count], total, rest[count:]


def part_body(near_ref, w_ref, *refs):
    pieces, out_ref = refs[:-1], refs[-1]
    wide = PAIR * HD
    side = lax.rem(lax.axis_index("tp"), 2)

    def product(g):
        part, lanes = pl.ds(pl.multiple_of(g * wide, wide), wide), lanes_of(g, wide)
        total = near_ref[:, lanes]
        for n, piece in enumerate(pieces):
            total += mm(piece[...], w_ref[part, lanes_of(2 * n + side, piece.shape[1])], NT)
        out_ref[:, lanes] = total

    loop(near_ref.shape[1] // wide, product)


def part_product(near, weight, pieces):
    rows, width = near.shape
    depth = pieces[0].shape[1]
    (out,) = call(
        part_body,
        "part_product",
        [(near, VMEM), (weight, VMEM)] + [(piece, VMEM) for piece in pieces],
        [((rows, width), F32, VMEM)],
        [],
        4,
        cost(2 * rows * width * len(pieces) * depth, 8 * rows * width),
    )
    return out


def last_body(blk, before_ref, near_ref, q_ref, w_ref, cum_ref, prior_ref, *refs):
    pieces, (total_ref, grad_hbm, sums_hbm, grad_ref, sums_ref, sems) = refs[:-6], refs[-6:]
    _, groups, group, _ = cum_ref.shape
    wide = group * HD

    def stores(g):
        these, lanes = pl.ds(g * group, group), lanes_of(g, wide)
        return (
            copy_of(grad_ref.at[:, lanes], grad_hbm.at[:, lanes], sems.at[0, g]),
            copy_of(sums_ref.at[0, these], sums_hbm.at[these], sems.at[1, g]),
        )

    def after_group(g):
        for copy in stores(g):
            copy.start()

    far_products(
        [blk], pieces, range(1, 2 * len(pieces), 2), w_ref, near_ref, q_ref, cum_ref, prior_ref, before_ref, total_ref, grad_ref,
        sums_ref, lax.rem(lax.axis_index("tp"), 2), lambda g: None, after_group, lambda g: None,
    )
    for g in range(groups):
        for copy in stores(g):
            copy.wait()


def last_product(before, near, queries, weight, pieces, cum, prior):
    rows, depth = pieces[0].shape
    blk_count, groups, group, _ = cum.shape
    heads = groups * group
    width = heads * HD
    states = (heads, HD, HD)
    total, grad, sums = call(
        functools.partial(last_body, blk_count - 1),
        "last_product",
        [(before, VMEM), (near, VMEM), (queries, VMEM), (weight, VMEM), (cum, VMEM), (prior, SMEM)]
        + [(piece, VMEM) for piece in pieces],
        [(states, BF16, VMEM), ((rows, width), BF16, HBM), (states, F32, HBM)],
        [
            pltpu.VMEM((rows, width), BF16),
            pltpu.VMEM((1, *states), F32),
            pltpu.SemaphoreType.DMA((2, groups)),
        ],
        8,
        cost(0, 0),
    )
    return grad, sums, total


def block_body(blks, grad_blks, q_hbm, k_hbm, v_hbm, grads_hbm, cum_ref, prior_ref, local_hbm, enter_ref, *refs):
    count = len(blks)
    gq_hbm, gk_hbm, gv_hbm, q_ref, k_ref, v_ref, grad_ref, local_ref, gq_ref, gk_ref, gv_ref = refs[-13:-2]
    load_sems, store_sems = refs[-2:]
    _, groups, group, _ = cum_ref.shape
    wide = group * HD

    def loads(n, g):
        lanes, these = lanes_of(g, wide), pl.ds(g * group, group)
        block = pl.ds((blks[0] + n) * BLK, BLK)
        return (
            copy_of(v_hbm.at[block, lanes], v_ref.at[n, :, lanes], load_sems.at[0, n, g]),
            copy_of(q_hbm.at[block, lanes], q_ref.at[n, :, lanes], load_sems.at[1, n, g]),
            copy_of(k_hbm.at[block, lanes], k_ref.at[n, :, lanes], load_sems.at[2, n, g]),
            copy_of(local_hbm.at[blks[0] + n, these], local_ref.at[n, these], load_sems.at[3, n, g]),
        )

    def grad_load(n, g, source=0):
        lanes = lanes_of(g, wide)
        block = pl.ds(grad_blks[source] * BLK, BLK)
        return copy_of(grads_hbm[source].at[block, lanes], grad_ref.at[n, :, lanes], load_sems.at[4, n, g])

    def stores(n, g):
        lanes = lanes_of(g, wide)
        block, part = pl.ds((blks[0] + n) * BLK, BLK), pl.ds(n * BLK, BLK)
        return (
            copy_of(gq_ref.at[n, :, lanes], gq_hbm.at[block, lanes], store_sems.at[0, n, g]),
            copy_of(gk_ref.at[n, :, lanes], gk_hbm.at[part, lanes], store_sems.at[1, n, g]),
            copy_of(gv_ref.at[n, :, lanes], gv_hbm.at[part, lanes], store_sems.at[2, n, g]),
        )

    def start(n, g):
        grad_load(n, g, n).start()
        for copy in loads(n, g):
            copy.start()

    for g in range(groups):
        start(0, g)
    at_row = lax.broadcasted_iota(jnp.int32, (BLK, BLK), 0)
    at_col = lax.broadcasted_iota(jnp.int32, (BLK, BLK), 1)
    causal, flipped = at_row >= at_col, at_row <= at_col

    def some_heads(at):
        n, g = lax.div(at, groups), lax.rem(at, groups)
        blk = blks[0] + n
        for m in range(1, count):

            @pl.when(n == m - 1)
            def _(m=m):
                start(m, g)

        grad_load(n, g).wait()
        for copy in loads(n, g):
            copy.wait()
        rows = cum_ref[blk, g]
        cum = rows.T
        head_weight = jnp.exp(cum)
        lanes, these = lanes_of(g, wide), pl.ds(g * group, group)
        queries, keys, values, grads = (ref[n, :, lanes] for ref in (q_ref, k_ref, v_ref, grad_ref))
        entered, here = enter_ref[these], local_ref[n, these]
        gq, gk, gv = [], [], []
        for h in range(group):
            head = head_in(h)
            q, k, v, grad = queries[:, head], keys[:, head], values[:, head], grads[:, head]
            by_row, by_col = cum[:, h : h + 1], rows[h : h + 1, :]
            mask = jnp.exp(jnp.where(causal, by_row - by_col, -1e30))
            turned = jnp.exp(jnp.where(flipped, by_col - by_row, -1e30))
            scores = (mm(grad, v, NT) * mask).astype(BF16)
            turned_scores = (mm(v, grad, NT) * turned).astype(BF16)
            turned_attn = (mm(k, q, NT) * turned).astype(BF16)
            enter = entered[h].astype(F32) * prior_ref[g * group + h, blk] + here[h]
            inter = mm(grad, enter.astype(BF16), NT) * head_weight[:, h : h + 1]
            gq.append((mm(scores, k, NN) + inter).astype(BF16))
            gk.append(mm(turned_scores, q, NN).astype(BF16))
            gv.append(mm(turned_attn, grad, NN).astype(BF16))
        gq_ref[n, :, lanes] = jnp.concatenate(gq, axis=1)
        gk_ref[n, :, lanes] = jnp.concatenate(gk, axis=1)
        gv_ref[n, :, lanes] = jnp.concatenate(gv, axis=1)
        for copy in stores(n, g):
            copy.start()

    loop(count * groups, some_heads)
    for n in range(count):
        for g in range(groups):
            for copy in stores(n, g):
                copy.wait()


def block_terms(blks, queries, keys, values, grads, cum, prior, local_enter, enter, gq):
    rows, width = queries.shape
    heads, groups, count = width // HD, cum.shape[1], len(blks)
    tile = pltpu.VMEM((count, BLK, width), BF16)
    part = ((count * BLK, width), BF16, HBM)
    ins = [(queries, HBM), (keys, HBM), (values, HBM)] + [(grad, HBM) for _, grad in grads]
    ins += [(cum, VMEM), (prior, SMEM), (local_enter, HBM), (enter, VMEM)]
    if gq is not None:
        ins.append((gq, HBM))

    def body(q_hbm, k_hbm, v_hbm, *refs):
        block_body(blks, [at for at, _ in grads], q_hbm, k_hbm, v_hbm, refs[:count], *refs[count:])

    return call(
        body,
        "block_terms",
        ins,
        [((rows, width), BF16, HBM), part, part],
        [tile] * 4
        + [pltpu.VMEM((count, heads, HD, HD), F32)]
        + [tile] * 3
        + [pltpu.SemaphoreType.DMA((5, count, groups)), pltpu.SemaphoreType.DMA((3, count, groups))],
        28,
        cost(
            count * BLK * width * (10 * BLK + 2 * HD),
            count * (14 * BLK * width + 6 * width * HD),
            count * BLK * heads * BLK,
        ),
        {len(ins) - 1: 0} if gq is not None else None,
    )


def later_body(k_hbm, v_hbm, cum_ref, enter_ref, *refs):
    blk_count, groups, group, _ = cum_ref.shape
    halves = len(refs) - 10 - (blk_count - 1)
    gk_parts, gv_parts = refs[: halves // 2], refs[halves // 2 : halves]
    each = blk_count // len(gk_parts)
    sums_hbm = refs[halves : halves + blk_count - 1]
    gk_hbm, gv_hbm, k_ref, v_ref, gk_ref, gv_ref, sums_ref, carry_ref = refs[halves + blk_count - 1 : -2]
    load_sems, store_sems = refs[-2:]
    wide = group * HD

    def loads(j, g):
        rows, lanes, these = pl.ds(j * BLK, BLK), lanes_of(g, wide), pl.ds(g * group, group)
        part = pl.ds(j % each * BLK, BLK)
        found = [
            copy_of(v_hbm.at[rows, lanes], v_ref.at[rows, lanes], load_sems.at[0, j, g]),
            copy_of(k_hbm.at[rows, lanes], k_ref.at[rows, lanes], load_sems.at[1, j, g]),
            copy_of(gk_parts[j // each].at[part, lanes], gk_ref.at[rows, lanes], load_sems.at[2, j, g]),
            copy_of(gv_parts[j // each].at[part, lanes], gv_ref.at[rows, lanes], load_sems.at[3, j, g]),
        ]
        if j:
            found.append(copy_of(sums_hbm[j - 1].at[these], sums_ref.at[j, these], load_sems.at[4, j, g]))
        return found

    def stores(j, g):
        rows, lanes = pl.ds(j * BLK, BLK), lanes_of(g, wide)
        return (
            copy_of(gk_ref.at[rows, lanes], gk_hbm.at[rows, lanes], store_sems.at[0, j, g]),
            copy_of(gv_ref.at[rows, lanes], gv_hbm.at[rows, lanes], store_sems.at[1, j, g]),
        )

    for g in range(groups):
        for copy in loads(blk_count - 1, g):
            copy.start()
    for j in reversed(range(blk_count)):

        def some_heads(g, j=j):
            if j:
                for copy in loads(j - 1, g):
                    copy.start()
            for copy in loads(j, g):
                copy.wait()
            rows = span(j, BLK)
            cum = cum_ref[j, g].T
            end = cum[BLK - 1 : BLK, :]
            weight = jnp.exp(end - cum)
            end_weight = jnp.exp(end)
            lanes, these = lanes_of(g, wide), pl.ds(g * group, group)
            keys, values = k_ref[rows, lanes], v_ref[rows, lanes]
            gk_in, gv_in = gk_ref[rows, lanes], gv_ref[rows, lanes]
            entered = enter_ref[these].astype(F32) if j + 1 == blk_count else carry_ref[these]
            here = sums_ref[j, these] if j else None
            gk, gv, left = [], [], []
            for h in range(group):
                head, tail = head_in(h), weight[:, h : h + 1]
                enter = entered[h].astype(BF16)
                gk.append((gk_in[:, head].astype(F32) + mm(values[:, head], enter, NT) * tail).astype(BF16))
                gv.append((gv_in[:, head].astype(F32) + mm(keys[:, head], enter, NN) * tail).astype(BF16))
                if j:
                    left.append(entered[h] * end_weight[:, h : h + 1] + here[h])
            gk_ref[rows, lanes] = jnp.concatenate(gk, axis=1)
            gv_ref[rows, lanes] = jnp.concatenate(gv, axis=1)
            if j:
                carry_ref[these] = jnp.stack(left)
            for copy in stores(j, g):
                copy.start()

        loop(groups, some_heads)
    for j in range(blk_count):
        for g in range(groups):
            for copy in stores(j, g):
                copy.wait()


def later_terms(keys, values, gk_parts, gv_parts, sums, cum, enter):
    rows, width = keys.shape
    heads, blk_count = width // HD, rows // BLK
    whole = pltpu.VMEM((rows, width), BF16)
    out = ((rows, width), BF16, HBM)
    return call(
        later_body,
        "later_terms",
        [(keys, HBM), (values, HBM), (cum, VMEM), (enter, VMEM)]
        + [(x, HBM) for x in gk_parts + gv_parts + sums],
        [out, out],
        [whole] * 4
        + [
            pltpu.VMEM((blk_count, heads, HD, HD), F32),
            pltpu.VMEM((heads, HD, HD), F32),
            pltpu.SemaphoreType.DMA((5, blk_count, cum.shape[1])),
            pltpu.SemaphoreType.DMA((2, blk_count, cum.shape[1])),
        ],
        28,
        cost(rows * width * 4 * HD, 12 * rows * width + 4 * blk_count * width * HD),
    )


def chain_body(reverse, got_ref, weight_ref, out_ref):
    devices, share = out_ref.shape[0], out_ref.shape[1]
    pieces = weight_ref.shape[1]
    part = share // pieces
    for p in range(pieces):
        rows = span(p, part)
        carry = jnp.zeros((part, HD), F32)
        for place in reversed(range(devices)) if reverse else range(devices):
            out_ref[place, rows] = carry.astype(BF16)
            carry = weight_ref[place, p] * carry + got_ref[place, rows].astype(F32)


def chain(got, weights, share, reverse):
    devices = got.shape[0]
    (out,) = call(
        functools.partial(chain_body, reverse),
        "chain_states",
        [(got, VMEM), (weights, SMEM)],
        [((devices, share, HD), BF16, VMEM)],
        [],
        16,
        cost(2 * devices * share * HD, 4 * devices * share * HD),
    )
    return out


def swap(x):
    devices = lax.axis_size("seq")
    flat = x.reshape(-1, HD)
    return lax.all_to_all(flat, "seq", 0, 0, tiled=True).reshape(devices, -1, HD)


def after(x, *earlier):
    return lax.optimization_barrier((x, *earlier))[0]


def local(queries, key_vectors, value_vectors, log_decay, grad_output, out_weight):
    rows, width = queries.shape
    heads, blk_count = width // HD, rows // BLK
    tp, me = lax.axis_size("tp"), lax.axis_index("tp")
    seq, place = lax.axis_size("seq"), lax.axis_index("seq")
    chips = tp // 2
    core = [(i, i ^ 1) for i in range(tp)]

    def from_chip(hops):
        return [(i, (i + 2 * hops) % tp) for i in range(tp)]

    own = grad_output
    starts = [0, 1, blk_count - 1, blk_count]
    cuts = [(a * BLK, b * BLK) for a, b in zip(starts, starts[1:])]
    head_rows = take_rows(own, cuts[0][1])
    sibling = lax.ppermute(after(own, head_rows), "tp", core)
    local_enter, fwd_total, cum, pair_cum, rest = key_totals(
        key_vectors, value_vectors, after(log_decay, head_rows), own, cuts[1:], seq
    )
    fwd_got = swap(fwd_total)
    first = [[lax.ppermute(x, "tp", from_chip(d)) for d in range(1, chips)] for x in [head_rows, *rest]]

    def hand_on(j, *earlier):
        arrived = []
        for x in first[j]:
            x = after(x, *earlier)
            arrived += [x, lax.ppermute(x, "tp", core)]
        return arrived

    end = cum[:, :, :, BLK - 1].reshape(blk_count, heads)
    prior = jnp.exp(jnp.cumsum(end, axis=0) - end).T

    near = near_product(own, sibling, out_weight)
    arrived = hand_on(0, near)
    fwd_got = after(fwd_got, near)

    share = heads * HD // seq
    pieces = max(share // HD, 1)
    spans = jnp.sum(fwd_got[:, share : share + 3, :heads].astype(F32), axis=1)
    mine = lax.dynamic_slice_in_dim(jnp.exp(spans), place * share // HD, pieces, axis=1)
    fwd_out = chain(fwd_got, mine, share, False)
    enter_fwd = swap(fwd_out).reshape(heads, HD, HD)

    first_grad, sums, total, _ = far_product(
        0, None, arrived, out_weight, near, queries, after(pair_cum, fwd_out), prior
    )
    arrived = hand_on(1, total)
    next_grad, next_sums, total, kept = far_product(
        1, total, arrived, out_weight, near, queries, pair_cum, prior
    )
    last_near, last_queries, far_weight = kept
    arrived = hand_on(2, next_grad)
    last_near = part_product(last_near, far_weight, arrived[::2])
    last_grad, last_sums, total = last_product(
        total, last_near, last_queries, far_weight, arrived[1::2], pair_cum, prior
    )
    grads = [(0, first_grad)] + [(j, next_grad) for j in range(blk_count - 2)] + [(0, last_grad)]
    sums = [*sums, *next_sums, last_sums]
    gq, parts = None, []

    bwd_got = swap(total)
    cum_now = after(cum, total)
    half = blk_count // 2
    for blks in (list(range(half)), list(range(half, blk_count))):
        if blks[0]:
            bwd_out = chain(after(bwd_got, gq), mine, share, True)
            enter_bwd = swap(bwd_out).reshape(heads, HD, HD)
            cum_now = after(cum, bwd_out)
        gq, *part = block_terms(
            blks,
            queries,
            key_vectors,
            value_vectors,
            [grads[j] for j in blks],
            cum_now,
            prior,
            local_enter,
            enter_fwd,
            gq,
        )
        parts.append(part)
    gk_parts, gv_parts = [list(x) for x in zip(*parts)]
    gk, gv = later_terms(key_vectors, value_vectors, gk_parts, gv_parts, sums[1:], cum, enter_bwd)
    return gq, gk, gv


def solution(mesh):
    in_specs = (
        P("seq", "tp"),
        P("seq", "tp"),
        P("seq", "tp"),
        P("tp", "seq"),
        P("seq", "tp"),
        P("tp", None),
    )
    out_specs = (P("seq", "tp"), P("seq", "tp"), P("seq", "tp"))
    return jax.shard_map(local, mesh=mesh, in_specs=in_specs, out_specs=out_specs, check_vma=False)
```
